32 devices in a mesh: batch: 4 (over z), seq: 4 (over y, x), head: 2 (over core).
Axes of the slice: x: 2, y: 2, z: 4, core: 2. Of those that a mesh axis runs over, the one named last changes fastest.
Arguments:
- hidden: bfloat16 [8, 1024, 2048], P('batch', 'seq'), may hold values from -6 to 6
- norm_gain: float32 [2048], replicated, may hold values from 0.5 to 1.5
- gate_input_weight: bfloat16 [2048, 2, 4096], P(None, None, 'head'), may hold values from -0.125 to 0.125
- w_bc: bfloat16 [2048, 256], replicated, may hold values from -0.125 to 0.125
- w_dt: bfloat16 [2048, 64], P(None, 'head'), may hold values from -0.125 to 0.125
- conv_x: float32 [5, 4096], P(None, 'head'), may hold values from -3 to 3
- conv_bc: float32 [5, 256], replicated, may hold values from -3 to 3
- head_params: float32 [3, 64], P(None, 'head'), as said below
- gate_gain: float32 [4096], P('head'), may hold values from 0.5 to 1.5
- w_out: bfloat16 [4096, 2048], P('head'), may hold values from -0.09375 to 0.09375
- lengths: int32 [8], P('batch'), may hold values from 256 to 1024, as said below
- cotangent: bfloat16 [8, 1024, 2048], P('batch', 'seq'), may hold values from -6 to 6
Outputs:
- mixed_out: bfloat16 [8, 1024, 2048], P('batch', 'seq')
- grad_hidden: float32 [8, 1024, 2048], P('batch', 'seq')
- grad_norm_gain: float32 [2048], replicated
- gradient_gate_input_weight: float32 [2048, 2, 4096], P(('batch', 'seq'), None, 'head')
- grad_w_bc: float32 [2048, 256], P(('batch', 'seq'))
- grad_w_dt: float32 [2048, 64], P(('batch', 'seq'), 'head')
- grad_conv_x: float32 [5, 4096], P(None, 'head')
- grad_conv_bc: float32 [5, 256], replicated
- grad_head_params: float32 [3, 64], P(None, 'head')
- grad_gate_gain: float32 [4096], P('head')
- grad_w_out: float32 [4096, 2048], P('head', ('batch', 'seq'))
The draws below stay inside these ranges and needn't reach their ends.
Inputs may be any that keep to these rules, and one draw needn't show every extreme that they name: `lengths`: in each aligned group of 2 sequences (those of one index of batch) exactly one sequence, chosen at random, has length 1024; the others are uniform between the bounds. Slots at or past a sequence's length are padding. `head_params`: row 1 is the logarithm of a positive decay rate; rows 0 and 2 are real numbers of order one.
All inputs are finite; a program needn't handle non-finite values.
Results may differ from the reference program's by a relative error of at most 0.0081.
Values sent between devices are 32-bit elements; how exact they have to be, the bound alone decides.
A program may use at most 192 MiB of HBM per device.

```python
import math
import jax
import jax.numpy as jnp
from jax import lax

D = 2048
HEADS = 64
STATE = 128
CONV = 4
SPAN = 256
SEQS_DEV = 2
INNER = 4096
LENGTH = 1024
SEQS = 8


def draw_lengths(key, part):
    key = jax.random.fold_in(key, 11)
    first, second = jax.random.split(key)
    drawn = jax.random.randint(first, (SEQS,), LENGTH // 4, LENGTH + 1)
    picked = jax.random.randint(second, (SEQS // SEQS_DEV,), 0, SEQS_DEV)
    places = jnp.arange(SEQS) % SEQS_DEV
    chosen = places == jnp.repeat(picked, SEQS_DEV)
    return jnp.where(chosen, LENGTH, drawn).astype(jnp.int32)


def draw_head_params(key, part):
    key = jax.random.fold_in(key, 5)
    first, second, third = jax.random.split(key, 3)
    slow_end = math.log(0.5 / (LENGTH * 0.015))
    fast_end = math.log(1.0 / (40.0 * 0.015))
    step_bias = jax.random.uniform(first, (HEADS,), jnp.float32, -5.0, -3.5)
    decay_log = jax.random.uniform(second, (HEADS,), jnp.float32, slow_end, fast_end)
    skip_weight = jax.random.uniform(third, (HEADS,), jnp.float32, 0.5, 1.5)
    return jnp.stack([step_bias, decay_log, skip_weight], axis=0).astype(jnp.float32)


def level_of(own_key, dims, shards, low, top_value):
    def one(position, shards_of):
        steps = jax.random.uniform(jax.random.fold_in(jax.random.fold_in(own_key, 6), position), (shards_of,), jnp.float32, low / len(shards), top_value / len(shards))
        return jnp.repeat(jnp.exp(steps), dims[position] // shards_of).reshape((-1,) + (1,) * (len(dims) - position - 1))

    level = one(*shards[0])
    for cut in shards[1:]:
        level = level * one(*cut)
    return level


def gaussian(stream_key, extent, scale, bound, cuts=(), held_as=jnp.bfloat16):
    values = jax.random.normal(stream_key, extent, jnp.float32) * scale
    if len(cuts) > 0:
        values = level_of(stream_key, extent, cuts, -0.22, 0.18) * values
    return jnp.clip(values, min=-bound, max=bound).astype(held_as)


def setup_inputs(seed: int = 0) -> dict:
    arg_keys = jax.random.split(jax.random.key(seed), 13)
    return {
        "hidden": gaussian(arg_keys[0], (SEQS, LENGTH, D), 1.0, 6.0, ((0, 4), (1, 4))),
        "norm_gain": jnp.clip(1.0 + 0.1 * jax.random.normal(arg_keys[1], (D,), jnp.float32), 0.5, 1.5),
        "gate_input_weight": gaussian(arg_keys[2], (D, 2, INNER), D ** -0.5, 0.125, ((2, 2),)),
        "w_bc": gaussian(arg_keys[3], (D, 2 * STATE), D ** -0.5, 0.125),
        "w_dt": gaussian(arg_keys[4], (D, HEADS), D ** -0.5, 0.125, ((1, 2),)),
        "conv_x": gaussian(arg_keys[5], (CONV + 1, INNER), 0.5, 3.0, ((1, 2),), jnp.float32),
        "conv_bc": gaussian(arg_keys[6], (CONV + 1, 2 * STATE), 0.5, 3.0, (), jnp.float32),
        "head_params": draw_head_params(jax.random.fold_in(arg_keys[12], 71), 0),
        "gate_gain": jnp.clip(1.0 + 0.1 * jax.random.normal(arg_keys[8], (INNER,), jnp.float32), 0.5, 1.5),
        "w_out": gaussian(arg_keys[9], (INNER, D), INNER ** -0.5, 0.09375, ((0, 2),)),
        "lengths": draw_lengths(jax.random.fold_in(arg_keys[12], 71), 0),
        "cotangent": gaussian(arg_keys[11], (SEQS, LENGTH, D), 1.0, 6.0, ((0, 4), (1, 4))),
    }


TOP_PRECISION = lax.Precision.HIGHEST
EPSILON = 1e-05

@jax.custom_vjp
def low(v):
    return lax.optimization_barrier(v.astype(jnp.bfloat16)).astype(jnp.float32)

@jax.custom_vjp
def lower_backward(v):
    return v

def low_keep(v):
    return (low(v), None)

def low_pass(kept, grad):
    return (grad,)

def back_keep(v):
    return (v, None)

def back_low(kept, grad):
    return (low(grad),)
low.defvjp(low_keep, low_pass)
lower_backward.defvjp(back_keep, back_low)

def state_space(x_act, step_dt, decay_a, b_act, c_act, state_in):
    batch, slots = (x_act.shape[0], x_act.shape[1])
    blocks = slots // SPAN

    def cut_blocks(value):
        return jnp.moveaxis(value.reshape((batch, blocks, SPAN) + value.shape[2:]), 1, 0)
    causal = jnp.arange(SPAN)[:, None] >= jnp.arange(SPAN)[None, :]

    def block_step(state, pieces):
        x_blk, dt_blk, b_blk, c_blk = pieces
        cumul = jnp.cumsum(dt_blk * decay_a, axis=1)
        spread = cumul[:, :, None, :] - cumul[:, None, :, :]
        mask_ij = causal[None, :, :, None]
        decay = jnp.where(mask_ij, jnp.exp(jnp.where(mask_ij, spread, 0.0)), 0.0)
        scores = jnp.einsum('bin,bjn->bij', c_blk, b_blk, precision=TOP_PRECISION)
        weights = scores[..., None] * decay * dt_blk[:, None, :, :]
        result = jnp.einsum('bijh,bjhp->bihp', weights, x_blk, precision=TOP_PRECISION)
        result = result + jnp.einsum('bin,bhpn->bihp', c_blk, state, precision=TOP_PRECISION) * jnp.exp(cumul)[..., None]
        last = cumul[:, -1, :]
        tail = jnp.exp(last[:, None, :] - cumul) * dt_blk
        state = jnp.exp(last)[:, :, None, None] * state + jnp.einsum('bjh,bjhp,bjn->bhpn', tail, x_blk, b_blk, precision=TOP_PRECISION)
        return (state, result)
    state_out, results = lax.scan(jax.checkpoint(block_step), state_in, (cut_blocks(x_act), cut_blocks(step_dt), cut_blocks(b_act), cut_blocks(c_act)))
    return (jnp.moveaxis(results, 0, 1).reshape(x_act.shape), state_out)

def rms_scale(value, gain):
    return value * lax.rsqrt(lax.optimization_barrier(jnp.mean(value * value, axis=-1, keepdims=True)) + EPSILON) * gain

def reference(hidden, norm_gain, gate_input_weight, w_bc, w_dt, conv_x, conv_bc, head_params, gate_gain, w_out, lengths, cotangent):
    seqs, length = (hidden.shape[0], hidden.shape[1])
    inner = gate_input_weight.shape[2]
    heads = w_dt.shape[1]
    width = inner // heads
    state_size = w_bc.shape[1] // 2
    positions = jnp.arange(length).astype(jnp.int32)
    mask = (positions[None, :] < lengths[:, None]).astype(jnp.float32)

    def forward(hidden_f, norm_gain, gate_input_weight, w_bc, w_dt, conv_x, conv_bc, head_params, gate_gain, w_out):
        normalized_rows = low(rms_scale(hidden_f, norm_gain))
        projected_gate_input = lower_backward(jnp.einsum('eqg,gjn->eqjn', normalized_rows, gate_input_weight, precision=TOP_PRECISION))
        proj_bc = lower_backward(jnp.einsum('btd,dc->btc', normalized_rows, w_bc, precision=TOP_PRECISION))
        proj_dt = lower_backward(jnp.einsum('btd,dh->bth', normalized_rows, w_dt, precision=TOP_PRECISION))
        gate_z = projected_gate_input[:, :, 0]
        pre_conv = jnp.concatenate([projected_gate_input[:, :, 1], proj_bc], axis=-1)
        conv_all = jnp.concatenate([conv_x, conv_bc], axis=1)
        padded = jnp.pad(pre_conv, ((0, 0), (CONV - 1, 0), (0, 0)))
        summed = conv_all[CONV] + padded[:, 0:length] * conv_all[0]
        for tap in range(1, CONV):
            summed = summed + padded[:, tap:tap + length] * conv_all[tap]
        active = jax.nn.silu(summed)
        x_act = active[..., :inner].reshape(seqs, length, heads, width)
        b_act = active[..., inner:inner + state_size]
        c_act = active[..., inner + state_size:]
        step_dt = jax.nn.softplus(proj_dt + head_params[0])
        decay_a = -jnp.exp(head_params[1])
        start = jnp.zeros((seqs, heads, width, state_size), jnp.float32)
        ssm_out, final = state_space(x_act, step_dt, decay_a, b_act, c_act, start)
        ssm_out = ssm_out + head_params[2][:, None] * x_act
        gated = ssm_out.reshape(seqs, length, inner) * jax.nn.silu(gate_z)
        normed_gate = low(rms_scale(gated, gate_gain))
        mixed = jnp.einsum('bti,id->btd', normed_gate, w_out, precision=TOP_PRECISION)
        return mask[..., None] * (hidden_f + mixed)
    primals = (hidden.astype(jnp.float32), norm_gain, gate_input_weight.astype(jnp.float32), w_bc.astype(jnp.float32), w_dt.astype(jnp.float32), conv_x, conv_bc, head_params, gate_gain, w_out.astype(jnp.float32))
    result, pullback = jax.vjp(forward, *primals)
    grads = pullback(cotangent.astype(jnp.float32))
    return (result.astype(jnp.bfloat16), grads[0], grads[1], grads[2], grads[3], grads[4], grads[5], grads[6], grads[7], grads[8], grads[9])
```

```python
import functools

import jax
import jax.numpy as jnp
from jax import lax
from jax.experimental import pallas as pl
from jax.experimental.pallas import tpu as pltpu
from jax.sharding import PartitionSpec as P

CONV = 4
EDGE = 8
LANES = 256
EPSILON = 1e-05
HIGHEST = lax.Precision.HIGHEST
F32 = jnp.float32
BF16 = jnp.bfloat16
VMEM_LIMIT = 48 * 1024 * 1024


def mm(a, b, dims=((1,), (0,)), precision=None):
    return lax.dot_general(a, b, (dims, ((), ())), precision=precision, preferred_element_type=F32)


def widen(columns, width):
    slots, heads = columns.shape
    lane = lax.broadcasted_iota(jnp.int32, (slots, heads * width), 1) // width
    result = jnp.broadcast_to(columns[:, 0:1], (slots, heads * width))
    for head in range(1, heads):
        result = jnp.where(lane == head, columns[:, head : head + 1], result)
    return result


def head_sums(value, heads):
    lanes = value.shape[1]
    row = lax.broadcasted_iota(jnp.int32, (lanes, heads), 0) // (lanes // heads)
    pick = (row == lax.broadcasted_iota(jnp.int32, (lanes, heads), 1)).astype(BF16)
    high = value.astype(BF16)
    low = (value - high.astype(F32)).astype(BF16)
    return mm(high, pick) + mm(low, pick)


def triangle(slots):
    row = lax.broadcasted_iota(jnp.int32, (slots, slots), 0)
    column = lax.broadcasted_iota(jnp.int32, (slots, slots), 1)
    return (row >= column).astype(F32)


def softplus(value):
    return jnp.maximum(value, 0.0) + jnp.log1p(jnp.exp(-jnp.abs(value)))


def slope(value, sig):
    return sig * (1.0 + value * (1.0 - sig))


def convolved(extended, taps, slots):
    total = taps[CONV : CONV + 1] + extended[EDGE : EDGE + slots] * taps[CONV - 1 : CONV]
    for tap in range(CONV - 1):
        start = EDGE - (CONV - 1) + tap
        total = total + extended[start : start + slots] * taps[tap : tap + 1]
    return total


def convolved_back(grad, extended, taps):
    slots, lanes = grad.shape
    padded = jnp.concatenate([grad, jnp.zeros((EDGE, lanes), F32)], axis=0)
    back = grad * taps[CONV - 1 : CONV]
    rows = []
    for tap in range(CONV):
        start = EDGE - (CONV - 1) + tap
        rows.append(jnp.sum(grad * extended[start : start + slots], axis=0, keepdims=True))
        if tap < CONV - 1:
            ahead = CONV - 1 - tap
            back = back + padded[ahead : ahead + slots] * taps[tap : tap + 1]
    rows.append(jnp.sum(grad, axis=0, keepdims=True))
    rows.append(jnp.zeros((8 - len(rows), lanes), F32))
    return back, jnp.concatenate(rows, axis=0)


def of_head(value, head, heads):
    lane = lax.broadcasted_iota(jnp.int32, value.shape, 1) // (value.shape[1] // heads)
    return jnp.where(lane == head, value, jnp.zeros_like(value))


def local_kernel(
    heads, width, pre_x, edge_x, taps_x, pre_bc, edge_bc, taps_bc, dtraw, params,
    local_out, local_state, total_decay, b_out, c_out, steps_out, scores,
):
    slots = pre_x.shape[1]
    state = b_out.shape[2]
    tri = triangle(slots)

    @pl.when(pl.program_id(1) == 0)
    def _():
        ext = jnp.concatenate([edge_bc[0], pre_bc[0]], axis=0)
        u = convolved(ext, taps_bc[...], slots)
        act = u * jax.nn.sigmoid(u)
        b_out[0] = act[:, :state]
        c_out[0] = act[:, state:]
        scores[...] = mm(act[:, state:], act[:, :state], ((1,), (1,)), HIGHEST) * tri

    ext = jnp.concatenate([edge_x[0], pre_x[0]], axis=0)
    u = convolved(ext, taps_x[...], slots)
    x = u * jax.nn.sigmoid(u)
    par = params[0]
    step = softplus(dtraw[0, 0] + par[0:1])
    rate = step * -jnp.exp(par[1:2])
    cumul = mm(tri, rate, precision=HIGHEST)
    cumul_t = mm(rate, tri, ((0,), (1,)), precision=HIGHEST)
    steps_out[0, 0] = jnp.concatenate([step, cumul], axis=1)
    last = cumul[slots - 1 : slots]
    total_decay[0] = widen(jnp.exp(last), width)
    xd = (widen(step, width) * x).astype(BF16)
    tail = (widen(jnp.exp(last - cumul), width) * xd.astype(F32)).astype(BF16)
    local_state[0] = mm(b_out[0].astype(BF16), tail, ((0,), (0,)))
    out = widen(par[2:3], width) * x
    for head in range(heads):
        decay = jnp.exp(jnp.minimum(cumul[:, head : head + 1] - cumul_t[head : head + 1], 0.0))
        weights = (scores[...] * decay).astype(BF16)
        out = out + mm(weights, of_head(xd, head, heads))
    local_out[0] = out


def gate_kernel(heads, width, local_out, entering, c_act, steps, z, grad_out, gain, y_out, sums):
    cumul = steps[0, 0][:, heads:]
    inter = mm(c_act[0].astype(BF16), entering[0].astype(BF16))
    y = local_out[0] + widen(jnp.exp(cumul), width) * inter
    y_out[0] = y
    zv = z[0]
    g = y * (zv * jax.nn.sigmoid(zv))
    squares = jnp.sum(g * g, axis=1, keepdims=True)
    dots = jnp.sum(grad_out[0] * gain[...] * g, axis=1, keepdims=True)
    both = jnp.concatenate([squares, dots], axis=1)

    @pl.when(pl.program_id(1) == 0)
    def _():
        sums[0] = both

    @pl.when(pl.program_id(1) > 0)
    def _():
        sums[0] += both


def gate_back_kernel(
    heads, width, inner_all, y, z, grad_out, gain, sums, c_act, steps,
    gated_out, grad_y, grad_z, gain_grad, leaving,
):
    inv = lax.rsqrt(sums[0][:, 0:1] / inner_all + EPSILON)
    mean = inv * sums[0][:, 1:2] / inner_all
    zv, yv = z[0], y[0]
    sig = jax.nn.sigmoid(zv)
    silu = zv * sig
    normed = yv * silu * inv
    gated_out[0] = (normed * gain[...]).astype(BF16)
    gain_grad[0] = jnp.sum(grad_out[0] * normed, axis=0, keepdims=True)
    dg = inv * (grad_out[0] * gain[...] - normed * mean)
    dy = dg * silu
    grad_y[0] = dy
    grad_z[0] = (dg * yv * slope(zv, sig)).astype(BF16)
    growth = widen(jnp.exp(steps[0, 0][:, heads:]), width)
    leaving[0] = mm(c_act[0].astype(BF16), (growth * dy).astype(BF16), ((0,), (0,)))


def scan_back_kernel(
    heads, width, pre_x, edge_x, taps_x, dtraw, params, steps, b_act, c_act, y, grad_y, entering, coming,
    grad_pre, tail_rows, head_rows, taps_grad, grad_dt, params_grad, grad_bc, grad_scores, scores,
):
    slots = pre_x.shape[1]
    state = b_act.shape[2]
    tri = triangle(slots)
    first = pl.program_id(1) == 0

    @pl.when(first)
    def _():
        scores[...] = mm(c_act[0], b_act[0], ((1,), (1,)), HIGHEST) * tri
        grad_scores[...] = jnp.zeros_like(grad_scores)
        grad_bc[...] = jnp.zeros_like(grad_bc)

    ext = jnp.concatenate([edge_x[0], pre_x[0]], axis=0)
    u = convolved(ext, taps_x[...], slots)
    sig = jax.nn.sigmoid(u)
    x = u * sig
    par = params[0]
    decay_a = -jnp.exp(par[1:2])
    step = steps[0, 0][:, :heads]
    cumul = steps[0, 0][:, heads:]
    cumul_t = mm(step * decay_a, tri, ((0,), (1,)), precision=HIGHEST)
    last = cumul[slots - 1 : slots]
    step_wide = widen(step, width)
    tail_wide = widen(jnp.exp(last - cumul), width)
    growth = widen(jnp.exp(cumul), width)
    skip = widen(par[2:3], width)
    xd = (step_wide * x).astype(BF16)
    xd_f = xd.astype(F32)
    dy = grad_y[0]
    dy_b = dy.astype(BF16)
    coming_b = coming[0].astype(BF16)
    from_next = tail_wide * mm(b_act[0].astype(BF16), coming_b)
    grad_xd = from_next
    total = jnp.zeros((slots, slots), F32)
    for head in range(heads):
        decay = jnp.exp(jnp.minimum(cumul[:, head : head + 1] - cumul_t[head : head + 1], 0.0))
        weights = (scores[...] * decay).astype(BF16)
        mine = of_head(dy_b, head, heads)
        grad_xd = grad_xd + mm(weights, mine, ((0,), (0,)))
        total = total + mm(mine, xd, ((1,), (1,))) * decay
    grad_scores[...] += total
    grad_c = mm((growth * dy).astype(BF16), entering[0].astype(BF16), ((1,), (1,)))
    grad_b = mm((tail_wide * xd_f).astype(BF16), coming_b, ((1,), (1,)))
    grad_bc[0] += jnp.concatenate([grad_b, grad_c], axis=1)

    direct = head_sums(x * grad_xd, heads)
    ys = y[0] - skip * x
    moved = head_sums(dy_b.astype(F32) * ys - xd_f * grad_xd, heads)
    ends = jnp.exp(widen(last, width)) * jnp.sum(coming[0] * entering[0], axis=0, keepdims=True)
    ends = ends + jnp.sum(xd_f * from_next, axis=0, keepdims=True)
    skips = jnp.sum(dy * x, axis=0, keepdims=True)
    rows = head_sums(jnp.concatenate([ends, skips, jnp.zeros((6, ends.shape[1]), F32)], axis=0), heads)
    later = mm(tri, moved, ((0,), (0,)), precision=HIGHEST) + rows[0:1]
    grad_step = (direct + decay_a * later) * jax.nn.sigmoid(dtraw[0, 0] + par[0:1])
    grad_dt[0, 0] = grad_step
    params_grad[0, 0] = jnp.concatenate(
        [
            jnp.sum(grad_step, axis=0, keepdims=True),
            jnp.sum(step * later, axis=0, keepdims=True) * decay_a,
            rows[1:2],
        ],
        axis=0,
    )
    du = (step_wide * grad_xd + skip * dy) * slope(u, sig)
    back, rows8 = convolved_back(du, ext, taps_x[...])
    grad_pre[0] = back.astype(BF16)
    tail_rows[0] = back[slots - EDGE :]
    head_rows[0] = du[:EDGE]
    taps_grad[0] = rows8

    @pl.when(pl.program_id(1) == pl.num_programs(1) - 1)
    def _():
        causal = grad_scores[...] * tri
        from_c = mm(causal, c_act[0], ((0,), (0,)), HIGHEST)
        grad_bc[0] += jnp.concatenate([from_c, mm(causal, b_act[0], precision=HIGHEST)], axis=1)


def conv_back_kernel(pre, edge, taps, grad_act, grad_pre, tail_rows, head_rows, taps_grad):
    slots = pre.shape[1]
    ext = jnp.concatenate([edge[0], pre[0]], axis=0)
    u = convolved(ext, taps[...], slots)
    du = grad_act[0] * slope(u, jax.nn.sigmoid(u))
    back, rows8 = convolved_back(du, ext, taps[...])
    grad_pre[0] = back.astype(BF16)
    tail_rows[0] = back[slots - EDGE :]
    head_rows[0] = du[:EDGE]
    taps_grad[0] = rows8


def narrow_kernel(value, result):
    result[...] = value[...].astype(BF16)


def narrow(value):
    rows, columns = value.shape
    block = pl.BlockSpec((rows // 2, columns), lambda i: (i, 0))
    return pl.pallas_call(
        narrow_kernel,
        grid=(2,),
        in_specs=[block],
        out_specs=block,
        out_shape=jax.ShapeDtypeStruct(value.shape, BF16),
        name="narrow",
    )(value)


def swapped(value, axis, bit):
    count = lax.axis_size(axis)
    return lax.ppermute(value, axis, [(i, i ^ bit) for i in range(count)])


def shifted(value, axis, steps):
    count = lax.axis_size(axis)
    initial, last = (max(0, -steps), min(count, count - steps))
    return lax.ppermute(value, axis, [(source, source + steps) for source in range(initial, last)])


def head_sum(value):
    if lax.axis_size("head") == 2:
        return value + swapped(value, "head", 1)
    return lax.psum(value, "head")


def passed_on(decay, part, reverse):
    count = lax.axis_size("seq")
    place = lax.axis_index("seq")
    both = jnp.concatenate([part, jnp.broadcast_to(decay, (decay.shape[0], 8, decay.shape[2]))], axis=1)
    gathered = lax.all_gather(both, "seq")
    rows = part.shape[1]
    state = jnp.zeros_like(part)
    for turn in range(count - 1):
        source = count - 1 - turn if reverse else turn
        ahead = source > place if reverse else source < place
        later = gathered[source, :, rows : rows + 1] * state + gathered[source, :, :rows]
        state = jnp.where(ahead, later, state)
    return state


def halves(value, axis, which):
    size = value.shape[axis] // 2
    return lax.dynamic_slice_in_dim(value, which * size, size, axis)


def pair_rows(rows):
    side = lax.axis_index("head")
    mine = swapped(halves(rows, 1, side).astype(F32), "batch", 1)
    theirs = narrow(swapped(mine, "head", 1))
    mine = narrow(mine)
    low = jnp.where(side == 0, mine, theirs)
    high = jnp.where(side == 0, theirs, mine)
    return jnp.concatenate([rows, jnp.concatenate([low, high], axis=1)], axis=0)


def pair_columns(columns):
    parity = lax.axis_index("batch") % 2
    sent = halves(columns, 1, 1 - parity).astype(F32)
    got = narrow(swapped(sent, "batch", 1))
    return jnp.concatenate([halves(columns, 1, parity), got], axis=0)


def pair_grad(rows, columns):
    z, s = lax.axis_index("batch"), lax.axis_index("seq")
    parity, upper = z % 2, z // 2
    sx, sy = s % 2, s // 2
    block = rows.shape[1] // 16
    part = mm(rows, columns, ((0,), (0,)))
    part = part.reshape(4, 2, 2, block, columns.shape[1])
    half = columns.shape[1] // 2

    def pick(value, axis, index):
        return lax.dynamic_index_in_dim(value, index, axis, False)

    a, b = part[..., :half], part[..., half:]
    a = pick(a, 2, sx) + swapped(pick(a, 2, 1 - sx), "seq", 1)
    b = pick(b, 1, sy) + swapped(pick(b, 1, 1 - sy), "seq", 2)
    a = pick(a, 1, sy) + swapped(pick(a, 1, 1 - sy), "seq", 2)
    b = pick(b, 1, sx) + swapped(pick(b, 1, 1 - sx), "seq", 1)
    both = jnp.concatenate([a, b], axis=-1).reshape(2, 2, block, columns.shape[1])
    both = pick(both, 0, upper) + swapped(pick(both, 0, 1 - upper), "batch", 2)
    own = pick(both, 0, parity)
    other = swapped(pick(both, 0, 1 - parity), "batch", 1)
    low = jnp.where(parity == 0, own, other)
    high = jnp.where(parity == 0, other, own)
    return jnp.concatenate([low, high], axis=1)


def everywhere_sum(values):
    if lax.axis_size("batch") != 4 or lax.axis_size("seq") != 4:
        return lax.psum(values, ("batch", "seq"))
    for axis in ("seq", "batch"):
        for bit in (1, 2):
            values = values + swapped(values, axis, bit)
    return values


def per_device(
    hidden,
    norm_gain,
    gate_input_weight,
    w_bc,
    w_dt,
    conv_x,
    conv_bc,
    head_params,
    gate_gain,
    w_out,
    lengths,
    cotangent,
):
    seqs, slots, model = hidden.shape
    rows = seqs * slots
    inner = gate_input_weight.shape[2]
    heads_dev = w_dt.shape[1]
    width = inner // heads_dev
    state = w_bc.shape[1] // 2
    inner_all = inner * lax.axis_size("head")
    heads = LANES // width
    groups = inner // LANES
    side = lax.axis_index("head")
    paired = lax.axis_size("batch") == 4 and lax.axis_size("seq") == 4 and lax.axis_size("head") == 2

    positions = lax.axis_index("seq") * slots + jnp.arange(slots)
    mask = (positions[None, :] < lengths[:, None]).astype(F32).reshape(rows, 1)
    hidden_f = hidden.reshape(rows, model).astype(F32)
    inv_rms = lax.rsqrt(jnp.mean(hidden_f * hidden_f, axis=-1, keepdims=True) + EPSILON)
    normed = (hidden_f * inv_rms * norm_gain).astype(BF16)
    grad_mix = (cotangent.reshape(rows, model).astype(F32) * mask).astype(BF16)
    w_z, w_x = gate_input_weight[:, 0], gate_input_weight[:, 1]

    pre_x = mm(normed, w_x).reshape(seqs, slots, inner)
    pre_bc = mm(normed, w_bc).reshape(seqs, slots, 2 * state)
    proj_dt = mm(normed, w_dt)
    edges = jnp.concatenate([pre_x[:, slots - EDGE :], pre_bc[:, slots - EDGE :]], axis=2)
    edges = shifted(edges, "seq", 1)
    edge_x, edge_bc = edges[..., :inner], edges[..., inner:]
    dtraw = proj_dt.reshape(seqs, slots, groups, heads).transpose(0, 2, 1, 3)
    params = head_params.reshape(3, groups, heads).transpose(1, 0, 2)
    gain = gate_gain.reshape(1, inner)

    grid = (seqs, groups)
    S = jax.ShapeDtypeStruct
    wide = pl.BlockSpec((1, slots, LANES), lambda b, g: (b, 0, g))
    edge = pl.BlockSpec((1, EDGE, LANES), lambda b, g: (b, 0, g))
    states = pl.BlockSpec((1, state, LANES), lambda b, g: (b, 0, g))
    line = pl.BlockSpec((1, 1, LANES), lambda b, g: (b, 0, g))
    taps = pl.BlockSpec((CONV + 1, LANES), lambda b, g: (0, g))
    gain_spec = pl.BlockSpec((1, LANES), lambda b, g: (0, g))
    per_seq = lambda *shape: pl.BlockSpec((1,) + shape, lambda b, g: (b,) + (0,) * len(shape))
    fixed = lambda *shape: pl.BlockSpec(shape, lambda b, g: (0,) * len(shape))
    by_head = lambda k: pl.BlockSpec((1, 1, slots, k), lambda b, g: (b, g, 0, 0))
    par_spec = pl.BlockSpec((1, 3, heads), lambda b, g: (g, 0, 0))
    wide_s = S((seqs, slots, inner), F32)
    wide_b = S((seqs, slots, inner), BF16)
    state_s = S((seqs, state, inner), F32)
    bc_b = S((seqs, slots, state), F32)
    settings = pltpu.CompilerParams(vmem_limit_bytes=VMEM_LIMIT)

    local_out, local_state, total_decay, b_act, c_act, steps = pl.pallas_call(
        functools.partial(local_kernel, heads, width),
        grid=grid,
        in_specs=[
            wide, edge, taps, per_seq(slots, 2 * state), per_seq(EDGE, 2 * state),
            fixed(CONV + 1, 2 * state), by_head(heads), par_spec,
        ],
        out_specs=[wide, states, line, per_seq(slots, state), per_seq(slots, state), by_head(2 * heads)],
        out_shape=[
            wide_s, state_s, S((seqs, 1, inner), F32), bc_b, bc_b,
            S((seqs, groups, slots, 2 * heads), F32),
        ],
        scratch_shapes=[pltpu.VMEM((slots, slots), F32)],
        compiler_params=settings,
        name="scan_local",
    )(pre_x, edge_x, conv_x, pre_bc, edge_bc, conv_bc, dtraw, params)

    entering = passed_on(total_decay, local_state, False)
    gate_z = mm(normed, w_z).reshape(seqs, slots, inner)
    grad_out = mm(grad_mix, w_out, ((1,), (1,))).reshape(seqs, slots, inner)

    y, sums = pl.pallas_call(
        functools.partial(gate_kernel, heads, width),
        grid=grid,
        in_specs=[wide, states, per_seq(slots, state), by_head(2 * heads), wide, wide, gain_spec],
        out_specs=[wide, per_seq(slots, 2)],
        out_shape=[wide_s, S((seqs, slots, 2), F32)],
        compiler_params=settings,
        name="gate",
    )(local_out, entering, c_act, steps, gate_z, grad_out, gain)
    sums = head_sum(sums)

    gated, grad_y, grad_z, gain_grad, leaving = pl.pallas_call(
        functools.partial(gate_back_kernel, heads, width, inner_all),
        grid=grid,
        in_specs=[wide, wide, wide, gain_spec, per_seq(slots, 2), per_seq(slots, state), by_head(2 * heads)],
        out_specs=[wide, wide, wide, line, states],
        out_shape=[wide_b, wide_s, wide_b, S((seqs, 1, inner), F32), state_s],
        compiler_params=settings,
        name="gate_back",
    )(y, gate_z, grad_out, gain, sums, c_act, steps)
    gated = gated.reshape(rows, inner)
    grad_z = grad_z.reshape(rows, inner)

    coming = passed_on(total_decay, leaving, True)

    if paired:
        mix_rows = pair_rows(grad_mix)
        normed_rows = pair_rows(normed)
        grad_w_out = pair_grad(mix_rows, pair_columns(gated)).T
        grad_w_z = pair_grad(normed_rows, pair_columns(grad_z))

    mixed = head_sum(mm(gated, w_out))
    mixed_out = (mask * (hidden_f + mixed)).astype(BF16).reshape(seqs, slots, model)

    (
        grad_pre, tail_x, first_x, taps_grad_x, grad_dt, params_grad, grad_bc,
    ) = pl.pallas_call(
        functools.partial(scan_back_kernel, heads, width),
        grid=grid,
        in_specs=[
            wide, edge, taps, by_head(heads), par_spec, by_head(2 * heads), per_seq(slots, state),
            per_seq(slots, state), wide, wide, states, states,
        ],
        out_specs=[
            wide, edge, edge, edge, by_head(heads),
            pl.BlockSpec((1, 1, 3, heads), lambda b, g: (b, g, 0, 0)), per_seq(slots, 2 * state),
        ],
        out_shape=[
            wide_b, S((seqs, EDGE, inner), F32), S((seqs, EDGE, inner), F32), S((seqs, EDGE, inner), F32),
            S((seqs, groups, slots, heads), F32), S((seqs, groups, 3, heads), F32),
            S((seqs, slots, 2 * state), F32),
        ],
        scratch_shapes=[pltpu.VMEM((slots, slots), F32), pltpu.VMEM((slots, slots), F32)],
        compiler_params=settings,
        name="scan_back",
    )(pre_x, edge_x, conv_x, dtraw, params, steps, b_act, c_act, y, grad_y, entering, coming)
    grad_bc = head_sum(grad_bc)

    one = lambda *shape: pl.BlockSpec((1,) + shape, lambda b: (b, 0, 0))
    rows8 = S((seqs, EDGE, 2 * state), F32)
    grad_pre_bc, tail_bc, first_bc, taps_grad_bc = pl.pallas_call(
        conv_back_kernel,
        grid=(seqs,),
        in_specs=[
            one(slots, 2 * state), one(EDGE, 2 * state),
            pl.BlockSpec((CONV + 1, 2 * state), lambda b: (0, 0)), one(slots, 2 * state),
        ],
        out_specs=[one(slots, 2 * state), one(EDGE, 2 * state), one(EDGE, 2 * state), one(EDGE, 2 * state)],
        out_shape=[S((seqs, slots, 2 * state), BF16), rows8, rows8, rows8],
        compiler_params=settings,
        name="conv_back",
    )(pre_bc, edge_bc, conv_bc, grad_bc)

    def mended(value, tail, first, weights):
        later = shifted(first, "seq", -1)
        add = jnp.zeros_like(tail)
        for tap in range(CONV - 1):
            ahead = CONV - 1 - tap
            moved = jnp.pad(later[:, :ahead], ((0, 0), (EDGE - ahead, 0), (0, 0)))
            add = add + moved * weights[tap]
        return lax.dynamic_update_slice(value, (tail + add).astype(BF16), (0, slots - EDGE, 0))

    grad_pre = mended(grad_pre, tail_x, first_x, conv_x).reshape(rows, inner)
    grad_pre_bc = mended(grad_pre_bc, tail_bc, first_bc, conv_bc).reshape(rows, 2 * state)
    grad_dtr = grad_dt.transpose(0, 2, 1, 3).reshape(rows, heads_dev).astype(BF16)

    portion = mm(grad_z, w_z, ((1,), (1,))) + mm(grad_pre, w_x, ((1,), (1,)))
    portion = portion + mm(grad_dtr, w_dt, ((1,), (1,)))
    grad_normed = head_sum(portion) + mm(grad_pre_bc, w_bc, ((1,), (1,)))
    scaled_input = hidden_f * inv_rms
    grad_norm_gain = jnp.sum(grad_normed * scaled_input, axis=0)
    grad_scaled = grad_normed * norm_gain
    input_dot = jnp.mean(grad_scaled * scaled_input, axis=-1, keepdims=True)
    grad_hidden = grad_mix.astype(F32) + inv_rms * (grad_scaled - scaled_input * input_dot)
    grad_hidden = grad_hidden.reshape(seqs, slots, model)

    if paired:
        bc_half = halves(grad_pre_bc, 1, side)
        fill = jnp.zeros((rows, state - heads_dev), BF16)
        half = inner // 2
        columns = jnp.concatenate(
            [grad_pre[:, :half], bc_half, grad_pre[:, half:], grad_dtr, fill], axis=1
        )
        grad_w_x = pair_grad(normed_rows, pair_columns(columns))
        bc_mine = grad_w_x[:, half : half + state]
        bc_other = swapped(bc_mine, "head", 1)
        grad_w_bc = jnp.concatenate(
            [jnp.where(side == 0, bc_mine, bc_other), jnp.where(side == 0, bc_other, bc_mine)], axis=1
        )
        grad_w_dt = grad_w_x[:, inner + state : inner + state + heads_dev]
        grad_w_x = jnp.concatenate([grad_w_x[:, :half], grad_w_x[:, half + state : inner + state]], axis=1)
        grad_weight = jnp.stack([grad_w_z, grad_w_x], axis=1)
    else:
        scatter = functools.partial(lax.psum_scatter, axis_name=("batch", "seq"), tiled=True)
        over_slots = ((0,), (0,))
        grad_weight = scatter(
            jnp.stack([mm(normed, grad_z, over_slots), mm(normed, grad_pre, over_slots)], axis=1),
            scatter_dimension=0,
        )
        grad_w_bc = scatter(mm(normed, grad_pre_bc, over_slots), scatter_dimension=0)
        grad_w_dt = scatter(mm(normed, grad_dtr, over_slots), scatter_dimension=0)
        grad_w_out = scatter(mm(gated, grad_mix, over_slots), scatter_dimension=1)

    head_grad = params_grad.sum(axis=0).transpose(1, 0, 2).reshape(3, heads_dev)
    taps_sum = jnp.concatenate([taps_grad_x.sum(axis=0), taps_grad_bc.sum(axis=0)], axis=1)[: CONV + 1]
    pieces = [taps_sum, head_grad, gain_grad.sum(axis=0), grad_norm_gain]
    flat = jnp.concatenate([piece.reshape(-1) for piece in pieces])
    flat = everywhere_sum(flat)
    parted, start = [], 0
    for piece in pieces:
        parted.append(flat[start : start + piece.size].reshape(piece.shape))
        start += piece.size
    grad_conv, grad_head, grad_gate_gain, grad_norm_gain = parted
    return (
        mixed_out,
        grad_hidden,
        grad_norm_gain,
        grad_weight,
        grad_w_bc,
        grad_w_dt,
        grad_conv[:, :inner],
        grad_conv[:, inner:],
        grad_head,
        grad_gate_gain.reshape(inner),
        grad_w_out,
    )


def solution(mesh):
    placed = (
        P("batch", "seq", None),
        P(),
        P(None, None, "head"),
        P(),
        P(None, "head"),
        P(None, "head"),
        P(),
        P(None, "head"),
        P("head"),
        P("head", None),
        P("batch"),
        P("batch", "seq", None),
    )
    return jax.shard_map(
        per_device,
        mesh=mesh,
        in_specs=placed,
        out_specs=(
            P("batch", "seq", None),
            P("batch", "seq", None),
            P(),
            P(("batch", "seq"), None, "head"),
            P(("batch", "seq"), None),
            P(("batch", "seq"), "head"),
            P(None, "head"),
            P(),
            P(None, "head"),
            P("head"),
            P("head", ("batch", "seq")),
        ),
        check_vma=False,
    )
```

```python
import functools

import jax
import jax.numpy as jnp
from jax import lax
from jax.experimental import pallas as pl
from jax.experimental.pallas import tpu as pltpu
from jax.sharding import PartitionSpec as P

CONV = 4
EDGE = 8
LANES = 256
EPSILON = 1e-05
HIGHEST = lax.Precision.HIGHEST
F32 = jnp.float32
BF16 = jnp.bfloat16
VMEM_LIMIT = 48 * 1024 * 1024
COST = 0.25


def mm(a, b, dims=((1,), (0,)), precision=None):
    return lax.dot_general(a, b, (dims, ((), ())), precision=precision, preferred_element_type=F32)


def widen(columns, width):
    slots, heads = columns.shape
    lane = lax.broadcasted_iota(jnp.int32, (slots, heads * width), 1) // width
    result = jnp.broadcast_to(columns[:, 0:1], (slots, heads * width))
    for head in range(1, heads):
        result = jnp.where(lane == head, columns[:, head : head + 1], result)
    return result


def head_sums(value, heads):
    lanes = value.shape[1]
    row = lax.broadcasted_iota(jnp.int32, (lanes, heads), 0) // (lanes // heads)
    pick = (row == lax.broadcasted_iota(jnp.int32, (lanes, heads), 1)).astype(BF16)
    high = value.astype(BF16)
    low = (value - high.astype(F32)).astype(BF16)
    return mm(high, pick) + mm(low, pick)


def triangle(slots):
    row = lax.broadcasted_iota(jnp.int32, (slots, slots), 0)
    column = lax.broadcasted_iota(jnp.int32, (slots, slots), 1)
    return (row >= column).astype(F32)


def softplus(value):
    return jnp.maximum(value, 0.0) + jnp.log1p(jnp.exp(-jnp.abs(value)))


def slope(value, sig):
    return sig * (1.0 + value * (1.0 - sig))


def convolved(extended, taps, slots):
    total = taps[CONV : CONV + 1] + extended[EDGE : EDGE + slots] * taps[CONV - 1 : CONV]
    for tap in range(CONV - 1):
        start = EDGE - (CONV - 1) + tap
        total = total + extended[start : start + slots] * taps[tap : tap + 1]
    return total


def convolved_back(grad, extended, taps):
    slots, lanes = grad.shape
    padded = jnp.concatenate([grad, jnp.zeros((EDGE, lanes), F32)], axis=0)
    back = grad * taps[CONV - 1 : CONV]
    rows = []
    for tap in range(CONV):
        start = EDGE - (CONV - 1) + tap
        rows.append(jnp.sum(grad * extended[start : start + slots], axis=0, keepdims=True))
        if tap < CONV - 1:
            ahead = CONV - 1 - tap
            back = back + padded[ahead : ahead + slots] * taps[tap : tap + 1]
    rows.append(jnp.sum(grad, axis=0, keepdims=True))
    rows.append(jnp.zeros((8 - len(rows), lanes), F32))
    return back, jnp.concatenate(rows, axis=0)


def of_head(value, head, heads):
    lane = lax.broadcasted_iota(jnp.int32, value.shape, 1) // (value.shape[1] // heads)
    return jnp.where(lane == head, value, jnp.zeros_like(value))


def call(kernel, inputs, in_specs, out_specs, out_shape, grid, name, micros, scratch=(), after=()):
    count = len(inputs)

    def body(*refs):
        kernel(*refs[:count], *refs[count + len(after) :])

    return pl.pallas_call(
        body,
        grid=grid,
        in_specs=list(in_specs) + [pl.BlockSpec(memory_space=pl.ANY)] * len(after),
        out_specs=out_specs,
        out_shape=out_shape,
        scratch_shapes=list(scratch),
        compiler_params=pltpu.CompilerParams(vmem_limit_bytes=VMEM_LIMIT),
        cost_estimate=pl.CostEstimate(
            flops=int(micros * COST * 1.1e9), bytes_accessed=int(micros * COST * 2e6), transcendentals=0
        ),
        name=name,
    )(*inputs, *after)


def steps_of(dtraw, par, tri):
    step = softplus(dtraw + par[0:1])
    rate = step * -jnp.exp(par[1:2])
    return step, rate, mm(tri, rate, precision=HIGHEST)


def state_kernel(
    heads, width, pre_x, edge_x, taps_x, pre_bc, edge_bc, taps_bc, dtraw, params,
    local_state, total_decay, b_out, c_out, steps_out,
):
    slots = pre_x.shape[1]
    state = b_out.shape[2]

    @pl.when(pl.program_id(1) == 0)
    def _():
        ext = jnp.concatenate([edge_bc[0], pre_bc[0]], axis=0)
        u = convolved(ext, taps_bc[...], slots)
        act = u * jax.nn.sigmoid(u)
        b_out[0] = act[:, :state]
        c_out[0] = act[:, state:]

    ext = jnp.concatenate([edge_x[0], pre_x[0]], axis=0)
    u = convolved(ext, taps_x[...], slots)
    x = u * jax.nn.sigmoid(u)
    step, _, cumul = steps_of(dtraw[0, 0], params[0], triangle(slots))
    steps_out[0, 0] = jnp.concatenate([step, cumul], axis=1)
    last = cumul[slots - 1 : slots]
    total_decay[0] = jnp.broadcast_to(widen(jnp.exp(last), width), (8, heads * width))
    xd = (widen(step, width) * x).astype(BF16)
    tail = (widen(jnp.exp(last - cumul), width) * xd.astype(F32)).astype(BF16)
    local_state[0] = mm(b_out[0].astype(BF16), tail, ((0,), (0,)))


def inside_kernel(heads, width, pre_x, edge_x, taps_x, steps, params, b_act, c_act, local_out, scores):
    slots = pre_x.shape[1]
    tri = triangle(slots)

    @pl.when(pl.program_id(1) == 0)
    def _():
        scores[...] = mm(c_act[0], b_act[0], ((1,), (1,)), HIGHEST) * tri

    ext = jnp.concatenate([edge_x[0], pre_x[0]], axis=0)
    u = convolved(ext, taps_x[...], slots)
    x = u * jax.nn.sigmoid(u)
    par = params[0]
    step, cumul = steps[0, 0][:, :heads], steps[0, 0][:, heads:]
    cumul_t = mm(step * -jnp.exp(par[1:2]), tri, ((0,), (1,)), precision=HIGHEST)
    xd = (widen(step, width) * x).astype(BF16)
    out = widen(par[2:3], width) * x
    for head in range(heads):
        decay = jnp.exp(jnp.minimum(cumul[:, head : head + 1] - cumul_t[head : head + 1], 0.0))
        weights = (scores[...] * decay).astype(BF16)
        out = out + mm(weights, of_head(xd, head, heads))
    local_out[0] = out


def gate_kernel(heads, width, local_out, entering, c_act, steps, z, grad_out, gain, y_out, sums):
    cumul = steps[0, 0][:, heads:]
    inter = mm(c_act[0].astype(BF16), entering[0].astype(BF16))
    y = local_out[0] + widen(jnp.exp(cumul), width) * inter
    y_out[0] = y
    zv = z[0]
    g = y * (zv * jax.nn.sigmoid(zv))
    squares = jnp.sum(g * g, axis=1, keepdims=True)
    dots = jnp.sum(grad_out[0] * gain[...] * g, axis=1, keepdims=True)
    both = jnp.concatenate([squares, dots], axis=1)

    @pl.when(pl.program_id(1) == 0)
    def _():
        sums[0] = both

    @pl.when(pl.program_id(1) > 0)
    def _():
        sums[0] += both


def gate_back_kernel(
    heads, width, inner_all, y, z, grad_out, gain, sums, c_act, steps,
    gated_out, grad_y, grad_z, gain_grad, leaving,
):
    inv = lax.rsqrt(sums[0][:, 0:1] / inner_all + EPSILON)
    mean = inv * sums[0][:, 1:2] / inner_all
    zv, yv = z[0], y[0]
    sig = jax.nn.sigmoid(zv)
    silu = zv * sig
    normed = yv * silu * inv
    gated_out[0] = (normed * gain[...]).astype(BF16)
    gain_grad[0] = jnp.sum(grad_out[0] * normed, axis=0, keepdims=True)
    dg = inv * (grad_out[0] * gain[...] - normed * mean)
    dy = dg * silu
    grad_y[0] = dy
    grad_z[0] = (dg * yv * slope(zv, sig)).astype(BF16)
    growth = widen(jnp.exp(steps[0, 0][:, heads:]), width)
    leaving[0] = mm(c_act[0].astype(BF16), (growth * dy).astype(BF16), ((0,), (0,)))


def inside_back_kernel(
    heads, width, pre_x, edge_x, taps_x, steps, params, b_act, c_act, grad_y, entering,
    grad_xd_out, grad_bc, grad_scores, scores,
):
    slots = pre_x.shape[1]
    tri = triangle(slots)

    @pl.when(pl.program_id(1) == 0)
    def _():
        scores[...] = mm(c_act[0], b_act[0], ((1,), (1,)), HIGHEST) * tri
        grad_scores[...] = jnp.zeros_like(grad_scores)
        grad_bc[...] = jnp.zeros_like(grad_bc)

    ext = jnp.concatenate([edge_x[0], pre_x[0]], axis=0)
    u = convolved(ext, taps_x[...], slots)
    x = u * jax.nn.sigmoid(u)
    par = params[0]
    step, cumul = steps[0, 0][:, :heads], steps[0, 0][:, heads:]
    cumul_t = mm(step * -jnp.exp(par[1:2]), tri, ((0,), (1,)), precision=HIGHEST)
    growth = widen(jnp.exp(cumul), width)
    xd = (widen(step, width) * x).astype(BF16)
    dy = grad_y[0]
    dy_b = dy.astype(BF16)
    grad_xd = jnp.zeros_like(dy)
    total = jnp.zeros((slots, slots), F32)
    for head in range(heads):
        decay = jnp.exp(jnp.minimum(cumul[:, head : head + 1] - cumul_t[head : head + 1], 0.0))
        weights = (scores[...] * decay).astype(BF16)
        mine = of_head(dy_b, head, heads)
        grad_xd = grad_xd + mm(weights, mine, ((0,), (0,)))
        total = total + mm(mine, xd, ((1,), (1,))) * decay
    grad_xd_out[0] = grad_xd
    grad_scores[...] += total
    grad_c = mm((growth * dy).astype(BF16), entering[0].astype(BF16), ((1,), (1,)))
    grad_bc[0] += jnp.concatenate([jnp.zeros_like(grad_c), grad_c], axis=1)

    @pl.when(pl.program_id(1) == pl.num_programs(1) - 1)
    def _():
        causal = grad_scores[...] * tri
        from_c = mm(causal, c_act[0], ((0,), (0,)), HIGHEST)
        grad_bc[0] += jnp.concatenate([from_c, mm(causal, b_act[0], precision=HIGHEST)], axis=1)


def scan_back_kernel(
    heads, width, pre_x, edge_x, taps_x, dtraw, params, steps, b_act, y, grad_y, inside, entering, coming,
    grad_pre, tail_rows, head_rows, taps_grad, grad_dt, params_grad, grad_b,
):
    slots = pre_x.shape[1]
    tri = triangle(slots)

    @pl.when(pl.program_id(1) == 0)
    def _():
        grad_b[...] = jnp.zeros_like(grad_b)

    ext = jnp.concatenate([edge_x[0], pre_x[0]], axis=0)
    u = convolved(ext, taps_x[...], slots)
    sig = jax.nn.sigmoid(u)
    x = u * sig
    par = params[0]
    decay_a = -jnp.exp(par[1:2])
    step = steps[0, 0][:, :heads]
    cumul = steps[0, 0][:, heads:]
    last = cumul[slots - 1 : slots]
    step_wide = widen(step, width)
    tail_wide = widen(jnp.exp(last - cumul), width)
    skip = widen(par[2:3], width)
    xd = (step_wide * x).astype(BF16)
    xd_f = xd.astype(F32)
    dy = grad_y[0]
    coming_b = coming[0].astype(BF16)
    from_next = tail_wide * mm(b_act[0].astype(BF16), coming_b)
    grad_xd = inside[0] + from_next
    grad_b[0] += mm((tail_wide * xd_f).astype(BF16), coming_b, ((1,), (1,)))

    direct = head_sums(x * grad_xd, heads)
    ys = y[0] - skip * x
    moved = head_sums(dy.astype(BF16).astype(F32) * ys - xd_f * grad_xd, heads)
    ends = jnp.exp(widen(last, width)) * jnp.sum(coming[0] * entering[0], axis=0, keepdims=True)
    ends = ends + jnp.sum(xd_f * from_next, axis=0, keepdims=True)
    skips = jnp.sum(dy * x, axis=0, keepdims=True)
    rows = head_sums(jnp.concatenate([ends, skips, jnp.zeros((6, ends.shape[1]), F32)], axis=0), heads)
    later = mm(tri, moved, ((0,), (0,)), precision=HIGHEST) + rows[0:1]
    grad_step = (direct + decay_a * later) * jax.nn.sigmoid(dtraw[0, 0] + par[0:1])
    grad_dt[0, 0] = grad_step
    params_grad[0, 0] = jnp.concatenate(
        [
            jnp.sum(grad_step, axis=0, keepdims=True),
            jnp.sum(step * later, axis=0, keepdims=True) * decay_a,
            rows[1:2],
        ],
        axis=0,
    )
    du = (step_wide * grad_xd + skip * dy) * slope(u, sig)
    back, rows8 = convolved_back(du, ext, taps_x[...])
    grad_pre[0] = back.astype(BF16)
    tail_rows[0] = back[slots - EDGE :]
    head_rows[0] = du[:EDGE]
    taps_grad[0] = rows8


def conv_back_kernel(pre, edge, taps, grad_act, grad_pre, tail_rows, head_rows, taps_grad):
    slots = pre.shape[1]
    ext = jnp.concatenate([edge[0], pre[0]], axis=0)
    u = convolved(ext, taps[...], slots)
    du = grad_act[0] * slope(u, jax.nn.sigmoid(u))
    back, rows8 = convolved_back(du, ext, taps[...])
    grad_pre[0] = back.astype(BF16)
    tail_rows[0] = back[slots - EDGE :]
    head_rows[0] = du[:EDGE]
    taps_grad[0] = rows8


def assemble_kernel(mine, theirs, side, result):
    first = side[0] == 0
    half = mine.shape[2]
    result[0, :, :half] = jnp.where(first, mine[0], theirs[0]).astype(BF16)
    result[0, :, half:] = jnp.where(first, theirs[0], mine[0]).astype(BF16)


def weight_kernel(parts, own_rows, far_rows, *refs):
    result, columns = refs[-2:]
    slots = own_rows.shape[0]

    @pl.when(pl.program_id(0) == 0)
    def _():
        for index in range(parts):
            columns[:, pl.ds(index * slots, slots)] = refs[index][...].T.astype(BF16)

    total = mm(columns[:, :slots], own_rows[...])
    for index in range(1, parts):
        total = total + mm(columns[:, index * slots : (index + 1) * slots], far_rows[index - 1])
    for tile in range(result.shape[0] * result.shape[1]):
        piece = total[:, tile * 128 : (tile + 1) * 128]
        if result.shape[0] == 1:
            result[0, tile] = piece
        else:
            result[tile, 0] = piece


def swapped(value, axis, bit):
    count = lax.axis_size(axis)
    return lax.ppermute(value, axis, [(i, i ^ bit) for i in range(count)])


def shifted(value, axis, steps):
    count = lax.axis_size(axis)
    initial, last = (max(0, -steps), min(count, count - steps))
    return lax.ppermute(value, axis, [(source, source + steps) for source in range(initial, last)])


def head_sum(value):
    if lax.axis_size("head") == 2:
        return value + swapped(value, "head", 1)
    return lax.psum(value, "head")


def gathered_pass(decay, part, reverse):
    count = lax.axis_size("seq")
    place = lax.axis_index("seq")
    gathered = lax.all_gather(jnp.concatenate([part, decay], axis=1), "seq")
    rows = part.shape[1]
    state = jnp.zeros_like(part)
    for turn in range(count - 1):
        source = count - 1 - turn if reverse else turn
        ahead = source > place if reverse else source < place
        later = gathered[source, :, rows : rows + 1] * state + gathered[source, :, :rows]
        state = jnp.where(ahead, later, state)
    return state


def chosen(pieces, index):
    low = jnp.where(index % 2 == 0, pieces[0], pieces[1])
    high = jnp.where(index % 2 == 0, pieces[2], pieces[3])
    return jnp.where(index < 2, low, high)


def quarter(value, axis, index):
    size = value.shape[axis] // 4
    return lax.dynamic_slice_in_dim(value, index * size, size, axis)


def tied(*values):
    return lax.optimization_barrier(values)


def passed_on(decay, part, reverse, first, second):
    if lax.axis_size("seq") != 4:
        beside_first = first()
        return gathered_pass(decay, part, reverse), beside_first, second(beside_first)
    place = lax.axis_index("seq")
    rows = part.shape[1]
    both = jnp.concatenate([part, decay], axis=1)
    got = [quarter(both, 2, place)] + [swapped(quarter(both, 2, place ^ d), "seq", d) for d in (1, 2, 3)]
    got, beside_first = tied(got, first())
    order = (3, 2, 1, 0) if reverse else (0, 1, 2, 3)
    state = jnp.zeros_like(got[0][:, :rows])
    enters = [None] * 4
    for source in order:
        enters[source] = state
        if source != order[-1]:
            piece = chosen(got, place ^ source)
            state = piece[:, rows : rows + 1] * state + piece[:, :rows]
    back = [chosen(enters, place)] + [swapped(chosen(enters, place ^ d), "seq", d) for d in (1, 2, 3)]
    back, beside_second = tied(back, second(beside_first))
    entering = jnp.concatenate([chosen(back, place ^ index) for index in range(4)], axis=2)
    return entering, beside_first, beside_second


def halves(value, axis, which):
    size = value.shape[axis] // 2
    return lax.dynamic_slice_in_dim(value, which * size, size, axis)


def core_half(value):
    return halves(value.astype(F32), 1, lax.axis_index("head"))


def rows_of_seq_first(half):
    cut = half.shape[1] // 2
    a, b = half[:, :cut], half[:, cut:]
    return a, b, swapped(a, "seq", 1), swapped(b, "seq", 2)


def rows_of_seq_second(a, b, a1, b2):
    return a1, swapped(jnp.stack([a, a1]), "seq", 2), b2, swapped(jnp.stack([b, b2]), "seq", 1)


def rows_of_seq_third(a1, a23, b2, b13):
    high = jnp.stack([b13[0], b2, b13[1]])
    return jnp.concatenate([jnp.concatenate([a1[None], a23], axis=0), high], axis=2)


def assembled(mine):
    side = lax.axis_index("head").reshape(1)
    theirs = swapped(mine, "head", 1)
    count, slots, half = mine.shape
    block = pl.BlockSpec((1, slots, half), lambda i: (i, 0, 0))
    return call(
        assemble_kernel,
        [mine, theirs, side],
        [block, block, pl.BlockSpec(memory_space=pltpu.SMEM)],
        pl.BlockSpec((1, slots, 2 * half), lambda i: (i, 0, 0)),
        jax.ShapeDtypeStruct((count, slots, 2 * half), BF16),
        (count,),
        "assemble",
        3 * count,
    )


def columns_of(value, axis, dim=1):
    place = lax.axis_index(axis)
    piece = lambda index: quarter(value, dim, index).astype(F32)
    return [piece(place)] + [swapped(piece(place ^ d), axis, d) for d in (1, 2, 3)]


def weight_part(own_rows, far_rows, columns, axis, after=()):
    slots, model = own_rows.shape
    size = columns[0].shape[1]
    parts = len(columns)
    whole = lambda a: pl.BlockSpec(a.shape, lambda i: (0,) * a.ndim)
    if axis == "seq":
        out_spec = pl.BlockSpec((1, 4, size, 128), lambda i: (i, 0, 0, 0))
    else:
        out_spec = pl.BlockSpec((4, 1, size, 128), lambda i: (0, i, 0, 0))
    return call(
        functools.partial(weight_kernel, parts),
        [own_rows, far_rows, *columns],
        [
            pl.BlockSpec((slots, model // 4), lambda i: (0, i)),
            pl.BlockSpec((parts - 1, slots, model // 4), lambda i: (0, 0, i)),
            *[whole(c) for c in columns],
        ],
        out_spec,
        jax.ShapeDtypeStruct((4, 4, size, 128), F32),
        (4,),
        "weight_part",
        9,
        scratch=[pltpu.VMEM((size, parts * slots), BF16)],
        after=after,
    )


def scattered_over_seq(part):
    place = lax.axis_index("seq")
    sx, sy = place % 2, place // 2
    part = part.reshape((2, 2) + part.shape[1:])
    pick = lambda value, axis, index: lax.dynamic_index_in_dim(value, index, axis, False)
    a, b = part[:, :, :2], part[:, :, 2:]
    a = pick(a, 1, sx) + swapped(pick(a, 1, 1 - sx), "seq", 1)
    b = pick(b, 0, sy) + swapped(pick(b, 0, 1 - sy), "seq", 2)
    a = pick(a, 0, sy) + swapped(pick(a, 0, 1 - sy), "seq", 2)
    b = pick(b, 0, sx) + swapped(pick(b, 0, 1 - sx), "seq", 1)
    return jnp.concatenate([a, b], axis=0)


def weight_done(part):
    summed = lax.psum_scatter(part, "batch", scatter_dimension=0, tiled=True)[0]
    place = lax.axis_index("seq")
    take = lambda index: lax.dynamic_index_in_dim(summed, index, 0, False)
    back = [take(place)] + [swapped(take(place ^ d), "seq", d) for d in (1, 2, 3)]
    return jnp.stack([chosen(back, place ^ index) for index in range(4)])


def pair_done(part):
    z = lax.axis_index("batch")
    parity, upper = z % 2, z // 2
    pick = lambda value, index: lax.dynamic_index_in_dim(value, index, 0, False)
    both = scattered_over_seq(part).reshape((2, 2) + part.shape[2:])
    both = pick(both, upper) + swapped(pick(both, 1 - upper), "batch", 2)
    own, other = pick(both, parity), swapped(pick(both, 1 - parity), "batch", 1)
    return jnp.concatenate([jnp.where(parity == 0, own, other), jnp.where(parity == 0, other, own)], axis=0)


def small_done(part):
    z, s = lax.axis_index("batch"), lax.axis_index("seq")
    part = part.reshape(-1, 2, 2, 2, 2, part.shape[1] // 16).transpose(4, 3, 1, 2, 0, 5)
    for axis, bit, index in (("seq", 1, s % 2), ("seq", 2, s // 2), ("batch", 2, z // 2), ("batch", 1, z % 2)):
        pick = lambda which: lax.dynamic_index_in_dim(part, which, 0, False)
        part = pick(index) + swapped(pick(1 - index), axis, bit)
    return part


def everywhere_sum(values):
    if lax.axis_size("batch") != 4 or lax.axis_size("seq") != 4:
        return lax.psum(values, ("batch", "seq"))
    for axis in ("seq", "batch"):
        for bit in (1, 2):
            values = values + swapped(values, axis, bit)
    return values


def per_device(
    hidden,
    norm_gain,
    gate_input_weight,
    w_bc,
    w_dt,
    conv_x,
    conv_bc,
    head_params,
    gate_gain,
    w_out,
    lengths,
    cotangent,
):
    seqs, slots, model = hidden.shape
    rows = seqs * slots
    inner = gate_input_weight.shape[2]
    heads_dev = w_dt.shape[1]
    width = inner // heads_dev
    state = w_bc.shape[1] // 2
    inner_all = inner * lax.axis_size("head")
    heads = LANES // width
    groups = inner // LANES
    side = lax.axis_index("head")
    paired = lax.axis_size("batch") == 4 and lax.axis_size("seq") == 4 and lax.axis_size("head") == 2

    positions = lax.axis_index("seq") * slots + jnp.arange(slots)
    mask = (positions[None, :] < lengths[:, None]).astype(F32).reshape(rows, 1)
    hidden_f = hidden.reshape(rows, model).astype(F32)
    inv_rms = lax.rsqrt(jnp.mean(hidden_f * hidden_f, axis=-1, keepdims=True) + EPSILON)
    normed = (hidden_f * inv_rms * norm_gain).astype(BF16)
    grad_mix = (cotangent.reshape(rows, model).astype(F32) * mask).astype(BF16)
    if paired:
        seq_first = rows_of_seq_first(core_half(normed))
        mix_far = swapped(core_half(grad_mix), "batch", 1)

    pre_bc = mm(normed, w_bc).reshape(seqs, slots, 2 * state)
    proj_dt = mm(normed, w_dt)
    projected = jnp.einsum("tg,gjn->tjn", normed, gate_input_weight, preferred_element_type=F32)
    gate_z = projected[:, 0].reshape(seqs, slots, inner)
    pre_x = projected[:, 1].reshape(seqs, slots, inner)
    edges = jnp.concatenate([pre_x[:, slots - EDGE :], pre_bc[:, slots - EDGE :]], axis=2)
    edges = shifted(edges, "seq", 1)
    edge_x, edge_bc = edges[..., :inner], edges[..., inner:]
    dtraw = proj_dt.reshape(seqs, slots, groups, heads).transpose(0, 2, 1, 3)
    params = head_params.reshape(3, groups, heads).transpose(1, 0, 2)
    gain = gate_gain.reshape(1, inner)

    grid = (seqs, groups)
    S = jax.ShapeDtypeStruct
    wide = pl.BlockSpec((1, slots, LANES), lambda b, g: (b, 0, g))
    edge = pl.BlockSpec((1, EDGE, LANES), lambda b, g: (b, 0, g))
    states = pl.BlockSpec((1, state, LANES), lambda b, g: (b, 0, g))
    line = pl.BlockSpec((1, 1, LANES), lambda b, g: (b, 0, g))
    taps = pl.BlockSpec((CONV + 1, LANES), lambda b, g: (0, g))
    gain_spec = pl.BlockSpec((1, LANES), lambda b, g: (0, g))
    per_seq = lambda *shape: pl.BlockSpec((1,) + shape, lambda b, g: (b,) + (0,) * len(shape))
    fixed = lambda *shape: pl.BlockSpec(shape, lambda b, g: (0,) * len(shape))
    by_head = lambda k: pl.BlockSpec((1, 1, slots, k), lambda b, g: (b, g, 0, 0))
    par_spec = pl.BlockSpec((1, 3, heads), lambda b, g: (g, 0, 0))
    wide_s = S((seqs, slots, inner), F32)
    wide_b = S((seqs, slots, inner), BF16)
    state_s = S((seqs, state, inner), F32)
    bc_b = S((seqs, slots, state), F32)
    settings = pltpu.CompilerParams(vmem_limit_bytes=VMEM_LIMIT)

    local_state, total_decay, b_act, c_act, steps = call(
        functools.partial(state_kernel, heads, width),
        [pre_x, edge_x, conv_x, pre_bc, edge_bc, conv_bc, dtraw, params],
        [
            wide, edge, taps, per_seq(slots, 2 * state), per_seq(EDGE, 2 * state),
            fixed(CONV + 1, 2 * state), by_head(heads), par_spec,
        ],
        [states, edge, per_seq(slots, state), per_seq(slots, state), by_head(2 * heads)],
        [
            state_s, S((seqs, EDGE, inner), F32), bc_b, bc_b,
            S((seqs, groups, slots, 2 * heads), F32),
        ],
        grid,
        "scan_state",
        17,
    )
    if paired:
        local_state, seq_first, grad_mix, steps = tied(local_state, seq_first, grad_mix, steps)

    def mix_back():
        return mm(grad_mix, w_out, ((1,), (1,))).reshape(seqs, slots, inner)

    def scan_inside(_):
        return call(
            functools.partial(inside_kernel, heads, width),
            [pre_x, edge_x, conv_x, steps, params, b_act, c_act],
            [wide, edge, taps, by_head(2 * heads), par_spec, per_seq(slots, state), per_seq(slots, state)],
            wide,
            wide_s,
            grid,
            "scan_inside",
            18,
            scratch=[pltpu.VMEM((slots, slots), F32)],
        )

    entering, grad_out, local_out = passed_on(total_decay, local_state, False, mix_back, scan_inside)
    if paired:
        entering, mix_far, seq_first = tied(entering, mix_far, seq_first)
        seq_second = rows_of_seq_second(*seq_first)

    y, sums = call(
        functools.partial(gate_kernel, heads, width),
        [local_out, entering, c_act, steps, gate_z, grad_out, gain],
        [wide, states, per_seq(slots, state), by_head(2 * heads), wide, wide, gain_spec],
        [wide, per_seq(slots, 2)],
        [wide_s, S((seqs, slots, 2), F32)],
        grid,
        "gate",
        15,
    )
    sums = head_sum(sums)

    gated, grad_y, grad_z, gain_grad, leaving = call(
        functools.partial(gate_back_kernel, heads, width, inner_all),
        [y, gate_z, grad_out, gain, sums, c_act, steps],
        [wide, wide, wide, gain_spec, per_seq(slots, 2), per_seq(slots, state), by_head(2 * heads)],
        [wide, wide, wide, line, states],
        [wide_b, wide_s, wide_b, S((seqs, 1, inner), F32), state_s],
        grid,
        "gate_back",
        17,
    )
    gated = gated.reshape(rows, inner)
    grad_z = grad_z.reshape(rows, inner)

    def scan_inside_back():
        inside, grad_bc = call(
            functools.partial(inside_back_kernel, heads, width),
            [pre_x, edge_x, conv_x, steps, params, b_act, c_act, grad_y, entering],
            [
                wide, edge, taps, by_head(2 * heads), par_spec, per_seq(slots, state), per_seq(slots, state),
                wide, states,
            ],
            [wide, per_seq(slots, 2 * state)],
            [wide_s, S((seqs, slots, 2 * state), F32)],
            grid,
            "scan_inside_back",
            26,
            scratch=[pltpu.VMEM((slots, slots), F32), pltpu.VMEM((slots, slots), F32)],
        )
        if not paired:
            return inside, grad_bc
        return inside, grad_bc, seq_second

    def rows_ready(beside):
        if not paired:
            return ()
        return assembled(rows_of_seq_third(*beside[2])), gated_far, mm(gated, w_out)

    if paired:
        parity = lax.axis_index("batch") % 2
        gated_own = halves(gated, 1, parity).astype(F32)
        gated_far = swapped(halves(gated, 1, 1 - parity).astype(F32), "batch", 1)

    coming, beside, ready = passed_on(total_decay, leaving, True, scan_inside_back, rows_ready)
    inside, grad_bc = beside[:2]
    if paired:
        normed_far, gated_far, mixed = ready
        coming, grad_z_sent, ready = tied(coming, grad_z, ready)
        z_columns = columns_of(grad_z_sent, "seq")
    else:
        mixed = mm(gated, w_out)
    mixed = head_sum(mixed)
    mixed_out = (mask * (hidden_f + mixed)).astype(BF16).reshape(seqs, slots, model)

    grad_pre, tail_x, first_x, taps_grad_x, grad_dt, params_grad, grad_b = call(
        functools.partial(scan_back_kernel, heads, width),
        [pre_x, edge_x, conv_x, dtraw, params, steps, b_act, y, grad_y, inside, entering, coming],
        [
            wide, edge, taps, by_head(heads), par_spec, by_head(2 * heads), per_seq(slots, state),
            wide, wide, wide, states, states,
        ],
        [
            wide, edge, edge, edge, by_head(heads),
            pl.BlockSpec((1, 1, 3, heads), lambda b, g: (b, g, 0, 0)), per_seq(slots, state),
        ],
        [
            wide_b, S((seqs, EDGE, inner), F32), S((seqs, EDGE, inner), F32), S((seqs, EDGE, inner), F32),
            S((seqs, groups, slots, heads), F32), S((seqs, groups, 3, heads), F32),
            S((seqs, slots, state), F32),
        ],
        grid,
        "scan_back",
        34,
    )
    if paired:
        grad_pre, z_columns, grad_dt, grad_b = tied(grad_pre, z_columns, grad_dt, grad_b)
    grad_bc = grad_bc + jnp.pad(grad_b, ((0, 0), (0, 0), (0, state)))
    grad_bc = head_sum(grad_bc)

    one = lambda *shape: pl.BlockSpec((1,) + shape, lambda b: (b, 0, 0))
    rows8 = S((seqs, EDGE, 2 * state), F32)
    grad_pre_bc, tail_bc, first_bc, taps_grad_bc = call(
        conv_back_kernel,
        [pre_bc, edge_bc, conv_bc, grad_bc],
        [
            one(slots, 2 * state), one(EDGE, 2 * state),
            pl.BlockSpec((CONV + 1, 2 * state), lambda b: (0, 0)), one(slots, 2 * state),
        ],
        [one(slots, 2 * state), one(EDGE, 2 * state), one(EDGE, 2 * state), one(EDGE, 2 * state)],
        [S((seqs, slots, 2 * state), BF16), rows8, rows8, rows8],
        (seqs,),
        "conv_back",
        3,
    )

    def mended(value, tail, first, weights):
        later = shifted(first, "seq", -1)
        add = jnp.zeros_like(tail)
        for tap in range(CONV - 1):
            ahead = CONV - 1 - tap
            moved = jnp.pad(later[:, :ahead], ((0, 0), (EDGE - ahead, 0), (0, 0)))
            add = add + moved * weights[tap]
        return lax.dynamic_update_slice(value, (tail + add).astype(BF16), (0, slots - EDGE, 0))

    grad_pre = mended(grad_pre, tail_x, first_x, conv_x).reshape(rows, inner)
    grad_pre_bc = mended(grad_pre_bc, tail_bc, first_bc, conv_bc).reshape(rows, 2 * state)
    grad_dtr = grad_dt.transpose(0, 2, 1, 3).reshape(rows, heads_dev).astype(BF16)

    grad_zx = jnp.stack([grad_z, grad_pre], axis=1)
    if paired:
        x_columns = columns_of(grad_pre, "seq")
        part_z = weight_part(normed, normed_far, z_columns, "seq")
        grad_w_z = weight_done(part_z)
        part_out = weight_part(grad_mix, assembled(mix_far[None]), [gated_own, gated_far], "batch", after=(part_z,))
        x_columns, part_out = tied(x_columns, part_out)
        part_x = weight_part(normed, normed_far, x_columns, "seq")
        grad_w_x = weight_done(part_x)
        small = jnp.concatenate([halves(grad_pre_bc, 1, side), grad_dtr], axis=1)
        part_small = mm(small, normed, ((0,), (0,)))
        part_x, part_small, grad_zx = tied(part_x, part_small, grad_zx)
        grad_w_out = pair_done(part_out)
        done_small = small_done(part_small)
        bc_mine = done_small[:state]
        bc_other = swapped(bc_mine, "head", 1)
        grad_w_bc = jnp.concatenate(
            [jnp.where(side == 0, bc_mine, bc_other), jnp.where(side == 0, bc_other, bc_mine)], axis=0
        ).T
        grad_w_dt = done_small[state:].T
        grad_weight = jnp.stack(
            [grad_w_z.reshape(inner, model // 16).T, grad_w_x.reshape(inner, model // 16).T], axis=1
        )
    else:
        scatter = functools.partial(lax.psum_scatter, axis_name=("batch", "seq"), tiled=True)
        over_slots = ((0,), (0,))
        grad_weight = scatter(
            jnp.stack([mm(normed, grad_z, over_slots), mm(normed, grad_pre, over_slots)], axis=1),
            scatter_dimension=0,
        )
        grad_w_bc = scatter(mm(normed, grad_pre_bc, over_slots), scatter_dimension=0)
        grad_w_dt = scatter(mm(normed, grad_dtr, over_slots), scatter_dimension=0)
        grad_w_out = scatter(mm(gated, grad_mix, over_slots), scatter_dimension=1)

    portion = jnp.einsum("tjn,gjn->tg", grad_zx, gate_input_weight, preferred_element_type=F32)
    portion = portion + mm(grad_dtr, w_dt, ((1,), (1,)))
    grad_normed = head_sum(portion) + mm(grad_pre_bc, w_bc, ((1,), (1,)))
    scaled_input = hidden_f * inv_rms
    grad_norm_gain = jnp.sum(grad_normed * scaled_input, axis=0)
    grad_scaled = grad_normed * norm_gain
    input_dot = jnp.mean(grad_scaled * scaled_input, axis=-1, keepdims=True)
    grad_hidden = grad_mix.astype(F32) + inv_rms * (grad_scaled - scaled_input * input_dot)
    grad_hidden = grad_hidden.reshape(seqs, slots, model)

    head_grad = params_grad.sum(axis=0).transpose(1, 0, 2).reshape(3, heads_dev)
    taps_sum = jnp.concatenate([taps_grad_x.sum(axis=0), taps_grad_bc.sum(axis=0)], axis=1)[: CONV + 1]
    pieces = [taps_sum, head_grad, gain_grad.sum(axis=0), grad_norm_gain]
    flat = jnp.concatenate([piece.reshape(-1) for piece in pieces])
    flat = everywhere_sum(flat)
    parted, start = [], 0
    for piece in pieces:
        parted.append(flat[start : start + piece.size].reshape(piece.shape))
        start += piece.size
    grad_conv, grad_head, grad_gate_gain, grad_norm_gain = parted
    return (
        mixed_out,
        grad_hidden,
        grad_norm_gain,
        grad_weight,
        grad_w_bc,
        grad_w_dt,
        grad_conv[:, :inner],
        grad_conv[:, inner:],
        grad_head,
        grad_gate_gain.reshape(inner),
        grad_w_out,
    )


def solution(mesh):
    placed = (
        P("batch", "seq", None),
        P(),
        P(None, None, "head"),
        P(),
        P(None, "head"),
        P(None, "head"),
        P(),
        P(None, "head"),
        P("head"),
        P("head", None),
        P("batch"),
        P("batch", "seq", None),
    )
    return jax.shard_map(
        per_device,
        mesh=mesh,
        in_specs=placed,
        out_specs=(
            P("batch", "seq", None),
            P("batch", "seq", None),
            P(),
            P(("batch", "seq"), None, "head"),
            P(("batch", "seq"), None),
            P(("batch", "seq"), "head"),
            P(None, "head"),
            P(),
            P(None, "head"),
            P("head"),
            P("head", ("batch", "seq")),
        ),
        check_vma=False,
    )
```

```python
import functools

import jax
import jax.numpy as jnp
from jax import lax
from jax.experimental import pallas as pl
from jax.experimental.pallas import tpu as pltpu
from jax.sharding import PartitionSpec as P

CONV = 4
EDGE = 8
LANES = 512
EPSILON = 1e-05
HIGHEST = lax.Precision.HIGHEST
F32 = jnp.float32
BF16 = jnp.bfloat16
VMEM_LIMIT = 48 * 1024 * 1024
COST = 0.25


def mm(a, b, dims=((1,), (0,)), precision=None):
    return lax.dot_general(a, b, (dims, ((), ())), precision=precision, preferred_element_type=F32)


def split(value, count):
    parts, rest = [], value
    for _ in range(count):
        part = rest.astype(BF16).astype(F32)
        parts.append(part)
        rest = rest - part
    return jnp.concatenate(parts, axis=0)


def of_head(rows, columns, heads):
    head = lax.broadcasted_iota(jnp.int32, (rows, columns), 0) % heads
    lane = lax.broadcasted_iota(jnp.int32, (rows, columns), 1) // (columns // heads)
    return (head == lane).astype(F32).astype(BF16)


def widen(rows, lanes):
    heads = rows.shape[0]
    return mm(split(rows, 2).astype(BF16), of_head(2 * heads, lanes, heads), ((0,), (0,)))


def head_sums(value, heads, parts=2):
    pick = of_head(heads, value.shape[1], heads)
    high = value.astype(BF16)
    total = mm(pick, high, ((1,), (1,)))
    if parts == 2:
        total = total + mm(pick, (value - high.astype(F32)).astype(BF16), ((1,), (1,)))
    return total


def row_sums(value):
    ones = jnp.ones((8, value.shape[1]), BF16)
    high = value.astype(BF16)
    return mm(ones, high, ((1,), (1,))) + mm(ones, (value - high.astype(F32)).astype(BF16), ((1,), (1,)))


def exact(rows, matrix, dims=((1,), (0,))):
    heads = rows.shape[0]
    result = mm(split(rows, 3).astype(BF16), matrix, dims)
    return result[:heads] + result[heads : 2 * heads] + result[2 * heads :]


def spreads(cumul):
    heads, slots = cumul.shape
    parts = split(cumul, 3)
    row = lax.broadcasted_iota(jnp.int32, parts.shape, 0) % heads

    def spread(head, start, size, end):
        mask = (row == head).astype(F32)
        left = jnp.concatenate([parts, mask], axis=0).astype(BF16)
        right = jnp.concatenate([mask, -parts], axis=0).astype(BF16)
        return mm(left[:, start : start + size], right[:, :end], ((0,), (0,)))

    return spread


def triangle(slots, dtype=F32):
    row = lax.broadcasted_iota(jnp.int32, (slots, slots), 0)
    column = lax.broadcasted_iota(jnp.int32, (slots, slots), 1)
    return (row >= column).astype(F32).astype(dtype)


def softplus(value):
    return jnp.maximum(value, 0.0) + jnp.log1p(jnp.exp(-jnp.abs(value)))


def slope(value, sig):
    return sig * (1.0 + value * (1.0 - sig))


def convolved(extended, taps, slots):
    total = taps[CONV : CONV + 1] + extended[EDGE : EDGE + slots] * taps[CONV - 1 : CONV]
    for tap in range(CONV - 1):
        start = EDGE - (CONV - 1) + tap
        total = total + extended[start : start + slots] * taps[tap : tap + 1]
    return total


def convolved_back(grad, pre, before, taps):
    slots, lanes = grad.shape
    padded = jnp.concatenate([grad, jnp.zeros((EDGE, lanes), F32)], axis=0)
    row = lax.broadcasted_iota(jnp.int32, (EDGE, lanes), 0)
    back = grad * taps[CONV - 1 : CONV]
    rows = []
    for tap in range(CONV - 1):
        ahead = CONV - 1 - tap
        moved = padded[ahead : ahead + slots]
        back = back + moved * taps[tap : tap + 1]
        first = jnp.where(row >= EDGE - ahead, pltpu.roll(grad[:EDGE], EDGE - ahead, 0), 0.0)
        total = jnp.sum(moved * pre, axis=0, keepdims=True)
        rows.append(total + jnp.sum(first * before, axis=0, keepdims=True))
    rows.append(jnp.sum(grad * pre, axis=0, keepdims=True))
    rows.append(jnp.sum(grad, axis=0, keepdims=True))
    rows.append(jnp.zeros((8 - len(rows), lanes), F32))
    return back, jnp.concatenate(rows, axis=0)


def pair_part_of(value, side, width):
    lane = lax.broadcasted_iota(jnp.int32, value.shape, 1) // width
    return jnp.where(lane == side, value, jnp.zeros_like(value))


def call(kernel, inputs, in_specs, out_specs, out_shape, grid, name, micros, scratch=(), index=None):
    scalars = () if index is None else (index.reshape(1),)
    return pl.pallas_call(
        kernel,
        grid_spec=pltpu.PrefetchScalarGridSpec(
            num_scalar_prefetch=len(scalars),
            grid=grid,
            in_specs=list(in_specs),
            out_specs=out_specs,
            scratch_shapes=list(scratch),
        ),
        out_shape=out_shape,
        compiler_params=pltpu.CompilerParams(vmem_limit_bytes=VMEM_LIMIT),
        cost_estimate=pl.CostEstimate(
            flops=int(micros * COST * 1.1e9), bytes_accessed=int(micros * COST * 2e6), transcendentals=0
        ),
        name=name,
    )(*scalars, *inputs)


def state_kernel(
    heads, pre_x, edge_x, taps_x, pre_bc, edge_bc, taps_bc, dtraw, params,
    local_state, total_decay, u_out, b_out, c_out, steps_out, b_turned,
):
    slots, lanes = pre_x.shape[1:]
    state = b_out.shape[2]

    @pl.when(pl.program_id(1) == 0)
    def _():
        ext = jnp.concatenate([edge_bc[0], pre_bc[0]], axis=0)
        u = convolved(ext, taps_bc[...], slots)
        act = u * jax.nn.sigmoid(u)
        b_out[0] = act[:, :state]
        c_out[0] = act[:, state:]
        b_turned[...] = act[:, :state].T.astype(BF16)

    ext = jnp.concatenate([edge_x[0], pre_x[0]], axis=0)
    u = convolved(ext, taps_x[...], slots)
    u_out[0] = u
    x = u * jax.nn.sigmoid(u)
    par = params[0]
    step = softplus(dtraw[0, 0] + par[:, 0:1])
    rate = step * -jnp.exp(par[:, 1:2])
    cumul = exact(rate, triangle(slots, BF16), ((1,), (1,)))
    steps_out[0, 0] = jnp.concatenate([step, cumul], axis=0)
    last = cumul[:, slots - 1 : slots]
    total_decay[0] = widen(jnp.broadcast_to(jnp.exp(last), (heads, 8)), lanes)
    xd = (widen(step, lanes) * x).astype(BF16)
    tail = (widen(jnp.exp(last - cumul), lanes) * xd.astype(F32)).astype(BF16)
    local_state[0] = mm(b_turned[...], tail)


def inside_kernel(heads, width, u, steps, params, b_act, c_act, local_out, scores):
    slots, lanes = u.shape[1:]

    @pl.when(pl.program_id(1) == 0)
    def _():
        scores[...] = mm(c_act[0], b_act[0], ((1,), (1,)), HIGHEST) * triangle(slots)

    uv = u[0]
    x = uv * jax.nn.sigmoid(uv)
    step, cumul = steps[0, 0][:heads], steps[0, 0][heads:]
    spread = spreads(cumul)
    xd = (widen(step, lanes) * x).astype(BF16)
    skip = widen(jnp.broadcast_to(params[0][:, 2:3], (heads, 8)), lanes)[0:1] * x
    half = slots // 2
    for pair in range(heads // 2):
        at = slice(pair * 2 * width, (pair + 1) * 2 * width)
        top, low = skip[:half, at], skip[half:, at]
        for side in range(2):
            head = 2 * pair + side
            mine = pair_part_of(xd[:, at], side, width)
            decay = jnp.exp(jnp.minimum(spread(head, 0, half, half), 0.0))
            top = top + mm((scores[:half, :half] * decay).astype(BF16), mine[:half])
            decay = jnp.exp(jnp.minimum(spread(head, half, half, slots), 0.0))
            low = low + mm((scores[half:] * decay).astype(BF16), mine)
        local_out[0, :half, at] = top
        local_out[0, half:, at] = low


def gate_kernel(heads, local_out, entering, c_act, steps, z, grad_out, gain, y_out, sums):
    lanes = z.shape[-1]
    growth = widen(jnp.exp(steps[0, 0][heads:]), lanes)
    y = local_out[0] + growth * mm(c_act[0].astype(BF16), entering[0].astype(BF16))
    y_out[0] = y
    zv = z[0]
    g = y * (zv * jax.nn.sigmoid(zv))
    squares = row_sums(g * g)
    dots = row_sums(grad_out[0] * gain[...] * g)
    row = lax.broadcasted_iota(jnp.int32, squares.shape, 0)
    both = jnp.where(row == 0, squares, jnp.where(row == 1, dots, 0.0))

    @pl.when(pl.program_id(1) == 0)
    def _():
        sums[0] = both

    @pl.when(pl.program_id(1) > 0)
    def _():
        sums[0] += both


def gate_back_kernel(
    heads, inner_all, y, z, grad_out, gain, sums, c_act, steps,
    gated_out, grad_y, grad_z, gain_grad, leaving, c_turned,
):
    lanes = z.shape[-1]

    @pl.when(pl.program_id(1) == 0)
    def _():
        c_turned[...] = c_act[0].T.astype(BF16)

    inv_row = lax.rsqrt(sums[0][0:1] / inner_all + EPSILON)
    mean_row = inv_row * sums[0][1:2] / inner_all
    rows = jnp.concatenate([split(inv_row, 2), split(mean_row, 2), jnp.zeros_like(sums[0][:4])], axis=0)
    row = lax.broadcasted_iota(jnp.int32, (8, lanes), 0)
    rows = rows.astype(BF16)
    inv = mm(rows, (row < 2).astype(F32).astype(BF16), ((0,), (0,)))
    mean = mm(rows, ((row >= 2) & (row < 4)).astype(F32).astype(BF16), ((0,), (0,)))
    zv, yv = z[0], y[0]
    sig = jax.nn.sigmoid(zv)
    silu = zv * sig
    normed = yv * silu * inv
    gated_out[0] = (normed * gain[...]).astype(BF16)
    gain_grad[0] = jnp.sum(grad_out[0] * normed, axis=0, keepdims=True)
    dg = inv * (grad_out[0] * gain[...] - normed * mean)
    dy = dg * silu
    grad_y[0] = dy
    grad_z[0] = (dg * yv * slope(zv, sig)).astype(BF16)
    growth = widen(jnp.exp(steps[0, 0][heads:]), lanes)
    leaving[0] = mm(c_turned[...], (growth * dy).astype(BF16))


def inside_back_kernel(
    heads, width, u, steps, b_act, c_act, grad_y, entering,
    grad_xd_out, grad_bc, grad_scores, scores,
):
    slots, lanes = u.shape[1:]

    @pl.when(pl.program_id(1) == 0)
    def _():
        scores[...] = mm(c_act[0], b_act[0], ((1,), (1,)), HIGHEST) * triangle(slots)
        grad_scores[...] = jnp.zeros_like(grad_scores)
        grad_bc[...] = jnp.zeros_like(grad_bc)

    uv = u[0]
    step, cumul = steps[0, 0][:heads], steps[0, 0][heads:]
    spread = spreads(cumul)
    xd = (widen(step, lanes) * (uv * jax.nn.sigmoid(uv))).astype(BF16)
    dy = grad_y[0]
    dy_b = dy.astype(BF16)
    half = slots // 2
    sum_top = jnp.zeros((half, half), F32)
    sum_low = jnp.zeros((half, slots), F32)
    for pair in range(heads // 2):
        at = slice(pair * 2 * width, (pair + 1) * 2 * width)
        xd_pair = xd[:, at]
        top, whole = None, None
        for side in range(2):
            head = 2 * pair + side
            mine = pair_part_of(dy_b[:, at], side, width)
            decay = jnp.exp(jnp.minimum(spread(head, 0, half, half), 0.0))
            weights = (scores[:half, :half] * decay).astype(BF16)
            part = mm(weights, mine[:half], ((0,), (0,)))
            top = part if top is None else top + part
            sum_top = sum_top + mm(mine[:half], xd_pair[:half], ((1,), (1,))) * decay
            decay = jnp.exp(jnp.minimum(spread(head, half, half, slots), 0.0))
            weights = (scores[half:] * decay).astype(BF16)
            part = mm(weights, mine[half:], ((0,), (0,)))
            whole = part if whole is None else whole + part
            sum_low = sum_low + mm(mine[half:], xd_pair, ((1,), (1,))) * decay
        grad_xd_out[0, :half, at] = whole[:half] + top
        grad_xd_out[0, half:, at] = whole[half:]
    grad_scores[:half, :half] += sum_top
    grad_scores[half:] += sum_low
    growth = widen(jnp.exp(cumul), lanes)
    grad_c = mm((growth * dy).astype(BF16), entering[0].astype(BF16), ((1,), (1,)))
    grad_bc[0] += jnp.concatenate([jnp.zeros_like(grad_c), grad_c], axis=1)

    @pl.when(pl.program_id(1) == pl.num_programs(1) - 1)
    def _():
        causal = grad_scores[...] * triangle(slots)
        from_c = mm(causal, c_act[0], ((0,), (0,)), HIGHEST)
        grad_bc[0] += jnp.concatenate([from_c, mm(causal, b_act[0], precision=HIGHEST)], axis=1)


def scan_back_kernel(
    heads, u, pre_x, edge_x, taps_x, dtraw, params, steps, b_act, y, grad_y, inside, entering, coming,
    grad_pre, tail_rows, head_rows, taps_grad, grad_dt, params_grad, grad_b,
):
    slots, lanes = u.shape[1:]

    @pl.when(pl.program_id(1) == 0)
    def _():
        grad_b[...] = jnp.zeros_like(grad_b)

    uv = u[0]
    sig = jax.nn.sigmoid(uv)
    x = uv * sig
    par = params[0]
    decay_a = -jnp.exp(par[:, 1:2])
    step, cumul = steps[0, 0][:heads], steps[0, 0][heads:]
    last = cumul[:, slots - 1 : slots]
    step_wide = widen(step, lanes)
    tail_wide = widen(jnp.exp(last - cumul), lanes)
    lines = widen(jnp.concatenate([jnp.exp(last)] * 4 + [par[:, 2:3]] * 4, axis=1), lanes)
    skip = lines[4:5]
    xd = (step_wide * x).astype(BF16)
    xd_f = xd.astype(F32)
    dy = grad_y[0]
    coming_b = coming[0].astype(BF16)
    from_next = tail_wide * mm(b_act[0].astype(BF16), coming_b)
    grad_xd = inside[0] + from_next
    grad_b[0] += mm((tail_wide * xd_f).astype(BF16), coming_b, ((1,), (1,)))

    direct = head_sums(x * grad_xd, heads, 1)
    ys = y[0] - skip * x
    moved = head_sums(dy.astype(BF16).astype(F32) * ys - xd_f * grad_xd, heads)
    ends = lines[0:1] * jnp.sum(coming[0] * entering[0], axis=0, keepdims=True)
    ends = ends + jnp.sum(xd_f * from_next, axis=0, keepdims=True)
    skips = jnp.sum(dy * x, axis=0, keepdims=True)
    columns = head_sums(jnp.concatenate([ends, skips, jnp.zeros((6, lanes), F32)], axis=0), heads)
    later = exact(moved, triangle(slots, BF16)) + columns[:, 0:1]
    grad_step = (direct + decay_a * later) * jax.nn.sigmoid(dtraw[0, 0] + par[:, 0:1])
    grad_dt[0, 0] = grad_step
    params_grad[0, 0] = jnp.concatenate(
        [
            jnp.sum(grad_step, axis=1, keepdims=True),
            jnp.sum(step * later, axis=1, keepdims=True) * decay_a,
            columns[:, 1:2],
        ],
        axis=1,
    )
    du = (step_wide * grad_xd + skip * dy) * slope(uv, sig)
    back, rows8 = convolved_back(du, pre_x[0], edge_x[0], taps_x[...])
    grad_pre[0] = back.astype(BF16)
    tail_rows[0] = back[slots - EDGE :]
    head_rows[0] = du[:EDGE]
    taps_grad[0] = rows8


def conv_back_kernel(pre, edge, taps, grad_act, grad_pre, tail_rows, head_rows, taps_grad):
    slots = pre.shape[1]
    ext = jnp.concatenate([edge[0], pre[0]], axis=0)
    u = convolved(ext, taps[...], slots)
    du = grad_act[0] * slope(u, jax.nn.sigmoid(u))
    back, rows8 = convolved_back(du, pre[0], edge[0], taps[...])
    grad_pre[0] = back.astype(BF16)
    tail_rows[0] = back[slots - EDGE :]
    head_rows[0] = du[:EDGE]
    taps_grad[0] = rows8


def assemble_kernel(mine, theirs, side, result):
    first = side[0] == 0
    half = mine.shape[2]
    result[0, :, :half] = jnp.where(first, mine[0], theirs[0]).astype(BF16)
    result[0, :, half:] = jnp.where(first, theirs[0], mine[0]).astype(BF16)


def weight_kernel(parts, own_rows, far_rows, *refs):
    result, columns = refs[-2:]
    slots = own_rows.shape[0]

    @pl.when(pl.program_id(0) == 0)
    def _():
        for index in range(parts):
            columns[:, pl.ds(index * slots, slots)] = refs[index][...].T.astype(BF16)

    total = mm(columns[:, :slots], own_rows[...])
    for index in range(1, parts):
        total = total + mm(columns[:, index * slots : (index + 1) * slots], far_rows[index - 1])
    for tile in range(result.shape[0] * result.shape[1]):
        piece = total[:, tile * 128 : (tile + 1) * 128]
        if result.shape[0] == 1:
            result[0, tile] = piece
        else:
            result[tile, 0] = piece


def pair_kernel(place, rows, far_rows, own, far, keep_a, send_a, keep_b, send_b, columns):
    slots = rows.shape[0]
    step = pl.program_id(0)

    @pl.when(step == 0)
    def _():
        columns[:, :slots] = own[...].T.astype(BF16)
        columns[:, slots:] = far[...].T.astype(BF16)

    total = mm(columns[:, :slots], rows[...]) + mm(columns[:, slots:], far_rows[...])
    for tile in range(4):
        piece = total[:, tile * 128 : (tile + 1) * 128]
        away = place[0] ^ tile
        for first, keep, send, bit in ((True, keep_a, send_a, away % 2), (False, keep_b, send_b, away // 2)):
            at = away // 2 if first else away % 2
            mine = step < 2 if first else step >= 2

            @pl.when(mine & (bit == 0))
            def _():
                keep[at, 0] = piece

            @pl.when(mine & (bit == 1))
            def _():
                send[at, 0] = piece


def mend_kernel(place, value, tail, later, taps, mended, *pieces):
    seqs, slots, _ = value.shape
    row = lax.broadcasted_iota(jnp.int32, (EDGE, value.shape[2]), 0)
    for seq in range(seqs):
        end = tail[seq]
        for tap in range(CONV - 1):
            ahead = CONV - 1 - tap
            moved = pltpu.roll(later[seq], EDGE - ahead, 0)
            end = end + jnp.where(row >= EDGE - ahead, moved, 0.0) * taps[tap : tap + 1]
        mended[seq] = jnp.concatenate([value[seq, : slots - 16], value[seq, slots - 16 :]], axis=0)
        last = jnp.concatenate([value[seq, slots - 16 :][: 16 - EDGE].astype(F32), end], axis=0).astype(BF16)
        mended[seq, slots - 16 :] = last
    for index, piece in enumerate(pieces):

        @pl.when(pl.program_id(0) == index)
        def _():
            for seq in range(seqs):
                piece[seq * slots : (seq + 1) * slots] = mended[seq].astype(F32)


def finish_kernel(place, *refs):
    result = refs[-1]
    for index in range(4):

        @pl.when(pl.program_id(0) == index)
        def _():
            result[:, 0] = refs[index][...].T
            result[:, 1] = refs[4 + index][...].T


def swapped(value, axis, bit):
    count = lax.axis_size(axis)
    return lax.ppermute(value, axis, [(i, i ^ bit) for i in range(count)])


def shifted(value, axis, steps):
    count = lax.axis_size(axis)
    initial, last = (max(0, -steps), min(count, count - steps))
    return lax.ppermute(value, axis, [(source, source + steps) for source in range(initial, last)])


def head_sum(value):
    if lax.axis_size("head") == 2:
        return value + swapped(value, "head", 1)
    return lax.psum(value, "head")


def gathered_pass(decay, part, reverse):
    count = lax.axis_size("seq")
    place = lax.axis_index("seq")
    gathered = lax.all_gather(jnp.concatenate([part, decay], axis=1), "seq")
    rows = part.shape[1]
    state = jnp.zeros_like(part)
    for turn in range(count - 1):
        source = count - 1 - turn if reverse else turn
        ahead = source > place if reverse else source < place
        later = gathered[source, :, rows : rows + 1] * state + gathered[source, :, :rows]
        state = jnp.where(ahead, later, state)
    return state


def chosen(pieces, index):
    low = jnp.where(index % 2 == 0, pieces[0], pieces[1])
    high = jnp.where(index % 2 == 0, pieces[2], pieces[3])
    return jnp.where(index < 2, low, high)


def quarter(value, axis, index):
    size = value.shape[axis] // 4
    return lax.dynamic_slice_in_dim(value, index * size, size, axis)


def tied(*values):
    return lax.optimization_barrier(values)


def passed_on(decay, part, reverse, first, second):
    if lax.axis_size("seq") != 4:
        beside_first = first()
        return gathered_pass(decay, part, reverse), beside_first, second(beside_first)
    place = lax.axis_index("seq")
    rows = part.shape[1]
    both = jnp.concatenate([part, decay], axis=1)
    got = [quarter(both, 2, place)] + [swapped(quarter(both, 2, place ^ d), "seq", d) for d in (1, 2, 3)]
    got, beside_first = tied(got, first())
    order = (3, 2, 1, 0) if reverse else (0, 1, 2, 3)
    state = jnp.zeros_like(got[0][:, :rows])
    enters = [None] * 4
    for source in order:
        enters[source] = state
        if source != order[-1]:
            piece = chosen(got, place ^ source)
            state = piece[:, rows : rows + 1] * state + piece[:, :rows]
    back = [chosen(enters, place)] + [swapped(chosen(enters, place ^ d), "seq", d) for d in (1, 2, 3)]
    back, beside_second = tied(back, second(beside_first))
    entering = jnp.concatenate([chosen(back, place ^ index) for index in range(4)], axis=2)
    return entering, beside_first, beside_second


def halves(value, axis, which):
    size = value.shape[axis] // 2
    return lax.dynamic_slice_in_dim(value, which * size, size, axis)


def core_half(value):
    return halves(value.astype(F32), 1, lax.axis_index("head"))


def rows_of_seq_first(half):
    cut = half.shape[1] // 2
    a, b = half[:, :cut], half[:, cut:]
    return a, b, swapped(a, "seq", 1), swapped(b, "seq", 2)


def rows_of_seq_second(a, b, a1, b2):
    return a1, swapped(jnp.stack([a, a1]), "seq", 2), b2, swapped(jnp.stack([b, b2]), "seq", 1)


def rows_of_seq_third(a1, a23, b2, b13):
    high = jnp.stack([b13[0], b2, b13[1]])
    return jnp.concatenate([jnp.concatenate([a1[None], a23], axis=0), high], axis=2)


def assembled(mine):
    side = lax.axis_index("head").reshape(1)
    theirs = swapped(mine, "head", 1)
    count, slots, half = mine.shape
    block = pl.BlockSpec((1, slots, half), lambda i: (i, 0, 0))
    return call(
        assemble_kernel,
        [mine, theirs, side],
        [block, block, pl.BlockSpec(memory_space=pltpu.SMEM)],
        pl.BlockSpec((1, slots, 2 * half), lambda i: (i, 0, 0)),
        jax.ShapeDtypeStruct((count, slots, 2 * half), BF16),
        (count,),
        "assemble",
        count,
    )


def columns_of(value, axis, dim=1):
    place = lax.axis_index(axis)
    piece = lambda index: quarter(value, dim, index).astype(F32)
    return [piece(place)] + [swapped(piece(place ^ d), axis, d) for d in (1, 2, 3)]


def weight_part(own_rows, far_rows, columns, axis):
    slots, model = own_rows.shape
    size = columns[0].shape[1]
    parts = len(columns)
    whole = lambda a: pl.BlockSpec(a.shape, lambda i: (0,) * a.ndim)
    if axis == "seq":
        out_spec = pl.BlockSpec((1, 4, size, 128), lambda i: (i, 0, 0, 0))
    else:
        out_spec = pl.BlockSpec((4, 1, size, 128), lambda i: (0, i, 0, 0))
    return call(
        functools.partial(weight_kernel, parts),
        [own_rows, far_rows, *columns],
        [
            pl.BlockSpec((slots, model // 4), lambda i: (0, i)),
            pl.BlockSpec((parts - 1, slots, model // 4), lambda i: (0, 0, i)),
            *[whole(c) for c in columns],
        ],
        out_spec,
        jax.ShapeDtypeStruct((4, 4, size, 128), F32),
        (4,),
        "weight_part",
        1,
        scratch=[pltpu.VMEM((size, parts * slots), BF16)],
    )


def over_batch(part):
    return lax.psum_scatter(part, "batch", scatter_dimension=0, tiled=True)[0]


def sent_back(summed, axis):
    place = lax.axis_index(axis)
    take = lambda index: lax.dynamic_index_in_dim(summed, index, 0, False)
    return [take(place)] + [swapped(take(place ^ d), axis, d) for d in (1, 2, 3)]


def finished(z_pieces, x_pieces):
    size, block = z_pieces[0].shape
    whole = pl.BlockSpec((size, block), lambda i, p: (0, 0))
    return call(
        finish_kernel,
        [*z_pieces, *x_pieces],
        [whole] * 8,
        pl.BlockSpec((block, 2, size), lambda i, p: (0, 0, i ^ p[0])),
        jax.ShapeDtypeStruct((block, 2, 4 * size), F32),
        (4,),
        "finish",
        4,
        index=lax.axis_index("seq"),
    )


def mended_pieces(value, tail, later, taps):
    seqs, slots, inner = value.shape
    size = inner // 4
    at = lambda *shape: pl.BlockSpec(shape + (size,), lambda i, p: (0,) * len(shape) + (i ^ p[0],))
    mended, *pieces = call(
        mend_kernel,
        [value, tail, later, taps],
        [at(seqs, slots), at(seqs, EDGE), at(seqs, EDGE), at(CONV + 1)],
        [at(seqs, slots)] + [pl.BlockSpec((seqs * slots, size), lambda i, p: (0, 0))] * 4,
        [jax.ShapeDtypeStruct(value.shape, BF16)] + [jax.ShapeDtypeStruct((seqs * slots, size), F32)] * 4,
        (4,),
        "mend",
        4,
        index=lax.axis_index("seq"),
    )
    return mended, pieces


def pair_part(rows, far_rows, own, far):
    slots, model = rows.shape
    size = own.shape[1]
    whole = lambda v: pl.BlockSpec(v.shape, lambda i, p: (0,) * v.ndim)
    part = pl.BlockSpec((slots, model // 4), lambda i, p: (0, i))
    a_spec = pl.BlockSpec((2, 1, size, 128), lambda i, p: (0, jnp.minimum(i, 1), 0, 0))
    b_spec = pl.BlockSpec((2, 1, size, 128), lambda i, p: (0, jnp.maximum(i - 2, 0), 0, 0))
    return call(
        pair_kernel,
        [rows, far_rows, own, far],
        [part, part, whole(own), whole(far)],
        [a_spec, a_spec, b_spec, b_spec],
        [jax.ShapeDtypeStruct((2, 2, size, 128), F32)] * 4,
        (4,),
        "pair_part",
        1,
        scratch=[pltpu.VMEM((size, 2 * slots), BF16)],
        index=lax.axis_index("seq"),
    )


def small_step(value, axis, bit, index):
    pick = lambda which: lax.dynamic_index_in_dim(value, which, 0, False)
    return pick(index) + swapped(pick(1 - index), axis, bit)


def first_transfers(parts, sum_z):
    keep_a, send_a, keep_b, send_b = parts
    return keep_a + swapped(send_a, "seq", 1), keep_b + swapped(send_b, "seq", 2), sent_back(sum_z, "seq")


def second_transfers(a, b, small):
    small = small.reshape(-1, 2, 2, 2, 2, small.shape[1] // 16).transpose(4, 3, 1, 2, 0, 5)
    a = a[0] + swapped(a[1], "seq", 2)
    b = b[0] + swapped(b[1], "seq", 1)
    return a, b, small_step(small, "seq", 1, lax.axis_index("seq") % 2)


def out_weight(pieces):
    even, odd = pieces[0] + pieces[2], pieces[1] + pieces[3]
    parity = lax.axis_index("batch") % 2
    return jnp.concatenate([jnp.where(parity == 0, even, odd), jnp.where(parity == 0, odd, even)], axis=0)


def added_over(values, axis):
    for bit in (1, 2):
        values = values + swapped(values, axis, bit)
    return values


def per_device(
    hidden,
    norm_gain,
    gate_input_weight,
    w_bc,
    w_dt,
    conv_x,
    conv_bc,
    head_params,
    gate_gain,
    w_out,
    lengths,
    cotangent,
):
    seqs, slots, model = hidden.shape
    rows = seqs * slots
    inner = gate_input_weight.shape[2]
    heads_dev = w_dt.shape[1]
    width = inner // heads_dev
    state = w_bc.shape[1] // 2
    inner_all = inner * lax.axis_size("head")
    heads = LANES // width
    groups = inner // LANES
    side = lax.axis_index("head")
    paired = lax.axis_size("batch") == 4 and lax.axis_size("seq") == 4 and lax.axis_size("head") == 2

    positions = lax.axis_index("seq") * slots + jnp.arange(slots)
    mask = (positions[None, :] < lengths[:, None]).astype(F32).reshape(rows, 1)
    hidden_f = hidden.reshape(rows, model).astype(F32)
    inv_rms = lax.rsqrt(jnp.mean(hidden_f * hidden_f, axis=-1, keepdims=True) + EPSILON)
    normed = (hidden_f * inv_rms * norm_gain).astype(BF16)
    grad_mix = (cotangent.reshape(rows, model).astype(F32) * mask).astype(BF16)
    if paired:
        seq_first = rows_of_seq_first(core_half(normed))
        mix_far = swapped(core_half(grad_mix), "batch", 1)

    proj = mm(normed, jnp.concatenate([w_bc, w_dt], axis=1))
    pre_bc = proj[:, : 2 * state].reshape(seqs, slots, 2 * state)
    projected = jnp.einsum("tg,gjn->tjn", normed, gate_input_weight, preferred_element_type=F32)
    gate_z = projected[:, 0].reshape(seqs, slots, inner)
    pre_x = projected[:, 1].reshape(seqs, slots, inner)
    edges = jnp.concatenate([pre_x[:, slots - EDGE :], pre_bc[:, slots - EDGE :]], axis=2)
    edges = shifted(edges, "seq", 1)
    edge_x, edge_bc = edges[..., :inner], edges[..., inner:]
    dtraw = proj[:, 2 * state :].reshape(seqs, slots, groups, heads).transpose(0, 2, 3, 1)
    params = head_params.reshape(3, groups, heads).transpose(1, 2, 0)
    gain = gate_gain.reshape(1, inner)

    grid = (seqs, groups)
    S = jax.ShapeDtypeStruct
    wide = pl.BlockSpec((1, slots, LANES), lambda b, g: (b, 0, g))
    edge = pl.BlockSpec((1, EDGE, LANES), lambda b, g: (b, 0, g))
    states = pl.BlockSpec((1, state, LANES), lambda b, g: (b, 0, g))
    line = pl.BlockSpec((1, 1, LANES), lambda b, g: (b, 0, g))
    taps = pl.BlockSpec((CONV + 1, LANES), lambda b, g: (0, g))
    gain_spec = pl.BlockSpec((1, LANES), lambda b, g: (0, g))
    per_seq = lambda *shape: pl.BlockSpec((1,) + shape, lambda b, g: (b,) + (0,) * len(shape))
    fixed = lambda *shape: pl.BlockSpec(shape, lambda b, g: (0,) * len(shape))
    by_head = lambda k: pl.BlockSpec((1, 1, k, slots), lambda b, g: (b, g, 0, 0))
    par_spec = pl.BlockSpec((1, heads, 3), lambda b, g: (g, 0, 0))
    wide_s = S((seqs, slots, inner), F32)
    wide_b = S((seqs, slots, inner), BF16)
    state_s = S((seqs, state, inner), F32)
    bc_b = S((seqs, slots, state), F32)
    settings = pltpu.CompilerParams(vmem_limit_bytes=VMEM_LIMIT)

    local_state, total_decay, u, b_act, c_act, steps = call(
        functools.partial(state_kernel, heads),
        [pre_x, edge_x, conv_x, pre_bc, edge_bc, conv_bc, dtraw, params],
        [
            wide, edge, taps, per_seq(slots, 2 * state), per_seq(EDGE, 2 * state),
            fixed(CONV + 1, 2 * state), by_head(heads), par_spec,
        ],
        [states, edge, wide, per_seq(slots, state), per_seq(slots, state), by_head(2 * heads)],
        [
            state_s, S((seqs, EDGE, inner), F32), wide_s, bc_b, bc_b,
            S((seqs, groups, 2 * heads, slots), F32),
        ],
        grid,
        "scan_state",
        17,
        scratch=[pltpu.VMEM((state, slots), BF16)],
    )
    if paired:
        local_state, seq_first, grad_mix, steps = tied(local_state, seq_first, grad_mix, steps)

    def mix_back():
        return mm(grad_mix, w_out, ((1,), (1,))).reshape(seqs, slots, inner)

    def scan_inside(_):
        return call(
            functools.partial(inside_kernel, heads, width),
            [u, steps, params, b_act, c_act],
            [wide, by_head(2 * heads), par_spec, per_seq(slots, state), per_seq(slots, state)],
            wide,
            wide_s,
            grid,
            "scan_inside",
            18,
            scratch=[pltpu.VMEM((slots, slots), F32)],
        )

    entering, grad_out, local_out = passed_on(total_decay, local_state, False, mix_back, scan_inside)
    if paired:
        entering, mix_far, seq_first = tied(entering, mix_far, seq_first)
        seq_second = rows_of_seq_second(*seq_first)

    y, sums = call(
        functools.partial(gate_kernel, heads),
        [local_out, entering, c_act, steps, gate_z, grad_out, gain],
        [wide, states, per_seq(slots, state), by_head(2 * heads), wide, wide, gain_spec],
        [wide, per_seq(8, slots)],
        [wide_s, S((seqs, 8, slots), F32)],
        grid,
        "gate",
        15,
    )
    sums = head_sum(sums)

    gated, grad_y, grad_z, gain_grad, leaving = call(
        functools.partial(gate_back_kernel, heads, inner_all),
        [y, gate_z, grad_out, gain, sums, c_act, steps],
        [wide, wide, wide, gain_spec, per_seq(8, slots), per_seq(slots, state), by_head(2 * heads)],
        [wide, wide, wide, line, states],
        [wide_b, wide_s, wide_b, S((seqs, 1, inner), F32), state_s],
        grid,
        "gate_back",
        17,
        scratch=[pltpu.VMEM((state, slots), BF16)],
    )
    gated = gated.reshape(rows, inner)
    grad_z = grad_z.reshape(rows, inner)

    def scan_inside_back():
        inside, grad_bc = call(
            functools.partial(inside_back_kernel, heads, width),
            [u, steps, b_act, c_act, grad_y, entering],
            [wide, by_head(2 * heads), per_seq(slots, state), per_seq(slots, state), wide, states],
            [wide, per_seq(slots, 2 * state)],
            [wide_s, S((seqs, slots, 2 * state), F32)],
            grid,
            "scan_inside_back",
            26,
            scratch=[pltpu.VMEM((slots, slots), F32), pltpu.VMEM((slots, slots), F32)],
        )
        if not paired:
            return inside, grad_bc
        return inside, grad_bc, seq_second

    def rows_ready(beside):
        if not paired:
            return ()
        return assembled(rows_of_seq_third(*beside[2])), mm(gated, w_out)

    coming, beside, ready = passed_on(total_decay, leaving, True, scan_inside_back, rows_ready)
    inside, grad_bc = beside[:2]
    if paired:
        coming, grad_z_sent, gated_sent, ready = tied(coming, grad_z, gated, ready)
        normed_far, mixed = ready
        z_columns = columns_of(grad_z_sent, "seq")
        parity = lax.axis_index("batch") % 2
        gated_own = halves(gated, 1, parity).astype(F32)
        gated_far = swapped(halves(gated_sent, 1, 1 - parity).astype(F32), "batch", 1)
    else:
        mixed = mm(gated, w_out)
    grad_pre, tail_x, first_x, taps_grad_x, grad_dt, params_grad, grad_b = call(
        functools.partial(scan_back_kernel, heads),
        [u, pre_x, edge_x, conv_x, dtraw, params, steps, b_act, y, grad_y, inside, entering, coming],
        [
            wide, wide, edge, taps, by_head(heads), par_spec, by_head(2 * heads), per_seq(slots, state),
            wide, wide, wide, states, states,
        ],
        [
            wide, edge, edge, edge, by_head(heads),
            pl.BlockSpec((1, 1, heads, 3), lambda b, g: (b, g, 0, 0)), per_seq(slots, state),
        ],
        [
            wide_b, S((seqs, EDGE, inner), F32), S((seqs, EDGE, inner), F32), S((seqs, EDGE, inner), F32),
            S((seqs, groups, heads, slots), F32), S((seqs, groups, heads, 3), F32),
            S((seqs, slots, state), F32),
        ],
        grid,
        "scan_back",
        34,
    )
    if paired:
        later_x = shifted(first_x, "seq", -1)
        grad_pre, z_columns, gated_far = tied(grad_pre, z_columns, gated_far)
        part_z = weight_part(normed, normed_far, z_columns, "seq")
        later_x, part_z, tail_x = tied(later_x, part_z, tail_x)
        sum_z = over_batch(part_z)
        grad_pre, pieces = mended_pieces(grad_pre, tail_x, later_x, conv_x)
        pieces, grad_b = tied(pieces, grad_b)
        x_columns = pieces[:1] + [swapped(pieces[d], "seq", d) for d in (1, 2, 3)]
    grad_bc = grad_bc + jnp.pad(grad_b, ((0, 0), (0, 0), (0, state)))
    grad_bc = head_sum(grad_bc)
    if paired:
        mix_far = assembled(mix_far[None])[0]
        parts_out = pair_part(grad_mix, mix_far, gated_own, gated_far)
        x_columns, parts_out, grad_bc = tied(x_columns, parts_out, grad_bc)
        part_x = weight_part(normed, normed_far, x_columns, "seq")
        sum_x = over_batch(part_x)
        part_x, grad_bc = tied(part_x, grad_bc)

    one = lambda *shape: pl.BlockSpec((1,) + shape, lambda b: (b, 0, 0))
    rows8 = S((seqs, EDGE, 2 * state), F32)
    grad_pre_bc, tail_bc, first_bc, taps_grad_bc = call(
        conv_back_kernel,
        [pre_bc, edge_bc, conv_bc, grad_bc],
        [
            one(slots, 2 * state), one(EDGE, 2 * state),
            pl.BlockSpec((CONV + 1, 2 * state), lambda b: (0, 0)), one(slots, 2 * state),
        ],
        [one(slots, 2 * state), one(EDGE, 2 * state), one(EDGE, 2 * state), one(EDGE, 2 * state)],
        [S((seqs, slots, 2 * state), BF16), rows8, rows8, rows8],
        (seqs,),
        "conv_back",
        3,
    )

    def mended(value, tail, first, weights):
        later = shifted(first, "seq", -1)
        add = jnp.zeros_like(tail)
        for tap in range(CONV - 1):
            ahead = CONV - 1 - tap
            moved = jnp.pad(later[:, :ahead], ((0, 0), (EDGE - ahead, 0), (0, 0)))
            add = add + moved * weights[tap]
        return lax.dynamic_update_slice(value, (tail + add).astype(BF16), (0, slots - EDGE, 0))

    if not paired:
        grad_pre = mended(grad_pre, tail_x, first_x, conv_x)
    grad_pre = grad_pre.reshape(rows, inner)
    grad_pre_bc = mended(grad_pre_bc, tail_bc, first_bc, conv_bc).reshape(rows, 2 * state)
    grad_dtr = grad_dt.transpose(0, 3, 1, 2).reshape(rows, heads_dev).astype(BF16)

    if paired:
        a, b, z_pieces = first_transfers(parts_out, sum_z)
        a, b, z_pieces, grad_pre_bc, grad_dtr, grad_pre = tied(a, b, z_pieces, grad_pre_bc, grad_dtr, grad_pre)
        small = jnp.concatenate([halves(grad_pre_bc, 1, side), grad_dtr], axis=1)
        small = mm(small, normed, ((0,), (0,)))
    grad_zx = jnp.stack([grad_z, grad_pre], axis=1)
    portion = jnp.einsum("tjn,gjn->tg", grad_zx, gate_input_weight, preferred_element_type=F32)
    portion = portion + mm(grad_dtr, w_dt, ((1,), (1,)))
    if paired:
        a, b, small = second_transfers(a, b, small)
        a, b, small, portion, mixed = tied(a, b, small, portion, mixed)
        out_pieces = sent_back(jnp.concatenate([a, b], axis=0), "batch")
        small = small_step(small, "seq", 2, lax.axis_index("seq") // 2)
    mixed = head_sum(mixed)
    mixed_out = (mask * (hidden_f + mixed)).astype(BF16).reshape(seqs, slots, model)
    grad_normed = head_sum(portion) + mm(grad_pre_bc, w_bc, ((1,), (1,)))
    scaled_input = hidden_f * inv_rms
    grad_norm_gain = jnp.sum(grad_normed * scaled_input, axis=0)
    grad_scaled = grad_normed * norm_gain
    input_dot = jnp.mean(grad_scaled * scaled_input, axis=-1, keepdims=True)
    grad_hidden = grad_mix.astype(F32) + inv_rms * (grad_scaled - scaled_input * input_dot)
    grad_hidden = grad_hidden.reshape(seqs, slots, model)

    head_grad = params_grad.sum(axis=0).transpose(2, 0, 1).reshape(3, heads_dev)
    taps_sum = jnp.concatenate([taps_grad_x.sum(axis=0), taps_grad_bc.sum(axis=0)], axis=1)[: CONV + 1]
    pieces = [taps_sum, head_grad, gain_grad.sum(axis=0), grad_norm_gain]
    flat = jnp.concatenate([piece.reshape(-1) for piece in pieces])
    if paired:
        flat = added_over(flat, "seq")
        out_pieces, sum_x, flat, small, grad_hidden, mixed_out = tied(
            out_pieces, sum_x, flat, small, grad_hidden, mixed_out
        )
        batch_place = lax.axis_index("batch")
        x_pieces = sent_back(sum_x, "seq")
        small = small_step(small, "batch", 2, batch_place // 2)
        done_small = small_step(small, "batch", 1, batch_place % 2)
        flat = added_over(flat, "batch")
        grad_weight = finished(z_pieces, x_pieces)
        grad_w_out = out_weight(out_pieces)
        bc_mine = done_small[:state]
        bc_other = swapped(bc_mine, "head", 1)
        grad_w_bc = jnp.concatenate(
            [jnp.where(side == 0, bc_mine, bc_other), jnp.where(side == 0, bc_other, bc_mine)], axis=0
        ).T
        grad_w_dt = done_small[state:].T
    else:
        scatter = functools.partial(lax.psum_scatter, axis_name=("batch", "seq"), tiled=True)
        over_slots = ((0,), (0,))
        grad_weight = scatter(
            jnp.stack([mm(normed, grad_z, over_slots), mm(normed, grad_pre, over_slots)], axis=1),
            scatter_dimension=0,
        )
        grad_w_bc = scatter(mm(normed, grad_pre_bc, over_slots), scatter_dimension=0)
        grad_w_dt = scatter(mm(normed, grad_dtr, over_slots), scatter_dimension=0)
        grad_w_out = scatter(mm(gated, grad_mix, over_slots), scatter_dimension=1)
        flat = lax.psum(flat, ("batch", "seq"))

    parted, start = [], 0
    for piece in pieces:
        parted.append(flat[start : start + piece.size].reshape(piece.shape))
        start += piece.size
    grad_conv, grad_head, grad_gate_gain, grad_norm_gain = parted
    return (
        mixed_out,
        grad_hidden,
        grad_norm_gain,
        grad_weight,
        grad_w_bc,
        grad_w_dt,
        grad_conv[:, :inner],
        grad_conv[:, inner:],
        grad_head,
        grad_gate_gain.reshape(inner),
        grad_w_out,
    )


def solution(mesh):
    placed = (
        P("batch", "seq", None),
        P(),
        P(None, None, "head"),
        P(),
        P(None, "head"),
        P(None, "head"),
        P(),
        P(None, "head"),
        P("head"),
        P("head", None),
        P("batch"),
        P("batch", "seq", None),
    )
    return jax.shard_map(
        per_device,
        mesh=mesh,
        in_specs=placed,
        out_specs=(
            P("batch", "seq", None),
            P("batch", "seq", None),
            P(),
            P(("batch", "seq"), None, "head"),
            P(("batch", "seq"), None),
            P(("batch", "seq"), "head"),
            P(None, "head"),
            P(),
            P(None, "head"),
            P("head"),
            P("head", ("batch", "seq")),
        ),
        check_vma=False,
    )
```

```python
import functools

import jax
import jax.numpy as jnp
from jax import lax
from jax.experimental import pallas as pl
from jax.experimental.pallas import tpu as pltpu
from jax.sharding import PartitionSpec as P

CONV = 4
EDGE = 8
LANES = 512
EPSILON = 1e-05
HIGHEST = lax.Precision.HIGHEST
F32 = jnp.float32
BF16 = jnp.bfloat16
VMEM_LIMIT = 48 * 1024 * 1024
COST = 0.25


def mm(a, b, dims=((1,), (0,)), precision=None):
    return lax.dot_general(a, b, (dims, ((), ())), precision=precision, preferred_element_type=F32)


def split(value, count):
    parts, rest = [], value
    for _ in range(count):
        part = rest.astype(BF16).astype(F32)
        parts.append(part)
        rest = rest - part
    return jnp.concatenate(parts, axis=0)


def of_head(rows, columns, heads):
    head = lax.broadcasted_iota(jnp.int32, (rows, columns), 0) % heads
    lane = lax.broadcasted_iota(jnp.int32, (rows, columns), 1) // (columns // heads)
    return (head == lane).astype(F32).astype(BF16)


def widen(rows, lanes):
    heads = rows.shape[0]
    return mm(split(rows, 2).astype(BF16), of_head(2 * heads, lanes, heads), ((0,), (0,)))


def head_sums(value, heads, parts=2):
    pick = of_head(heads, value.shape[1], heads)
    high = value.astype(BF16)
    total = mm(pick, high, ((1,), (1,)))
    if parts == 2:
        total = total + mm(pick, (value - high.astype(F32)).astype(BF16), ((1,), (1,)))
    return total


def row_sums(value):
    ones = jnp.ones((8, value.shape[1]), BF16)
    high = value.astype(BF16)
    return mm(ones, high, ((1,), (1,))) + mm(ones, (value - high.astype(F32)).astype(BF16), ((1,), (1,)))


def exact(rows, matrix, dims=((1,), (0,))):
    heads = rows.shape[0]
    result = mm(split(rows, 3).astype(BF16), matrix, dims)
    return result[:heads] + result[heads : 2 * heads] + result[2 * heads :]


def spreads(cumul):
    heads, slots = cumul.shape
    parts = split(cumul, 3)
    row = lax.broadcasted_iota(jnp.int32, parts.shape, 0) % heads

    def spread(head, start, size, end):
        mask = (row == head).astype(F32)
        left = jnp.concatenate([parts, mask], axis=0).astype(BF16)
        right = jnp.concatenate([mask, -parts], axis=0).astype(BF16)
        return mm(left[:, start : start + size], right[:, :end], ((0,), (0,)))

    return spread


def triangle(slots, dtype=F32):
    row = lax.broadcasted_iota(jnp.int32, (slots, slots), 0)
    column = lax.broadcasted_iota(jnp.int32, (slots, slots), 1)
    return (row >= column).astype(F32).astype(dtype)


def softplus(value):
    return jnp.maximum(value, 0.0) + jnp.log1p(jnp.exp(-jnp.abs(value)))


def slope(value, sig):
    return sig * (1.0 + value * (1.0 - sig))


def convolved(extended, taps, slots):
    total = taps[CONV : CONV + 1] + extended[EDGE : EDGE + slots] * taps[CONV - 1 : CONV]
    for tap in range(CONV - 1):
        start = EDGE - (CONV - 1) + tap
        total = total + extended[start : start + slots] * taps[tap : tap + 1]
    return total


def convolved_back(grad, pre, before, taps):
    slots, lanes = grad.shape
    padded = jnp.concatenate([grad, jnp.zeros((EDGE, lanes), F32)], axis=0)
    row = lax.broadcasted_iota(jnp.int32, (EDGE, lanes), 0)
    back = grad * taps[CONV - 1 : CONV]
    rows = []
    for tap in range(CONV - 1):
        ahead = CONV - 1 - tap
        moved = padded[ahead : ahead + slots]
        back = back + moved * taps[tap : tap + 1]
        first = jnp.where(row >= EDGE - ahead, pltpu.roll(grad[:EDGE], EDGE - ahead, 0), 0.0)
        total = jnp.sum(moved * pre, axis=0, keepdims=True)
        rows.append(total + jnp.sum(first * before, axis=0, keepdims=True))
    rows.append(jnp.sum(grad * pre, axis=0, keepdims=True))
    rows.append(jnp.sum(grad, axis=0, keepdims=True))
    rows.append(jnp.zeros((8 - len(rows), lanes), F32))
    return back, jnp.concatenate(rows, axis=0)


def pair_part_of(value, side, width):
    lane = lax.broadcasted_iota(jnp.int32, value.shape, 1) // width
    return jnp.where(lane == side, value, jnp.zeros_like(value))


def call(kernel, inputs, in_specs, out_specs, out_shape, grid, name, micros, scratch=(), index=None):
    scalars = () if index is None else (index.reshape(-1),)
    return pl.pallas_call(
        kernel,
        grid_spec=pltpu.PrefetchScalarGridSpec(
            num_scalar_prefetch=len(scalars),
            grid=grid,
            in_specs=list(in_specs),
            out_specs=out_specs,
            scratch_shapes=list(scratch),
        ),
        out_shape=out_shape,
        compiler_params=pltpu.CompilerParams(vmem_limit_bytes=VMEM_LIMIT),
        cost_estimate=pl.CostEstimate(
            flops=int(micros * COST * 1.1e9), bytes_accessed=int(micros * COST * 2e6), transcendentals=0
        ),
        name=name,
    )(*scalars, *inputs)


def state_kernel(
    heads, pre_x, edge_x, taps_x, pre_bc, edge_bc, taps_bc, dtraw, params,
    state_out, u_out, b_out, c_out, steps_out, b_turned,
):
    slots, lanes = pre_x.shape[1:]
    state = b_out.shape[2]

    @pl.when(pl.program_id(1) == 0)
    def _():
        ext = jnp.concatenate([edge_bc[0], pre_bc[0]], axis=0)
        u = convolved(ext, taps_bc[...], slots)
        act = u * jax.nn.sigmoid(u)
        b_out[0] = act[:, :state]
        c_out[0] = act[:, state:]
        b_turned[...] = act[:, :state].T.astype(BF16)

    ext = jnp.concatenate([edge_x[0], pre_x[0]], axis=0)
    u = convolved(ext, taps_x[...], slots)
    u_out[0] = u
    x = u * jax.nn.sigmoid(u)
    par = params[0]
    step = softplus(dtraw[0, 0] + par[:, 0:1])
    rate = step * -jnp.exp(par[:, 1:2])
    cumul = exact(rate, triangle(slots, BF16), ((1,), (1,)))
    steps_out[0, 0] = jnp.concatenate([step, cumul], axis=0)
    last = cumul[:, slots - 1 : slots]
    state_out[0, state:] = widen(jnp.broadcast_to(jnp.exp(last), (heads, 8)), lanes)
    xd = (widen(step, lanes) * x).astype(BF16)
    tail = (widen(jnp.exp(last - cumul), lanes) * xd.astype(F32)).astype(BF16)
    state_out[0, :state] = mm(b_turned[...], tail)


def inside_kernel(heads, width, u, steps, params, b_act, c_act, local_out, scores):
    slots, lanes = u.shape[1:]

    @pl.when(pl.program_id(1) == 0)
    def _():
        scores[...] = mm(c_act[0], b_act[0], ((1,), (1,)), HIGHEST) * triangle(slots)

    uv = u[0]
    x = uv * jax.nn.sigmoid(uv)
    step, cumul = steps[0, 0][:heads], steps[0, 0][heads:]
    spread = spreads(cumul)
    xd = (widen(step, lanes) * x).astype(BF16)
    skip = widen(jnp.broadcast_to(params[0][:, 2:3], (heads, 8)), lanes)[0:1] * x
    half = slots // 2
    for pair in range(heads // 2):
        at = slice(pair * 2 * width, (pair + 1) * 2 * width)
        top, low = skip[:half, at], skip[half:, at]
        for side in range(2):
            head = 2 * pair + side
            mine = pair_part_of(xd[:, at], side, width)
            decay = jnp.exp(jnp.minimum(spread(head, 0, half, half), 0.0))
            top = top + mm((scores[:half, :half] * decay).astype(BF16), mine[:half])
            decay = jnp.exp(jnp.minimum(spread(head, half, half, slots), 0.0))
            low = low + mm((scores[half:] * decay).astype(BF16), mine)
        local_out[0, :half, at] = top
        local_out[0, half:, at] = low


def gate_kernel(heads, local_out, entering, c_act, steps, z, grad_out, gain, y_out, sums):
    lanes = z.shape[-1]
    growth = widen(jnp.exp(steps[0, 0][heads:]), lanes)
    y = local_out[0] + growth * mm(c_act[0].astype(BF16), entering[0].astype(BF16))
    y_out[0] = y
    zv = z[0]
    g = y * (zv * jax.nn.sigmoid(zv))
    squares = row_sums(g * g)
    dots = row_sums(grad_out[0] * gain[...] * g)
    row = lax.broadcasted_iota(jnp.int32, squares.shape, 0)
    both = jnp.where(row == 0, squares, jnp.where(row == 1, dots, 0.0))

    @pl.when(pl.program_id(1) == 0)
    def _():
        sums[0] = both

    @pl.when(pl.program_id(1) > 0)
    def _():
        sums[0] += both


def gate_back_kernel(
    heads, inner_all, y, z, grad_out, gain, sums, c_act, steps, decay,
    gated_out, grad_y, grad_z, gain_grad, leaving, c_turned,
):
    lanes = z.shape[-1]

    @pl.when(pl.program_id(1) == 0)
    def _():
        c_turned[...] = c_act[0].T.astype(BF16)

    inv_row = lax.rsqrt(sums[0][0:1] / inner_all + EPSILON)
    mean_row = inv_row * sums[0][1:2] / inner_all
    rows = jnp.concatenate([split(inv_row, 2), split(mean_row, 2), jnp.zeros_like(sums[0][:4])], axis=0)
    row = lax.broadcasted_iota(jnp.int32, (8, lanes), 0)
    rows = rows.astype(BF16)
    inv = mm(rows, (row < 2).astype(F32).astype(BF16), ((0,), (0,)))
    mean = mm(rows, ((row >= 2) & (row < 4)).astype(F32).astype(BF16), ((0,), (0,)))
    zv, yv = z[0], y[0]
    sig = jax.nn.sigmoid(zv)
    silu = zv * sig
    normed = yv * silu * inv
    gated_out[0] = (normed * gain[...]).astype(BF16)
    gain_grad[0] = jnp.sum(grad_out[0] * normed, axis=0, keepdims=True)
    dg = inv * (grad_out[0] * gain[...] - normed * mean)
    dy = dg * silu
    grad_y[0] = dy
    grad_z[0] = (dg * yv * slope(zv, sig)).astype(BF16)
    growth = widen(jnp.exp(steps[0, 0][heads:]), lanes)
    state = c_turned.shape[0]
    leaving[0, :state] = mm(c_turned[...], (growth * dy).astype(BF16))
    leaving[0, state:] = decay[0]


def inside_back_kernel(
    heads, width, u, steps, b_act, c_act, grad_y, entering,
    grad_xd_out, grad_bc, grad_scores, scores,
):
    slots, lanes = u.shape[1:]

    @pl.when(pl.program_id(1) == 0)
    def _():
        scores[...] = mm(c_act[0], b_act[0], ((1,), (1,)), HIGHEST) * triangle(slots)
        grad_scores[...] = jnp.zeros_like(grad_scores)
        grad_bc[...] = jnp.zeros_like(grad_bc)

    uv = u[0]
    step, cumul = steps[0, 0][:heads], steps[0, 0][heads:]
    spread = spreads(cumul)
    xd = (widen(step, lanes) * (uv * jax.nn.sigmoid(uv))).astype(BF16)
    dy = grad_y[0]
    dy_b = dy.astype(BF16)
    half = slots // 2
    sum_top = jnp.zeros((half, half), F32)
    sum_low = jnp.zeros((half, slots), F32)
    for pair in range(heads // 2):
        at = slice(pair * 2 * width, (pair + 1) * 2 * width)
        xd_pair = xd[:, at]
        top, whole = None, None
        for side in range(2):
            head = 2 * pair + side
            mine = pair_part_of(dy_b[:, at], side, width)
            decay = jnp.exp(jnp.minimum(spread(head, 0, half, half), 0.0))
            weights = (scores[:half, :half] * decay).astype(BF16)
            part = mm(weights, mine[:half], ((0,), (0,)))
            top = part if top is None else top + part
            sum_top = sum_top + mm(mine[:half], xd_pair[:half], ((1,), (1,))) * decay
            decay = jnp.exp(jnp.minimum(spread(head, half, half, slots), 0.0))
            weights = (scores[half:] * decay).astype(BF16)
            part = mm(weights, mine[half:], ((0,), (0,)))
            whole = part if whole is None else whole + part
            sum_low = sum_low + mm(mine[half:], xd_pair, ((1,), (1,))) * decay
        grad_xd_out[0, :half, at] = whole[:half] + top
        grad_xd_out[0, half:, at] = whole[half:]
    grad_scores[:half, :half] += sum_top
    grad_scores[half:] += sum_low
    growth = widen(jnp.exp(cumul), lanes)
    grad_c = mm((growth * dy).astype(BF16), entering[0].astype(BF16), ((1,), (1,)))
    grad_bc[0] += jnp.concatenate([jnp.zeros_like(grad_c), grad_c], axis=1)

    @pl.when(pl.program_id(1) == pl.num_programs(1) - 1)
    def _():
        causal = grad_scores[...] * triangle(slots)
        from_c = mm(causal, c_act[0], ((0,), (0,)), HIGHEST)
        grad_bc[0] += jnp.concatenate([from_c, mm(causal, b_act[0], precision=HIGHEST)], axis=1)


def scan_back_kernel(
    heads, u, pre_x, edge_x, taps_x, dtraw, params, steps, b_act, y, grad_y, inside, entering, coming,
    grad_pre, tail_rows, head_rows, taps_grad, grad_dt, params_grad, grad_b,
):
    slots, lanes = u.shape[1:]

    @pl.when(pl.program_id(1) == 0)
    def _():
        grad_b[...] = jnp.zeros_like(grad_b)

    uv = u[0]
    sig = jax.nn.sigmoid(uv)
    x = uv * sig
    par = params[0]
    decay_a = -jnp.exp(par[:, 1:2])
    step, cumul = steps[0, 0][:heads], steps[0, 0][heads:]
    last = cumul[:, slots - 1 : slots]
    step_wide = widen(step, lanes)
    tail_wide = widen(jnp.exp(last - cumul), lanes)
    lines = widen(jnp.concatenate([jnp.exp(last)] * 4 + [par[:, 2:3]] * 4, axis=1), lanes)
    skip = lines[4:5]
    xd = (step_wide * x).astype(BF16)
    xd_f = xd.astype(F32)
    dy = grad_y[0]
    coming_b = coming[0].astype(BF16)
    from_next = tail_wide * mm(b_act[0].astype(BF16), coming_b)
    grad_xd = inside[0] + from_next
    grad_b[0] += mm((tail_wide * xd_f).astype(BF16), coming_b, ((1,), (1,)))

    direct = head_sums(x * grad_xd, heads, 1)
    ys = y[0] - skip * x
    moved = head_sums(dy.astype(BF16).astype(F32) * ys - xd_f * grad_xd, heads)
    ends = lines[0:1] * jnp.sum(coming[0] * entering[0], axis=0, keepdims=True)
    ends = ends + jnp.sum(xd_f * from_next, axis=0, keepdims=True)
    skips = jnp.sum(dy * x, axis=0, keepdims=True)
    columns = head_sums(jnp.concatenate([ends, skips, jnp.zeros((6, lanes), F32)], axis=0), heads)
    later = exact(moved, triangle(slots, BF16)) + columns[:, 0:1]
    grad_step = (direct + decay_a * later) * jax.nn.sigmoid(dtraw[0, 0] + par[:, 0:1])
    grad_dt[0, 0] = grad_step
    params_grad[0, 0] = jnp.concatenate(
        [
            jnp.sum(grad_step, axis=1, keepdims=True),
            jnp.sum(step * later, axis=1, keepdims=True) * decay_a,
            columns[:, 1:2],
        ],
        axis=1,
    )
    du = (step_wide * grad_xd + skip * dy) * slope(uv, sig)
    back, rows8 = convolved_back(du, pre_x[0], edge_x[0], taps_x[...])
    grad_pre[0] = back.astype(BF16)
    tail_rows[0] = back[slots - EDGE :]
    head_rows[0] = du[:EDGE]
    taps_grad[0] = rows8


def conv_back_kernel(pre, edge, taps, grad_act, grad_pre, tail_rows, head_rows, taps_grad):
    slots = pre.shape[1]
    ext = jnp.concatenate([edge[0], pre[0]], axis=0)
    u = convolved(ext, taps[...], slots)
    du = grad_act[0] * slope(u, jax.nn.sigmoid(u))
    back, rows8 = convolved_back(du, pre[0], edge[0], taps[...])
    grad_pre[0] = back.astype(BF16)
    tail_rows[0] = back[slots - EDGE :]
    head_rows[0] = du[:EDGE]
    taps_grad[0] = rows8


def assemble_kernel(mine, theirs, side, result):
    first = side[0] == 0
    half = mine.shape[2]
    result[0, :, :half] = jnp.where(first, mine[0], theirs[0]).astype(BF16)
    result[0, :, half:] = jnp.where(first, theirs[0], mine[0]).astype(BF16)


def weight_kernel(parts, own_rows, far_rows, *refs):
    result, columns = refs[-2:]
    slots = own_rows.shape[0]

    @pl.when(pl.program_id(0) == 0)
    def _():
        for index in range(parts):
            columns[:, pl.ds(index * slots, slots)] = refs[index][...].T.astype(BF16)

    total = mm(columns[:, :slots], own_rows[...])
    for index in range(1, parts):
        total = total + mm(columns[:, index * slots : (index + 1) * slots], far_rows[index - 1])
    for tile in range(result.shape[0] * result.shape[1]):
        piece = total[:, tile * 128 : (tile + 1) * 128]
        if result.shape[0] == 1:
            result[0, tile] = piece
        else:
            result[tile, 0] = piece


def pair_kernel(place, rows, far_rows, own, far, keep_a, send_a, keep_b, send_b, columns):
    slots = rows.shape[0]
    step = pl.program_id(0)

    @pl.when(step == 0)
    def _():
        columns[:, :slots] = own[...].T.astype(BF16)
        columns[:, slots:] = far[...].T.astype(BF16)

    total = mm(columns[:, :slots], rows[...]) + mm(columns[:, slots:], far_rows[...])
    for tile in range(4):
        piece = total[:, tile * 128 : (tile + 1) * 128]
        away = place[0] ^ tile
        for first, keep, send, bit in ((True, keep_a, send_a, away % 2), (False, keep_b, send_b, away // 2)):
            at = away // 2 if first else away % 2
            mine = step < 2 if first else step >= 2

            @pl.when(mine & (bit == 0))
            def _():
                keep[at, 0] = piece

            @pl.when(mine & (bit == 1))
            def _():
                send[at, 0] = piece


def mend_kernel(place, value, tail, later, taps, mended, *pieces):
    seqs, slots, _ = value.shape
    row = lax.broadcasted_iota(jnp.int32, (EDGE, value.shape[2]), 0)
    for seq in range(seqs):
        end = tail[seq]
        for tap in range(CONV - 1):
            ahead = CONV - 1 - tap
            moved = pltpu.roll(later[seq], EDGE - ahead, 0)
            end = end + jnp.where(row >= EDGE - ahead, moved, 0.0) * taps[tap : tap + 1]
        mended[seq] = jnp.concatenate([value[seq, : slots - 16], value[seq, slots - 16 :]], axis=0)
        last = jnp.concatenate([value[seq, slots - 16 :][: 16 - EDGE].astype(F32), end], axis=0).astype(BF16)
        mended[seq, slots - 16 :] = last
    for index, piece in enumerate(pieces):

        @pl.when(pl.program_id(0) == index)
        def _():
            for seq in range(seqs):
                piece[seq * slots : (seq + 1) * slots] = mended[seq].astype(F32)


def finish_kernel(place, *refs):
    result = refs[-1]
    for index in range(4):

        @pl.when(pl.program_id(0) == index)
        def _():
            result[:, 0] = refs[index][...].T
            result[:, 1] = refs[4 + index][...].T


def swapped(value, axis, bit):
    count = lax.axis_size(axis)
    return lax.ppermute(value, axis, [(i, i ^ bit) for i in range(count)])


def shifted(value, axis, steps):
    count = lax.axis_size(axis)
    initial, last = (max(0, -steps), min(count, count - steps))
    return lax.ppermute(value, axis, [(source, source + steps) for source in range(initial, last)])


def head_sum(value):
    if lax.axis_size("head") == 2:
        return value + swapped(value, "head", 1)
    return lax.psum(value, "head")


def gathered_pass(both, rows, reverse):
    count = lax.axis_size("seq")
    place = lax.axis_index("seq")
    gathered = lax.all_gather(both, "seq")
    state = jnp.zeros_like(both[:, :rows])
    for turn in range(count - 1):
        source = count - 1 - turn if reverse else turn
        ahead = source > place if reverse else source < place
        later = gathered[source, :, rows : rows + 1] * state + gathered[source, :, :rows]
        state = jnp.where(ahead, later, state)
    return state


def chosen(pieces, index):
    low = jnp.where(index % 2 == 0, pieces[0], pieces[1])
    high = jnp.where(index % 2 == 0, pieces[2], pieces[3])
    return jnp.where(index < 2, low, high)


def quarter(value, axis, index):
    size = value.shape[axis] // 4
    return lax.dynamic_slice_in_dim(value, index * size, size, axis)


def tied(*values):
    return lax.optimization_barrier(values)


def passed_on(both, rows, reverse, first, second):
    if lax.axis_size("seq") != 4:
        beside_first = first()
        return gathered_pass(both, rows, reverse), beside_first, second(beside_first)
    place = lax.axis_index("seq")
    got = [quarter(both, 2, place)] + [swapped(quarter(both, 2, place ^ d), "seq", d) for d in (1, 2, 3)]
    got, beside_first = tied(got, first())
    order = (3, 2, 1, 0) if reverse else (0, 1, 2, 3)
    state = jnp.zeros_like(got[0][:, :rows])
    enters = [None] * 4
    for source in order:
        enters[source] = state
        if source != order[-1]:
            piece = chosen(got, place ^ source)
            state = piece[:, rows : rows + 1] * state + piece[:, :rows]
    back = [chosen(enters, place)] + [swapped(chosen(enters, place ^ d), "seq", d) for d in (1, 2, 3)]
    back, beside_second = tied(back, second(beside_first))
    entering = jnp.concatenate([chosen(back, place ^ index) for index in range(4)], axis=2)
    return entering, beside_first, beside_second


def halves(value, axis, which):
    size = value.shape[axis] // 2
    return lax.dynamic_slice_in_dim(value, which * size, size, axis)


def core_half(value):
    return halves(value.astype(F32), 1, lax.axis_index("head"))


def rows_of_seq_first(half):
    cut = half.shape[1] // 2
    a, b = half[:, :cut], half[:, cut:]
    return a, b, swapped(a, "seq", 1), swapped(b, "seq", 2)


def rows_of_seq_second(a, b, a1, b2):
    return a1, swapped(jnp.stack([a, a1]), "seq", 2), b2, swapped(jnp.stack([b, b2]), "seq", 1)


def rows_of_seq_third(a1, a23, b2, b13):
    high = jnp.stack([b13[0], b2, b13[1]])
    return jnp.concatenate([jnp.concatenate([a1[None], a23], axis=0), high], axis=2)


def assembled(mine):
    side = lax.axis_index("head").reshape(1)
    theirs = swapped(mine, "head", 1)
    count, slots, half = mine.shape
    block = pl.BlockSpec((1, slots, half), lambda i: (i, 0, 0))
    return call(
        assemble_kernel,
        [mine, theirs, side],
        [block, block, pl.BlockSpec(memory_space=pltpu.SMEM)],
        pl.BlockSpec((1, slots, 2 * half), lambda i: (i, 0, 0)),
        jax.ShapeDtypeStruct((count, slots, 2 * half), BF16),
        (count,),
        "assemble",
        count,
    )


def columns_of(value, axis, dim=1):
    place = lax.axis_index(axis)
    piece = lambda index: quarter(value, dim, index).astype(F32)
    return [piece(place)] + [swapped(piece(place ^ d), axis, d) for d in (1, 2, 3)]


def weight_part(own_rows, far_rows, columns, axis):
    slots, model = own_rows.shape
    size = columns[0].shape[1]
    parts = len(columns)
    whole = lambda a: pl.BlockSpec(a.shape, lambda i: (0,) * a.ndim)
    if axis == "seq":
        out_spec = pl.BlockSpec((1, 4, size, 128), lambda i: (i, 0, 0, 0))
    else:
        out_spec = pl.BlockSpec((4, 1, size, 128), lambda i: (0, i, 0, 0))
    return call(
        functools.partial(weight_kernel, parts),
        [own_rows, far_rows, *columns],
        [
            pl.BlockSpec((slots, model // 4), lambda i: (0, i)),
            pl.BlockSpec((parts - 1, slots, model // 4), lambda i: (0, 0, i)),
            *[whole(c) for c in columns],
        ],
        out_spec,
        jax.ShapeDtypeStruct((4, 4, size, 128), F32),
        (4,),
        "weight_part",
        1,
        scratch=[pltpu.VMEM((size, parts * slots), BF16)],
    )


def over_batch(part):
    return lax.psum_scatter(part, "batch", scatter_dimension=0, tiled=True)[0]


def sent_back(summed, axis):
    place = lax.axis_index(axis)
    take = lambda index: lax.dynamic_index_in_dim(summed, index, 0, False)
    return [take(place)] + [swapped(take(place ^ d), axis, d) for d in (1, 2, 3)]


def finished(z_pieces, x_pieces):
    size, block = z_pieces[0].shape
    whole = pl.BlockSpec((size, block), lambda i, p: (0, 0))
    return call(
        finish_kernel,
        [*z_pieces, *x_pieces],
        [whole] * 8,
        pl.BlockSpec((block, 2, size), lambda i, p: (0, 0, i ^ p[0])),
        jax.ShapeDtypeStruct((block, 2, 4 * size), F32),
        (4,),
        "finish",
        4,
        index=lax.axis_index("seq"),
    )


def mended_pieces(value, tail, later, taps):
    seqs, slots, inner = value.shape
    size = inner // 4
    at = lambda *shape: pl.BlockSpec(shape + (size,), lambda i, p: (0,) * len(shape) + (i ^ p[0],))
    mended, *pieces = call(
        mend_kernel,
        [value, tail, later, taps],
        [at(seqs, slots), at(seqs, EDGE), at(seqs, EDGE), at(CONV + 1)],
        [at(seqs, slots)] + [pl.BlockSpec((seqs * slots, size), lambda i, p: (0, 0))] * 4,
        [jax.ShapeDtypeStruct(value.shape, BF16)] + [jax.ShapeDtypeStruct((seqs * slots, size), F32)] * 4,
        (4,),
        "mend",
        4,
        index=lax.axis_index("seq"),
    )
    return mended, pieces


def pair_part(rows, far_rows, own, far):
    slots, model = rows.shape
    size = own.shape[1]
    whole = lambda v: pl.BlockSpec(v.shape, lambda i, p: (0,) * v.ndim)
    part = pl.BlockSpec((slots, model // 4), lambda i, p: (0, i))
    a_spec = pl.BlockSpec((2, 1, size, 128), lambda i, p: (0, jnp.minimum(i, 1), 0, 0))
    b_spec = pl.BlockSpec((2, 1, size, 128), lambda i, p: (0, jnp.maximum(i - 2, 0), 0, 0))
    return call(
        pair_kernel,
        [rows, far_rows, own, far],
        [part, part, whole(own), whole(far)],
        [a_spec, a_spec, b_spec, b_spec],
        [jax.ShapeDtypeStruct((2, 2, size, 128), F32)] * 4,
        (4,),
        "pair_part",
        1,
        scratch=[pltpu.VMEM((size, 2 * slots), BF16)],
        index=lax.axis_index("seq"),
    )


def small_step(value, axis, bit, index):
    pick = lambda which: lax.dynamic_index_in_dim(value, which, 0, False)
    return pick(index) + swapped(pick(1 - index), axis, bit)


def first_transfers(parts, sum_z):
    keep_a, send_a, keep_b, send_b = parts
    return keep_a + swapped(send_a, "seq", 1), keep_b + swapped(send_b, "seq", 2), sent_back(sum_z, "seq")


def second_transfers(a, b, small):
    small = small.reshape(-1, 2, 2, 2, 2, small.shape[1] // 16).transpose(4, 3, 1, 2, 0, 5)
    a = a[0] + swapped(a[1], "seq", 2)
    b = b[0] + swapped(b[1], "seq", 1)
    small = small_step(small, "seq", 1, lax.axis_index("seq") % 2)
    small = small_step(small, "seq", 2, lax.axis_index("seq") // 2)
    small = small.reshape((4,) + small.shape[2:])
    return jnp.concatenate([jnp.concatenate([a, b], axis=0), small], axis=1)


def out_weight(pieces, small):
    even, odd = pieces[0] + pieces[2], pieces[1] + pieces[3]
    size = even.shape[0] - small
    parity = lax.axis_index("batch") % 2
    low = jnp.where(parity == 0, even[:size], odd[:size])
    high = jnp.where(parity == 0, odd[:size], even[:size])
    return jnp.concatenate([low, high], axis=0), even[size:] + odd[size:]


def added_over(values, axis):
    far = [swapped(values, axis, d) for d in (1, 2, 3)]
    return (values + far[0]) + (far[1] + far[2])


def per_device(
    hidden,
    norm_gain,
    gate_input_weight,
    w_bc,
    w_dt,
    conv_x,
    conv_bc,
    head_params,
    gate_gain,
    w_out,
    lengths,
    cotangent,
):
    seqs, slots, model = hidden.shape
    rows = seqs * slots
    inner = gate_input_weight.shape[2]
    heads_dev = w_dt.shape[1]
    width = inner // heads_dev
    state = w_bc.shape[1] // 2
    inner_all = inner * lax.axis_size("head")
    heads = LANES // width
    groups = inner // LANES
    side = lax.axis_index("head")
    paired = lax.axis_size("batch") == 4 and lax.axis_size("seq") == 4 and lax.axis_size("head") == 2

    positions = lax.axis_index("seq") * slots + jnp.arange(slots)
    mask = (positions[None, :] < lengths[:, None]).astype(F32).reshape(rows, 1)
    hidden_f = hidden.reshape(rows, model).astype(F32)
    inv_rms = lax.rsqrt(jnp.mean(hidden_f * hidden_f, axis=-1, keepdims=True) + EPSILON)
    normed = (hidden_f * inv_rms * norm_gain).astype(BF16)
    grad_mix = (cotangent.reshape(rows, model).astype(F32) * mask).astype(BF16)
    if paired:
        seq_first = rows_of_seq_first(core_half(normed))
        mix_far = swapped(core_half(grad_mix), "batch", 1)

    proj = mm(normed, jnp.concatenate([w_bc, w_dt], axis=1))
    pre_bc = proj[:, : 2 * state].reshape(seqs, slots, 2 * state)
    projected = jnp.einsum("tg,gjn->tjn", normed, gate_input_weight, preferred_element_type=F32)
    projected = projected.transpose(1, 0, 2).reshape(2, seqs, slots, inner)
    edges = jnp.concatenate([projected[1, :, slots - EDGE :], pre_bc[:, slots - EDGE :]], axis=2)
    edges = shifted(edges, "seq", 1)
    edge_x, edge_bc = edges[..., :inner], edges[..., inner:]
    dtraw = proj[:, 2 * state :].reshape(seqs, slots, groups, heads).transpose(0, 2, 3, 1)
    params = head_params.reshape(3, groups, heads).transpose(1, 2, 0)
    gain = gate_gain.reshape(1, inner)

    part_of = lambda j: pl.BlockSpec((None, 1, slots, LANES), lambda b, g: (j, b, 0, g))
    grid = (seqs, groups)
    S = jax.ShapeDtypeStruct
    wide = pl.BlockSpec((1, slots, LANES), lambda b, g: (b, 0, g))
    edge = pl.BlockSpec((1, EDGE, LANES), lambda b, g: (b, 0, g))
    states = pl.BlockSpec((1, state, LANES), lambda b, g: (b, 0, g))
    line = pl.BlockSpec((1, 1, LANES), lambda b, g: (b, 0, g))
    taps = pl.BlockSpec((CONV + 1, LANES), lambda b, g: (0, g))
    gain_spec = pl.BlockSpec((1, LANES), lambda b, g: (0, g))
    per_seq = lambda *shape: pl.BlockSpec((1,) + shape, lambda b, g: (b,) + (0,) * len(shape))
    fixed = lambda *shape: pl.BlockSpec(shape, lambda b, g: (0,) * len(shape))
    by_head = lambda k: pl.BlockSpec((1, 1, k, slots), lambda b, g: (b, g, 0, 0))
    par_spec = pl.BlockSpec((1, heads, 3), lambda b, g: (g, 0, 0))
    wide_s = S((seqs, slots, inner), F32)
    wide_b = S((seqs, slots, inner), BF16)
    decay_s = S((seqs, state + EDGE, inner), F32)
    with_decay = pl.BlockSpec((1, state + EDGE, LANES), lambda b, g: (b, 0, g))
    decay_spec = pl.BlockSpec((1, EDGE, LANES), lambda b, g: (b, state // EDGE, g))
    bc_b = S((seqs, slots, state), F32)
    settings = pltpu.CompilerParams(vmem_limit_bytes=VMEM_LIMIT)

    local_state, u, b_act, c_act, steps = call(
        functools.partial(state_kernel, heads),
        [projected, edge_x, conv_x, pre_bc, edge_bc, conv_bc, dtraw, params],
        [
            part_of(1), edge, taps, per_seq(slots, 2 * state), per_seq(EDGE, 2 * state),
            fixed(CONV + 1, 2 * state), by_head(heads), par_spec,
        ],
        [with_decay, wide, per_seq(slots, state), per_seq(slots, state), by_head(2 * heads)],
        [
            decay_s, wide_s, bc_b, bc_b,
            S((seqs, groups, 2 * heads, slots), F32),
        ],
        grid,
        "scan_state",
        17,
        scratch=[pltpu.VMEM((state, slots), BF16)],
    )
    if paired:
        local_state, seq_first, grad_mix, steps = tied(local_state, seq_first, grad_mix, steps)

    def mix_back():
        return mm(grad_mix, w_out, ((1,), (1,))).reshape(seqs, slots, inner)

    def scan_inside(_):
        return call(
            functools.partial(inside_kernel, heads, width),
            [u, steps, params, b_act, c_act],
            [wide, by_head(2 * heads), par_spec, per_seq(slots, state), per_seq(slots, state)],
            wide,
            wide_s,
            grid,
            "scan_inside",
            18,
            scratch=[pltpu.VMEM((slots, slots), F32)],
        )

    entering, grad_out, local_out = passed_on(local_state, state, False, mix_back, scan_inside)
    if paired:
        entering, mix_far, seq_first = tied(entering, mix_far, seq_first)
        seq_second = rows_of_seq_second(*seq_first)

    y, sums = call(
        functools.partial(gate_kernel, heads),
        [local_out, entering, c_act, steps, projected, grad_out, gain],
        [wide, states, per_seq(slots, state), by_head(2 * heads), part_of(0), wide, gain_spec],
        [wide, per_seq(8, slots)],
        [wide_s, S((seqs, 8, slots), F32)],
        grid,
        "gate",
        15,
    )
    sums = head_sum(sums)

    gated, grad_y, grad_z, gain_grad, leaving = call(
        functools.partial(gate_back_kernel, heads, inner_all),
        [y, projected, grad_out, gain, sums, c_act, steps, local_state],
        [
            wide, part_of(0), wide, gain_spec, per_seq(8, slots), per_seq(slots, state), by_head(2 * heads),
            decay_spec,
        ],
        [wide, wide, wide, line, with_decay],
        [wide_b, wide_s, wide_b, S((seqs, 1, inner), F32), decay_s],
        grid,
        "gate_back",
        17,
        scratch=[pltpu.VMEM((state, slots), BF16)],
    )
    gated = gated.reshape(rows, inner)
    grad_z = grad_z.reshape(rows, inner)

    def scan_inside_back():
        inside, grad_bc = call(
            functools.partial(inside_back_kernel, heads, width),
            [u, steps, b_act, c_act, grad_y, entering],
            [wide, by_head(2 * heads), per_seq(slots, state), per_seq(slots, state), wide, states],
            [wide, per_seq(slots, 2 * state)],
            [wide_s, S((seqs, slots, 2 * state), F32)],
            grid,
            "scan_inside_back",
            26,
            scratch=[pltpu.VMEM((slots, slots), F32), pltpu.VMEM((slots, slots), F32)],
        )
        if not paired:
            return inside, grad_bc
        return inside, grad_bc, seq_second

    def rows_ready(beside):
        if not paired:
            return ()
        return assembled(rows_of_seq_third(*beside[2])), mm(gated, w_out)

    coming, beside, ready = passed_on(leaving, state, True, scan_inside_back, rows_ready)
    inside, grad_bc = beside[:2]
    if paired:
        coming, grad_z_sent, gated_sent, ready = tied(coming, grad_z, gated, ready)
        normed_far, mixed = ready
        z_columns = columns_of(grad_z_sent, "seq")
        parity = lax.axis_index("batch") % 2
        gated_own = halves(gated, 1, parity).astype(F32)
        gated_far = swapped(halves(gated_sent, 1, 1 - parity).astype(F32), "batch", 1)
    else:
        mixed = mm(gated, w_out)
    grad_pre, tail_x, first_x, taps_grad_x, grad_dt, params_grad, grad_b = call(
        functools.partial(scan_back_kernel, heads),
        [u, projected, edge_x, conv_x, dtraw, params, steps, b_act, y, grad_y, inside, entering, coming],
        [
            wide, part_of(1), edge, taps, by_head(heads), par_spec, by_head(2 * heads), per_seq(slots, state),
            wide, wide, wide, states, states,
        ],
        [
            wide, edge, edge, edge, by_head(heads),
            pl.BlockSpec((1, 1, heads, 3), lambda b, g: (b, g, 0, 0)), per_seq(slots, state),
        ],
        [
            wide_b, S((seqs, EDGE, inner), F32), S((seqs, EDGE, inner), F32), S((seqs, EDGE, inner), F32),
            S((seqs, groups, heads, slots), F32), S((seqs, groups, heads, 3), F32),
            S((seqs, slots, state), F32),
        ],
        grid,
        "scan_back",
        34,
    )
    if paired:
        later_x = shifted(first_x, "seq", -1)
        grad_pre, z_columns, gated_far = tied(grad_pre, z_columns, gated_far)
        part_z = weight_part(normed, normed_far, z_columns, "seq")
        later_x, part_z, tail_x = tied(later_x, part_z, tail_x)
        sum_z = over_batch(part_z)
        grad_pre, pieces = mended_pieces(grad_pre, tail_x, later_x, conv_x)
        pieces, grad_b = tied(pieces, grad_b)
        x_columns = pieces[:1] + [swapped(pieces[d], "seq", d) for d in (1, 2, 3)]
    grad_bc = grad_bc + jnp.pad(grad_b, ((0, 0), (0, 0), (0, state)))
    grad_bc = head_sum(grad_bc)
    if paired:
        mix_far = assembled(mix_far[None])[0]
        parts_out = pair_part(grad_mix, mix_far, gated_own, gated_far)
        x_columns, parts_out, grad_bc = tied(x_columns, parts_out, grad_bc)
        part_x = weight_part(normed, normed_far, x_columns, "seq")
        sum_x = over_batch(part_x)
        part_x, grad_bc = tied(part_x, grad_bc)

    one = lambda *shape: pl.BlockSpec((1,) + shape, lambda b: (b, 0, 0))
    rows8 = S((seqs, EDGE, 2 * state), F32)
    grad_pre_bc, tail_bc, first_bc, taps_grad_bc = call(
        conv_back_kernel,
        [pre_bc, edge_bc, conv_bc, grad_bc],
        [
            one(slots, 2 * state), one(EDGE, 2 * state),
            pl.BlockSpec((CONV + 1, 2 * state), lambda b: (0, 0)), one(slots, 2 * state),
        ],
        [one(slots, 2 * state), one(EDGE, 2 * state), one(EDGE, 2 * state), one(EDGE, 2 * state)],
        [S((seqs, slots, 2 * state), BF16), rows8, rows8, rows8],
        (seqs,),
        "conv_back",
        3,
    )

    def mended(value, tail, first, weights):
        later = shifted(first, "seq", -1)
        add = jnp.zeros_like(tail)
        for tap in range(CONV - 1):
            ahead = CONV - 1 - tap
            moved = jnp.pad(later[:, :ahead], ((0, 0), (EDGE - ahead, 0), (0, 0)))
            add = add + moved * weights[tap]
        return lax.dynamic_update_slice(value, (tail + add).astype(BF16), (0, slots - EDGE, 0))

    if not paired:
        grad_pre = mended(grad_pre, tail_x, first_x, conv_x)
    grad_pre = grad_pre.reshape(rows, inner)
    grad_pre_bc = mended(grad_pre_bc, tail_bc, first_bc, conv_bc).reshape(rows, 2 * state)
    grad_dtr = grad_dt.transpose(0, 3, 1, 2).reshape(rows, heads_dev).astype(BF16)

    if paired:
        a, b, z_pieces = first_transfers(parts_out, sum_z)
        a, b, z_pieces, grad_pre_bc, grad_dtr, grad_pre = tied(a, b, z_pieces, grad_pre_bc, grad_dtr, grad_pre)
        small = jnp.concatenate([halves(grad_pre_bc, 1, side), grad_dtr], axis=1)
        small = mm(small, normed, ((0,), (0,)))
    grad_zx = jnp.stack([grad_z, grad_pre], axis=1)
    portion = jnp.einsum("tjn,gjn->tg", grad_zx, gate_input_weight, preferred_element_type=F32)
    portion = portion + mm(grad_dtr, w_dt, ((1,), (1,)))
    if paired:
        small_rows = small.shape[0]
        out_sum, portion, mixed, sum_x = tied(second_transfers(a, b, small), portion, mixed, sum_x)
        out_pieces = sent_back(out_sum, "batch")
        x_pieces = sent_back(sum_x, "seq")
    mixed = head_sum(mixed)
    mixed_out = (mask * (hidden_f + mixed)).astype(BF16).reshape(seqs, slots, model)
    grad_normed = head_sum(portion) + mm(grad_pre_bc, w_bc, ((1,), (1,)))
    scaled_input = hidden_f * inv_rms
    grad_norm_gain = jnp.sum(grad_normed * scaled_input, axis=0)
    grad_scaled = grad_normed * norm_gain
    input_dot = jnp.mean(grad_scaled * scaled_input, axis=-1, keepdims=True)
    grad_hidden = grad_mix.astype(F32) + inv_rms * (grad_scaled - scaled_input * input_dot)
    grad_hidden = grad_hidden.reshape(seqs, slots, model)

    head_grad = params_grad.sum(axis=0).transpose(2, 0, 1).reshape(3, heads_dev)
    taps_sum = jnp.concatenate([taps_grad_x.sum(axis=0), taps_grad_bc.sum(axis=0)], axis=1)[: CONV + 1]
    pieces = [taps_sum, head_grad, gain_grad.sum(axis=0), grad_norm_gain]
    flat = jnp.concatenate([piece.reshape(-1) for piece in pieces])
    if paired:
        flat = added_over(flat, "seq")
        out_pieces, x_pieces, flat, grad_hidden, mixed_out = tied(out_pieces, x_pieces, flat, grad_hidden, mixed_out)
        flat = added_over(flat, "batch")
        grad_weight = finished(z_pieces, x_pieces)
        grad_w_out, done_small = out_weight(out_pieces, small_rows)
        bc_mine = done_small[:state]
        bc_other = swapped(bc_mine, "head", 1)
        grad_w_bc = jnp.concatenate(
            [jnp.where(side == 0, bc_mine, bc_other), jnp.where(side == 0, bc_other, bc_mine)], axis=0
        ).T
        grad_w_dt = done_small[state:].T
    else:
        scatter = functools.partial(lax.psum_scatter, axis_name=("batch", "seq"), tiled=True)
        over_slots = ((0,), (0,))
        grad_weight = scatter(
            jnp.stack([mm(normed, grad_z, over_slots), mm(normed, grad_pre, over_slots)], axis=1),
            scatter_dimension=0,
        )
        grad_w_bc = scatter(mm(normed, grad_pre_bc, over_slots), scatter_dimension=0)
        grad_w_dt = scatter(mm(normed, grad_dtr, over_slots), scatter_dimension=0)
        grad_w_out = scatter(mm(gated, grad_mix, over_slots), scatter_dimension=1)
        flat = lax.psum(flat, ("batch", "seq"))

    parted, start = [], 0
    for piece in pieces:
        parted.append(flat[start : start + piece.size].reshape(piece.shape))
        start += piece.size
    grad_conv, grad_head, grad_gate_gain, grad_norm_gain = parted
    return (
        mixed_out,
        grad_hidden,
        grad_norm_gain,
        grad_weight,
        grad_w_bc,
        grad_w_dt,
        grad_conv[:, :inner],
        grad_conv[:, inner:],
        grad_head,
        grad_gate_gain.reshape(inner),
        grad_w_out,
    )


def solution(mesh):
    placed = (
        P("batch", "seq", None),
        P(),
        P(None, None, "head"),
        P(),
        P(None, "head"),
        P(None, "head"),
        P(),
        P(None, "head"),
        P("head"),
        P("head", None),
        P("batch"),
        P("batch", "seq", None),
    )
    return jax.shard_map(
        per_device,
        mesh=mesh,
        in_specs=placed,
        out_specs=(
            P("batch", "seq", None),
            P("batch", "seq", None),
            P(),
            P(("batch", "seq"), None, "head"),
            P(("batch", "seq"), None),
            P(("batch", "seq"), "head"),
            P(None, "head"),
            P(),
            P(None, "head"),
            P("head"),
            P("head", ("batch", "seq")),
        ),
        check_vma=False,
    )
```

```python
import functools

import jax
import jax.numpy as jnp
from jax import lax
from jax.experimental import pallas as pl
from jax.experimental.pallas import tpu as pltpu
from jax.sharding import PartitionSpec as P

CONV = 4
EDGE = 8
LANES = 512
EPSILON = 1e-05
HIGHEST = lax.Precision.HIGHEST
F32 = jnp.float32
BF16 = jnp.bfloat16
VMEM_LIMIT = 48 * 1024 * 1024
COST = 0.25


def mm(a, b, dims=((1,), (0,)), precision=None):
    return lax.dot_general(a, b, (dims, ((), ())), precision=precision, preferred_element_type=F32)


def split(value, count):
    parts, rest = [], value
    for _ in range(count):
        part = rest.astype(BF16).astype(F32)
        parts.append(part)
        rest = rest - part
    return jnp.concatenate(parts, axis=0)


def of_head(rows, columns, heads):
    head = lax.broadcasted_iota(jnp.int32, (rows, columns), 0) % heads
    lane = lax.broadcasted_iota(jnp.int32, (rows, columns), 1) // (columns // heads)
    return (head == lane).astype(F32).astype(BF16)


def widen(rows, lanes):
    heads = rows.shape[0]
    return mm(split(rows, 2).astype(BF16), of_head(2 * heads, lanes, heads), ((0,), (0,)))


def head_sums(value, heads, parts=2):
    pick = of_head(heads, value.shape[1], heads)
    high = value.astype(BF16)
    total = mm(pick, high, ((1,), (1,)))
    if parts == 2:
        total = total + mm(pick, (value - high.astype(F32)).astype(BF16), ((1,), (1,)))
    return total


def row_sums(value):
    ones = jnp.ones((8, value.shape[1]), BF16)
    high = value.astype(BF16)
    return mm(ones, high, ((1,), (1,))) + mm(ones, (value - high.astype(F32)).astype(BF16), ((1,), (1,)))


def exact(rows, matrix, dims=((1,), (0,))):
    heads = rows.shape[0]
    result = mm(split(rows, 3).astype(BF16), matrix, dims)
    return result[:heads] + result[heads : 2 * heads] + result[2 * heads :]


def spreads(cumul):
    heads, slots = cumul.shape
    parts = split(cumul, 3)
    row = lax.broadcasted_iota(jnp.int32, parts.shape, 0) % heads

    def spread(head, start, size, end):
        mask = (row == head).astype(F32)
        left = jnp.concatenate([parts, mask], axis=0).astype(BF16)
        right = jnp.concatenate([mask, -parts], axis=0).astype(BF16)
        return mm(left[:, start : start + size], right[:, :end], ((0,), (0,)))

    return spread


def triangle(slots, dtype=F32):
    row = lax.broadcasted_iota(jnp.int32, (slots, slots), 0)
    column = lax.broadcasted_iota(jnp.int32, (slots, slots), 1)
    return (row >= column).astype(F32).astype(dtype)


def softplus(value):
    return jnp.maximum(value, 0.0) + jnp.log1p(jnp.exp(-jnp.abs(value)))


def slope(value, sig):
    return sig * (1.0 + value * (1.0 - sig))


def convolved(extended, taps, slots):
    total = taps[CONV : CONV + 1] + extended[EDGE : EDGE + slots] * taps[CONV - 1 : CONV]
    for tap in range(CONV - 1):
        start = EDGE - (CONV - 1) + tap
        total = total + extended[start : start + slots] * taps[tap : tap + 1]
    return total


def convolved_back(grad, pre, before, taps):
    slots, lanes = grad.shape
    padded = jnp.concatenate([grad, jnp.zeros((EDGE, lanes), F32)], axis=0)
    row = lax.broadcasted_iota(jnp.int32, (EDGE, lanes), 0)
    back = grad * taps[CONV - 1 : CONV]
    rows = []
    for tap in range(CONV - 1):
        ahead = CONV - 1 - tap
        moved = padded[ahead : ahead + slots]
        back = back + moved * taps[tap : tap + 1]
        first = jnp.where(row >= EDGE - ahead, pltpu.roll(grad[:EDGE], EDGE - ahead, 0), 0.0)
        total = jnp.sum(moved * pre, axis=0, keepdims=True)
        rows.append(total + jnp.sum(first * before, axis=0, keepdims=True))
    rows.append(jnp.sum(grad * pre, axis=0, keepdims=True))
    rows.append(jnp.sum(grad, axis=0, keepdims=True))
    rows.append(jnp.zeros((8 - len(rows), lanes), F32))
    return back, jnp.concatenate(rows, axis=0)


def pair_part_of(value, side, width):
    lane = lax.broadcasted_iota(jnp.int32, value.shape, 1) // width
    return jnp.where(lane == side, value, jnp.zeros_like(value))


def call(kernel, inputs, in_specs, out_specs, out_shape, grid, name, micros, scratch=(), index=None):
    scalars = () if index is None else (index.reshape(-1),)
    return pl.pallas_call(
        kernel,
        grid_spec=pltpu.PrefetchScalarGridSpec(
            num_scalar_prefetch=len(scalars),
            grid=grid,
            in_specs=list(in_specs),
            out_specs=out_specs,
            scratch_shapes=list(scratch),
        ),
        out_shape=out_shape,
        compiler_params=pltpu.CompilerParams(vmem_limit_bytes=VMEM_LIMIT),
        cost_estimate=pl.CostEstimate(
            flops=int(micros * COST * 1.1e9), bytes_accessed=int(micros * COST * 2e6), transcendentals=0
        ),
        name=name,
    )(*scalars, *inputs)


def state_kernel(
    heads, pre_x, edge_x, taps_x, pre_bc, edge_bc, taps_bc, dtraw, params,
    state_out, u_out, b_out, c_out, steps_out, b_turned,
):
    slots, lanes = pre_x.shape[1:]
    state = b_out.shape[2]

    @pl.when(pl.program_id(1) == 0)
    def _():
        ext = jnp.concatenate([edge_bc[0], pre_bc[0]], axis=0)
        u = convolved(ext, taps_bc[...], slots)
        act = u * jax.nn.sigmoid(u)
        b_out[0] = act[:, :state]
        c_out[0] = act[:, state:]
        b_turned[...] = act[:, :state].T.astype(BF16)

    ext = jnp.concatenate([edge_x[0], pre_x[0]], axis=0)
    u = convolved(ext, taps_x[...], slots)
    u_out[0] = u
    x = u * jax.nn.sigmoid(u)
    par = params[0]
    step = softplus(dtraw[0, 0] + par[:, 0:1])
    rate = step * -jnp.exp(par[:, 1:2])
    cumul = exact(rate, triangle(slots, BF16), ((1,), (1,)))
    steps_out[0, 0] = jnp.concatenate([step, cumul], axis=0)
    last = cumul[:, slots - 1 : slots]
    state_out[0, state:] = widen(jnp.broadcast_to(jnp.exp(last), (heads, 8)), lanes)
    xd = (widen(step, lanes) * x).astype(BF16)
    tail = (widen(jnp.exp(last - cumul), lanes) * xd.astype(F32)).astype(BF16)
    state_out[0, :state] = mm(b_turned[...], tail)


def inside_kernel(heads, width, u, steps, params, b_act, c_act, local_out, scores):
    slots, lanes = u.shape[1:]

    @pl.when(pl.program_id(1) == 0)
    def _():
        scores[...] = mm(c_act[0], b_act[0], ((1,), (1,)), HIGHEST) * triangle(slots)

    uv = u[0]
    x = uv * jax.nn.sigmoid(uv)
    step, cumul = steps[0, 0][:heads], steps[0, 0][heads:]
    spread = spreads(cumul)
    xd = (widen(step, lanes) * x).astype(BF16)
    skip = widen(jnp.broadcast_to(params[0][:, 2:3], (heads, 8)), lanes)[0:1] * x
    half = slots // 2
    for pair in range(heads // 2):
        at = slice(pair * 2 * width, (pair + 1) * 2 * width)
        top, low = skip[:half, at], skip[half:, at]
        for side in range(2):
            head = 2 * pair + side
            mine = pair_part_of(xd[:, at], side, width)
            decay = jnp.exp(jnp.minimum(spread(head, 0, half, half), 0.0))
            top = top + mm((scores[:half, :half] * decay).astype(BF16), mine[:half])
            decay = jnp.exp(jnp.minimum(spread(head, half, half, slots), 0.0))
            low = low + mm((scores[half:] * decay).astype(BF16), mine)
        local_out[0, :half, at] = top
        local_out[0, half:, at] = low


def gate_kernel(heads, local_out, entering, c_act, steps, z, grad_out, gain, y_out, sums):
    lanes = z.shape[-1]
    growth = widen(jnp.exp(steps[0, 0][heads:]), lanes)
    y = local_out[0] + growth * mm(c_act[0].astype(BF16), entering[0].astype(BF16))
    y_out[0] = y
    zv = z[0]
    g = y * (zv * jax.nn.sigmoid(zv))
    squares = row_sums(g * g)
    dots = row_sums(grad_out[0] * gain[...] * g)
    row = lax.broadcasted_iota(jnp.int32, squares.shape, 0)
    both = jnp.where(row == 0, squares, jnp.where(row == 1, dots, 0.0))

    @pl.when(pl.program_id(1) == 0)
    def _():
        sums[0] = both

    @pl.when(pl.program_id(1) > 0)
    def _():
        sums[0] += both


def gate_back_kernel(
    heads, inner_all, y, z, grad_out, gain, sums, c_act, steps, decay,
    gated_out, grad_y, grad_z, gain_grad, leaving, c_turned,
):
    lanes = z.shape[-1]

    @pl.when(pl.program_id(1) == 0)
    def _():
        c_turned[...] = c_act[0].T.astype(BF16)

    inv_row = lax.rsqrt(sums[0][0:1] / inner_all + EPSILON)
    mean_row = inv_row * sums[0][1:2] / inner_all
    rows = jnp.concatenate([split(inv_row, 2), split(mean_row, 2), jnp.zeros_like(sums[0][:4])], axis=0)
    row = lax.broadcasted_iota(jnp.int32, (8, lanes), 0)
    rows = rows.astype(BF16)
    inv = mm(rows, (row < 2).astype(F32).astype(BF16), ((0,), (0,)))
    mean = mm(rows, ((row >= 2) & (row < 4)).astype(F32).astype(BF16), ((0,), (0,)))
    zv, yv = z[0], y[0]
    sig = jax.nn.sigmoid(zv)
    silu = zv * sig
    normed = yv * silu * inv
    gated_out[0] = (normed * gain[...]).astype(BF16)
    gain_grad[0] = jnp.sum(grad_out[0] * normed, axis=0, keepdims=True)
    dg = inv * (grad_out[0] * gain[...] - normed * mean)
    dy = dg * silu
    grad_y[0] = dy
    grad_z[0] = (dg * yv * slope(zv, sig)).astype(BF16)
    growth = widen(jnp.exp(steps[0, 0][heads:]), lanes)
    state = c_turned.shape[0]
    leaving[0, :state] = mm(c_turned[...], (growth * dy).astype(BF16))
    leaving[0, state:] = decay[0]


def inside_back_kernel(
    heads, width, u, steps, b_act, c_act, grad_y, entering,
    grad_xd_out, grad_bc, grad_scores, scores,
):
    slots, lanes = u.shape[1:]

    @pl.when(pl.program_id(1) == 0)
    def _():
        scores[...] = mm(c_act[0], b_act[0], ((1,), (1,)), HIGHEST) * triangle(slots)
        grad_scores[...] = jnp.zeros_like(grad_scores)
        grad_bc[...] = jnp.zeros_like(grad_bc)

    uv = u[0]
    step, cumul = steps[0, 0][:heads], steps[0, 0][heads:]
    spread = spreads(cumul)
    xd = (widen(step, lanes) * (uv * jax.nn.sigmoid(uv))).astype(BF16)
    dy = grad_y[0]
    dy_b = dy.astype(BF16)
    half = slots // 2
    sum_top = jnp.zeros((half, half), F32)
    sum_low = jnp.zeros((half, slots), F32)
    for pair in range(heads // 2):
        at = slice(pair * 2 * width, (pair + 1) * 2 * width)
        xd_pair = xd[:, at]
        top, whole = None, None
        for side in range(2):
            head = 2 * pair + side
            mine = pair_part_of(dy_b[:, at], side, width)
            decay = jnp.exp(jnp.minimum(spread(head, 0, half, half), 0.0))
            weights = (scores[:half, :half] * decay).astype(BF16)
            part = mm(weights, mine[:half], ((0,), (0,)))
            top = part if top is None else top + part
            sum_top = sum_top + mm(mine[:half], xd_pair[:half], ((1,), (1,))) * decay
            decay = jnp.exp(jnp.minimum(spread(head, half, half, slots), 0.0))
            weights = (scores[half:] * decay).astype(BF16)
            part = mm(weights, mine[half:], ((0,), (0,)))
            whole = part if whole is None else whole + part
            sum_low = sum_low + mm(mine[half:], xd_pair, ((1,), (1,))) * decay
        grad_xd_out[0, :half, at] = whole[:half] + top
        grad_xd_out[0, half:, at] = whole[half:]
    grad_scores[:half, :half] += sum_top
    grad_scores[half:] += sum_low
    growth = widen(jnp.exp(cumul), lanes)
    grad_c = mm((growth * dy).astype(BF16), entering[0].astype(BF16), ((1,), (1,)))
    grad_bc[0] += jnp.concatenate([jnp.zeros_like(grad_c), grad_c], axis=1)

    @pl.when(pl.program_id(1) == pl.num_programs(1) - 1)
    def _():
        causal = grad_scores[...] * triangle(slots)
        from_c = mm(causal, c_act[0], ((0,), (0,)), HIGHEST)
        grad_bc[0] += jnp.concatenate([from_c, mm(causal, b_act[0], precision=HIGHEST)], axis=1)


def scan_back_kernel(
    heads, u, pre_x, edge_x, taps_x, dtraw, params, steps, b_act, y, grad_y, inside, entering, coming,
    grad_pre, tail_rows, head_rows, taps_grad, grad_dt, params_grad, grad_b,
):
    slots, lanes = u.shape[1:]

    @pl.when(pl.program_id(1) == 0)
    def _():
        grad_b[...] = jnp.zeros_like(grad_b)

    uv = u[0]
    sig = jax.nn.sigmoid(uv)
    x = uv * sig
    par = params[0]
    decay_a = -jnp.exp(par[:, 1:2])
    step, cumul = steps[0, 0][:heads], steps[0, 0][heads:]
    last = cumul[:, slots - 1 : slots]
    step_wide = widen(step, lanes)
    tail_wide = widen(jnp.exp(last - cumul), lanes)
    lines = widen(jnp.concatenate([jnp.exp(last)] * 4 + [par[:, 2:3]] * 4, axis=1), lanes)
    skip = lines[4:5]
    xd = (step_wide * x).astype(BF16)
    xd_f = xd.astype(F32)
    dy = grad_y[0]
    coming_b = coming[0].astype(BF16)
    from_next = tail_wide * mm(b_act[0].astype(BF16), coming_b)
    grad_xd = inside[0] + from_next
    grad_b[0] += mm((tail_wide * xd_f).astype(BF16), coming_b, ((1,), (1,)))

    direct = head_sums(x * grad_xd, heads, 1)
    ys = y[0] - skip * x
    moved = head_sums(dy.astype(BF16).astype(F32) * ys - xd_f * grad_xd, heads)
    ends = lines[0:1] * jnp.sum(coming[0] * entering[0], axis=0, keepdims=True)
    ends = ends + jnp.sum(xd_f * from_next, axis=0, keepdims=True)
    skips = jnp.sum(dy * x, axis=0, keepdims=True)
    columns = head_sums(jnp.concatenate([ends, skips, jnp.zeros((6, lanes), F32)], axis=0), heads)
    later = exact(moved, triangle(slots, BF16)) + columns[:, 0:1]
    grad_step = (direct + decay_a * later) * jax.nn.sigmoid(dtraw[0, 0] + par[:, 0:1])
    grad_dt[0, 0] = grad_step
    params_grad[0, 0] = jnp.concatenate(
        [
            jnp.sum(grad_step, axis=1, keepdims=True),
            jnp.sum(step * later, axis=1, keepdims=True) * decay_a,
            columns[:, 1:2],
        ],
        axis=1,
    )
    du = (step_wide * grad_xd + skip * dy) * slope(uv, sig)
    back, rows8 = convolved_back(du, pre_x[0], edge_x[0], taps_x[...])
    grad_pre[0] = back.astype(BF16)
    tail_rows[0] = back[slots - EDGE :]
    head_rows[0] = du[:EDGE]
    taps_grad[0] = rows8


def conv_back_kernel(pre, edge, taps, grad_act, grad_pre, tail_rows, head_rows, taps_grad):
    slots = pre.shape[1]
    ext = jnp.concatenate([edge[0], pre[0]], axis=0)
    u = convolved(ext, taps[...], slots)
    du = grad_act[0] * slope(u, jax.nn.sigmoid(u))
    back, rows8 = convolved_back(du, pre[0], edge[0], taps[...])
    grad_pre[0] = back.astype(BF16)
    tail_rows[0] = back[slots - EDGE :]
    head_rows[0] = du[:EDGE]
    taps_grad[0] = rows8


def assemble_kernel(mine, theirs, side, result):
    first = side[0] == 0
    half = mine.shape[2]
    result[0, :, :half] = jnp.where(first, mine[0], theirs[0]).astype(BF16)
    result[0, :, half:] = jnp.where(first, theirs[0], mine[0]).astype(BF16)


def weight_kernel(parts, own_rows, far_rows, *refs):
    result, columns = refs[-2:]
    slots = own_rows.shape[0]

    @pl.when(pl.program_id(0) == 0)
    def _():
        for index in range(parts):
            columns[:, pl.ds(index * slots, slots)] = refs[index][...].T.astype(BF16)

    total = mm(columns[:, :slots], own_rows[...])
    for index in range(1, parts):
        total = total + mm(columns[:, index * slots : (index + 1) * slots], far_rows[index - 1])
    for tile in range(result.shape[0] * result.shape[1]):
        piece = total[:, tile * 128 : (tile + 1) * 128]
        if result.shape[0] == 1:
            result[0, tile] = piece
        else:
            result[tile, 0] = piece


def pair_kernel(place, rows, far_rows, own, far, keep_a, send_a, keep_b, send_b, columns):
    slots = rows.shape[0]
    step = pl.program_id(0)

    @pl.when(step == 0)
    def _():
        columns[:, :slots] = own[...].T.astype(BF16)
        columns[:, slots:] = far[...].T.astype(BF16)

    total = mm(columns[:, :slots], rows[...]) + mm(columns[:, slots:], far_rows[...])
    for tile in range(4):
        piece = total[:, tile * 128 : (tile + 1) * 128]
        away = place[0] ^ tile
        for first, keep, send, bit in ((True, keep_a, send_a, away % 2), (False, keep_b, send_b, away // 2)):
            at = away // 2 if first else away % 2
            mine = step < 2 if first else step >= 2

            @pl.when(mine & (bit == 0))
            def _():
                keep[at, 0] = piece

            @pl.when(mine & (bit == 1))
            def _():
                send[at, 0] = piece


def mend_kernel(place, value, tail, later, taps, mended, *pieces):
    seqs, slots, _ = value.shape
    row = lax.broadcasted_iota(jnp.int32, (EDGE, value.shape[2]), 0)
    for seq in range(seqs):
        end = tail[seq]
        for tap in range(CONV - 1):
            ahead = CONV - 1 - tap
            moved = pltpu.roll(later[seq], EDGE - ahead, 0)
            end = end + jnp.where(row >= EDGE - ahead, moved, 0.0) * taps[tap : tap + 1]
        last = jnp.concatenate([value[seq, slots - 16 :][: 16 - EDGE].astype(F32), end], axis=0).astype(BF16)
        mended[seq, : slots - 16] = value[seq, : slots - 16]
        mended[seq, slots - 16 :] = last
        for index, piece in enumerate(pieces):

            @pl.when(pl.program_id(0) == index)
            def _():
                piece[seq * slots : (seq + 1) * slots - 16] = value[seq, : slots - 16].astype(F32)
                piece[(seq + 1) * slots - 16 : (seq + 1) * slots] = last.astype(F32)


def finish_kernel(place, *refs):
    result = refs[-1]
    for index in range(4):

        @pl.when(pl.program_id(0) == index)
        def _():
            result[:, 0] = refs[index][...].T
            result[:, 1] = refs[4 + index][...].T


def swapped(value, axis, bit):
    count = lax.axis_size(axis)
    return lax.ppermute(value, axis, [(i, i ^ bit) for i in range(count)])


def shifted(value, axis, steps):
    count = lax.axis_size(axis)
    initial, last = (max(0, -steps), min(count, count - steps))
    return lax.ppermute(value, axis, [(source, source + steps) for source in range(initial, last)])


def head_sum(value):
    if lax.axis_size("head") == 2:
        return value + swapped(value, "head", 1)
    return lax.psum(value, "head")


def gathered_pass(both, rows, reverse):
    count = lax.axis_size("seq")
    place = lax.axis_index("seq")
    gathered = lax.all_gather(both, "seq")
    state = jnp.zeros_like(both[:, :rows])
    for turn in range(count - 1):
        source = count - 1 - turn if reverse else turn
        ahead = source > place if reverse else source < place
        later = gathered[source, :, rows : rows + 1] * state + gathered[source, :, :rows]
        state = jnp.where(ahead, later, state)
    return state


def chosen(pieces, index):
    low = jnp.where(index % 2 == 0, pieces[0], pieces[1])
    high = jnp.where(index % 2 == 0, pieces[2], pieces[3])
    return jnp.where(index < 2, low, high)


def quarter(value, axis, index):
    size = value.shape[axis] // 4
    return lax.dynamic_slice_in_dim(value, index * size, size, axis)


def tied(*values):
    return lax.optimization_barrier(values)


def passed_on(both, rows, reverse, first, second):
    if lax.axis_size("seq") != 4:
        beside_first = first()
        return gathered_pass(both, rows, reverse), beside_first, second(beside_first)
    place = lax.axis_index("seq")
    got = [quarter(both, 2, place)] + [swapped(quarter(both, 2, place ^ d), "seq", d) for d in (1, 2, 3)]
    got, beside_first = tied(got, first())
    order = (3, 2, 1, 0) if reverse else (0, 1, 2, 3)
    state = jnp.zeros_like(got[0][:, :rows])
    enters = [None] * 4
    for source in order:
        enters[source] = state
        if source != order[-1]:
            piece = chosen(got, place ^ source)
            state = piece[:, rows : rows + 1] * state + piece[:, :rows]
    back = [chosen(enters, place)] + [swapped(chosen(enters, place ^ d), "seq", d) for d in (1, 2, 3)]
    back, beside_second = tied(back, second(beside_first))
    entering = jnp.concatenate([chosen(back, place ^ index) for index in range(4)], axis=2)
    return entering, beside_first, beside_second


def halves(value, axis, which):
    size = value.shape[axis] // 2
    return lax.dynamic_slice_in_dim(value, which * size, size, axis)


def core_half(value):
    return halves(value.astype(F32), 1, lax.axis_index("head"))


def rows_of_seq_first(half):
    cut = half.shape[1] // 2
    a, b = half[:, :cut], half[:, cut:]
    return a, b, swapped(a, "seq", 1), swapped(b, "seq", 2)


def rows_of_seq_second(a, b, a1, b2):
    return a1, swapped(jnp.stack([a, a1]), "seq", 2), b2, swapped(jnp.stack([b, b2]), "seq", 1)


def rows_of_seq_third(a1, a23, b2, b13):
    high = jnp.stack([b13[0], b2, b13[1]])
    return jnp.concatenate([jnp.concatenate([a1[None], a23], axis=0), high], axis=2)


def assembled(mine):
    side = lax.axis_index("head").reshape(1)
    theirs = swapped(mine, "head", 1)
    count, slots, half = mine.shape
    block = pl.BlockSpec((1, slots, half), lambda i: (i, 0, 0))
    return call(
        assemble_kernel,
        [mine, theirs, side],
        [block, block, pl.BlockSpec(memory_space=pltpu.SMEM)],
        pl.BlockSpec((1, slots, 2 * half), lambda i: (i, 0, 0)),
        jax.ShapeDtypeStruct((count, slots, 2 * half), BF16),
        (count,),
        "assemble",
        count,
    )


def columns_of(value, axis, dim=1):
    place = lax.axis_index(axis)
    piece = lambda index: quarter(value, dim, index).astype(F32)
    return [piece(place)] + [swapped(piece(place ^ d), axis, d) for d in (1, 2, 3)]


def weight_part(own_rows, far_rows, columns, axis):
    slots, model = own_rows.shape
    size = columns[0].shape[1]
    parts = len(columns)
    whole = lambda a: pl.BlockSpec(a.shape, lambda i: (0,) * a.ndim)
    if axis == "seq":
        out_spec = pl.BlockSpec((1, 4, size, 128), lambda i: (i, 0, 0, 0))
    else:
        out_spec = pl.BlockSpec((4, 1, size, 128), lambda i: (0, i, 0, 0))
    return call(
        functools.partial(weight_kernel, parts),
        [own_rows, far_rows, *columns],
        [
            pl.BlockSpec((slots, model // 4), lambda i: (0, i)),
            pl.BlockSpec((parts - 1, slots, model // 4), lambda i: (0, 0, i)),
            *[whole(c) for c in columns],
        ],
        out_spec,
        jax.ShapeDtypeStruct((4, 4, size, 128), F32),
        (4,),
        "weight_part",
        1,
        scratch=[pltpu.VMEM((size, parts * slots), BF16)],
    )


def over_batch(part):
    return lax.psum_scatter(part, "batch", scatter_dimension=0, tiled=True)[0]


def sent_back(summed, axis):
    place = lax.axis_index(axis)
    take = lambda index: lax.dynamic_index_in_dim(summed, index, 0, False)
    return [take(place)] + [swapped(take(place ^ d), axis, d) for d in (1, 2, 3)]


def finished(z_pieces, x_pieces):
    size, block = z_pieces[0].shape
    whole = pl.BlockSpec((size, block), lambda i, p: (0, 0))
    return call(
        finish_kernel,
        [*z_pieces, *x_pieces],
        [whole] * 8,
        pl.BlockSpec((block, 2, size), lambda i, p: (0, 0, i ^ p[0])),
        jax.ShapeDtypeStruct((block, 2, 4 * size), F32),
        (4,),
        "finish",
        4,
        index=lax.axis_index("seq"),
    )


def mended_pieces(value, tail, later, taps):
    seqs, slots, inner = value.shape
    size = inner // 4
    at = lambda *shape: pl.BlockSpec(shape + (size,), lambda i, p: (0,) * len(shape) + (i ^ p[0],))
    mended, *pieces = call(
        mend_kernel,
        [value, tail, later, taps],
        [at(seqs, slots), at(seqs, EDGE), at(seqs, EDGE), at(CONV + 1)],
        [at(seqs, slots)] + [pl.BlockSpec((seqs * slots, size), lambda i, p: (0, 0))] * 4,
        [jax.ShapeDtypeStruct(value.shape, BF16)] + [jax.ShapeDtypeStruct((seqs * slots, size), F32)] * 4,
        (4,),
        "mend",
        4,
        index=lax.axis_index("seq"),
    )
    return mended, pieces


def pair_part(rows, far_rows, own, far):
    slots, model = rows.shape
    size = own.shape[1]
    whole = lambda v: pl.BlockSpec(v.shape, lambda i, p: (0,) * v.ndim)
    part = pl.BlockSpec((slots, model // 4), lambda i, p: (0, i))
    a_spec = pl.BlockSpec((2, 1, size, 128), lambda i, p: (0, jnp.minimum(i, 1), 0, 0))
    b_spec = pl.BlockSpec((2, 1, size, 128), lambda i, p: (0, jnp.maximum(i - 2, 0), 0, 0))
    return call(
        pair_kernel,
        [rows, far_rows, own, far],
        [part, part, whole(own), whole(far)],
        [a_spec, a_spec, b_spec, b_spec],
        [jax.ShapeDtypeStruct((2, 2, size, 128), F32)] * 4,
        (4,),
        "pair_part",
        1,
        scratch=[pltpu.VMEM((size, 2 * slots), BF16)],
        index=lax.axis_index("seq"),
    )


def small_step(value, axis, bit, index):
    pick = lambda which: lax.dynamic_index_in_dim(value, which, 0, False)
    return pick(index) + swapped(pick(1 - index), axis, bit)


def first_transfers(parts, sum_z):
    keep_a, send_a, keep_b, send_b = parts
    return keep_a + swapped(send_a, "seq", 1), keep_b + swapped(send_b, "seq", 2), sent_back(sum_z, "seq")


def second_transfers(a, b, small):
    small = small.reshape(-1, 2, 2, 2, 2, small.shape[1] // 16).transpose(4, 3, 1, 2, 0, 5)
    a = a[0] + swapped(a[1], "seq", 2)
    b = b[0] + swapped(b[1], "seq", 1)
    small = small_step(small, "seq", 1, lax.axis_index("seq") % 2)
    small = small_step(small, "seq", 2, lax.axis_index("seq") // 2)
    small = small.reshape((4,) + small.shape[2:])
    return jnp.concatenate([jnp.concatenate([a, b], axis=0), small], axis=1)


def out_weight(pieces, small):
    even, odd = pieces[0] + pieces[2], pieces[1] + pieces[3]
    size = even.shape[0] - small
    parity = lax.axis_index("batch") % 2
    low = jnp.where(parity == 0, even[:size], odd[:size])
    high = jnp.where(parity == 0, odd[:size], even[:size])
    return jnp.concatenate([low, high], axis=0), even[size:] + odd[size:]


def added_over(values, axis):
    far = [swapped(values, axis, d) for d in (1, 2, 3)]
    return (values + far[0]) + (far[1] + far[2])


def per_device(
    hidden,
    norm_gain,
    gate_input_weight,
    w_bc,
    w_dt,
    conv_x,
    conv_bc,
    head_params,
    gate_gain,
    w_out,
    lengths,
    cotangent,
):
    seqs, slots, model = hidden.shape
    rows = seqs * slots
    inner = gate_input_weight.shape[2]
    heads_dev = w_dt.shape[1]
    width = inner // heads_dev
    state = w_bc.shape[1] // 2
    inner_all = inner * lax.axis_size("head")
    heads = LANES // width
    groups = inner // LANES
    side = lax.axis_index("head")
    paired = lax.axis_size("batch") == 4 and lax.axis_size("seq") == 4 and lax.axis_size("head") == 2

    positions = lax.axis_index("seq") * slots + jnp.arange(slots)
    mask = (positions[None, :] < lengths[:, None]).astype(F32).reshape(rows, 1)
    hidden_f = hidden.reshape(rows, model).astype(F32)
    inv_rms = lax.rsqrt(jnp.mean(hidden_f * hidden_f, axis=-1, keepdims=True) + EPSILON)
    normed = (hidden_f * inv_rms * norm_gain).astype(BF16)
    grad_mix = (cotangent.reshape(rows, model).astype(F32) * mask).astype(BF16)
    if paired:
        seq_first = rows_of_seq_first(core_half(normed))
        mix_far = swapped(core_half(grad_mix), "batch", 1)

    proj = mm(normed, jnp.concatenate([w_bc, w_dt], axis=1))
    pre_bc = proj[:, : 2 * state].reshape(seqs, slots, 2 * state)
    projected = jnp.einsum("tg,gjn->tjn", normed, gate_input_weight, preferred_element_type=F32)
    projected = projected.transpose(1, 0, 2).reshape(2, seqs, slots, inner)
    edges = jnp.concatenate([projected[1, :, slots - EDGE :], pre_bc[:, slots - EDGE :]], axis=2)
    edges = shifted(edges, "seq", 1)
    edge_x, edge_bc = edges[..., :inner], edges[..., inner:]
    dtraw = proj[:, 2 * state :].reshape(seqs, slots, groups, heads).transpose(0, 2, 3, 1)
    params = head_params.reshape(3, groups, heads).transpose(1, 2, 0)
    gain = gate_gain.reshape(1, inner)

    part_of = lambda j: pl.BlockSpec((None, 1, slots, LANES), lambda b, g: (j, b, 0, g))
    grid = (seqs, groups)
    S = jax.ShapeDtypeStruct
    wide = pl.BlockSpec((1, slots, LANES), lambda b, g: (b, 0, g))
    edge = pl.BlockSpec((1, EDGE, LANES), lambda b, g: (b, 0, g))
    states = pl.BlockSpec((1, state, LANES), lambda b, g: (b, 0, g))
    line = pl.BlockSpec((1, 1, LANES), lambda b, g: (b, 0, g))
    taps = pl.BlockSpec((CONV + 1, LANES), lambda b, g: (0, g))
    gain_spec = pl.BlockSpec((1, LANES), lambda b, g: (0, g))
    per_seq = lambda *shape: pl.BlockSpec((1,) + shape, lambda b, g: (b,) + (0,) * len(shape))
    fixed = lambda *shape: pl.BlockSpec(shape, lambda b, g: (0,) * len(shape))
    by_head = lambda k: pl.BlockSpec((1, 1, k, slots), lambda b, g: (b, g, 0, 0))
    par_spec = pl.BlockSpec((1, heads, 3), lambda b, g: (g, 0, 0))
    wide_s = S((seqs, slots, inner), F32)
    wide_b = S((seqs, slots, inner), BF16)
    decay_s = S((seqs, state + EDGE, inner), F32)
    with_decay = pl.BlockSpec((1, state + EDGE, LANES), lambda b, g: (b, 0, g))
    decay_spec = pl.BlockSpec((1, EDGE, LANES), lambda b, g: (b, state // EDGE, g))
    bc_b = S((seqs, slots, state), F32)
    settings = pltpu.CompilerParams(vmem_limit_bytes=VMEM_LIMIT)

    local_state, u, b_act, c_act, steps = call(
        functools.partial(state_kernel, heads),
        [projected, edge_x, conv_x, pre_bc, edge_bc, conv_bc, dtraw, params],
        [
            part_of(1), edge, taps, per_seq(slots, 2 * state), per_seq(EDGE, 2 * state),
            fixed(CONV + 1, 2 * state), by_head(heads), par_spec,
        ],
        [with_decay, wide, per_seq(slots, state), per_seq(slots, state), by_head(2 * heads)],
        [
            decay_s, wide_s, bc_b, bc_b,
            S((seqs, groups, 2 * heads, slots), F32),
        ],
        grid,
        "scan_state",
        17,
        scratch=[pltpu.VMEM((state, slots), BF16)],
    )
    if paired:
        local_state, seq_first, grad_mix, steps = tied(local_state, seq_first, grad_mix, steps)

    def mix_back():
        return mm(grad_mix, w_out, ((1,), (1,))).reshape(seqs, slots, inner)

    def scan_inside(_):
        return call(
            functools.partial(inside_kernel, heads, width),
            [u, steps, params, b_act, c_act],
            [wide, by_head(2 * heads), par_spec, per_seq(slots, state), per_seq(slots, state)],
            wide,
            wide_s,
            grid,
            "scan_inside",
            18,
            scratch=[pltpu.VMEM((slots, slots), F32)],
        )

    entering, grad_out, local_out = passed_on(local_state, state, False, mix_back, scan_inside)
    if paired:
        entering, mix_far, seq_first = tied(entering, mix_far, seq_first)
        seq_second = rows_of_seq_second(*seq_first)

    y, sums = call(
        functools.partial(gate_kernel, heads),
        [local_out, entering, c_act, steps, projected, grad_out, gain],
        [wide, states, per_seq(slots, state), by_head(2 * heads), part_of(0), wide, gain_spec],
        [wide, per_seq(8, slots)],
        [wide_s, S((seqs, 8, slots), F32)],
        grid,
        "gate",
        15,
    )
    sums = head_sum(sums)

    gated, grad_y, grad_z, gain_grad, leaving = call(
        functools.partial(gate_back_kernel, heads, inner_all),
        [y, projected, grad_out, gain, sums, c_act, steps, local_state],
        [
            wide, part_of(0), wide, gain_spec, per_seq(8, slots), per_seq(slots, state), by_head(2 * heads),
            decay_spec,
        ],
        [wide, wide, wide, line, with_decay],
        [wide_b, wide_s, wide_b, S((seqs, 1, inner), F32), decay_s],
        grid,
        "gate_back",
        17,
        scratch=[pltpu.VMEM((state, slots), BF16)],
    )
    gated = gated.reshape(rows, inner)
    grad_z = grad_z.reshape(rows, inner)

    def scan_inside_back():
        inside, grad_bc = call(
            functools.partial(inside_back_kernel, heads, width),
            [u, steps, b_act, c_act, grad_y, entering],
            [wide, by_head(2 * heads), per_seq(slots, state), per_seq(slots, state), wide, states],
            [wide, per_seq(slots, 2 * state)],
            [wide_s, S((seqs, slots, 2 * state), F32)],
            grid,
            "scan_inside_back",
            26,
            scratch=[pltpu.VMEM((slots, slots), F32), pltpu.VMEM((slots, slots), F32)],
        )
        if not paired:
            return inside, grad_bc
        return inside, grad_bc, seq_second

    def rows_ready(beside):
        if not paired:
            return ()
        return assembled(rows_of_seq_third(*beside[2])), mm(gated, w_out)

    coming, beside, ready = passed_on(leaving, state, True, scan_inside_back, rows_ready)
    inside, grad_bc = beside[:2]
    if paired:
        coming, grad_z_sent, gated_sent, ready = tied(coming, grad_z, gated, ready)
        normed_far, mixed = ready
        z_columns = columns_of(grad_z_sent, "seq")
        parity = lax.axis_index("batch") % 2
        gated_own = halves(gated, 1, parity).astype(F32)
        gated_far = swapped(halves(gated_sent, 1, 1 - parity).astype(F32), "batch", 1)
    else:
        mixed = mm(gated, w_out)
    grad_pre, tail_x, first_x, taps_grad_x, grad_dt, params_grad, grad_b = call(
        functools.partial(scan_back_kernel, heads),
        [u, projected, edge_x, conv_x, dtraw, params, steps, b_act, y, grad_y, inside, entering, coming],
        [
            wide, part_of(1), edge, taps, by_head(heads), par_spec, by_head(2 * heads), per_seq(slots, state),
            wide, wide, wide, states, states,
        ],
        [
            wide, edge, edge, edge, by_head(heads),
            pl.BlockSpec((1, 1, heads, 3), lambda b, g: (b, g, 0, 0)), per_seq(slots, state),
        ],
        [
            wide_b, S((seqs, EDGE, inner), F32), S((seqs, EDGE, inner), F32), S((seqs, EDGE, inner), F32),
            S((seqs, groups, heads, slots), F32), S((seqs, groups, heads, 3), F32),
            S((seqs, slots, state), F32),
        ],
        grid,
        "scan_back",
        34,
    )
    if paired:
        later_x = shifted(first_x, "seq", -1)
        grad_pre, z_columns, gated_far = tied(grad_pre, z_columns, gated_far)
        part_z = weight_part(normed, normed_far, z_columns, "seq")
        later_x, part_z, tail_x = tied(later_x, part_z, tail_x)
        sum_z = over_batch(part_z)
        grad_pre, pieces = mended_pieces(grad_pre, tail_x, later_x, conv_x)
        pieces, grad_b = tied(pieces, grad_b)
        x_columns = pieces[:1] + [swapped(pieces[d], "seq", d) for d in (1, 2, 3)]
    grad_bc = grad_bc + jnp.pad(grad_b, ((0, 0), (0, 0), (0, state)))
    grad_bc = head_sum(grad_bc)
    if paired:
        mix_far = assembled(mix_far[None])[0]
        parts_out = pair_part(grad_mix, mix_far, gated_own, gated_far)
        x_columns, parts_out, grad_bc = tied(x_columns, parts_out, grad_bc)
        part_x = weight_part(normed, normed_far, x_columns, "seq")
        sum_x = over_batch(part_x)
        part_x, grad_bc = tied(part_x, grad_bc)

    one = lambda *shape: pl.BlockSpec((1,) + shape, lambda b: (b, 0, 0))
    rows8 = S((seqs, EDGE, 2 * state), F32)
    grad_pre_bc, tail_bc, first_bc, taps_grad_bc = call(
        conv_back_kernel,
        [pre_bc, edge_bc, conv_bc, grad_bc],
        [
            one(slots, 2 * state), one(EDGE, 2 * state),
            pl.BlockSpec((CONV + 1, 2 * state), lambda b: (0, 0)), one(slots, 2 * state),
        ],
        [one(slots, 2 * state), one(EDGE, 2 * state), one(EDGE, 2 * state), one(EDGE, 2 * state)],
        [S((seqs, slots, 2 * state), BF16), rows8, rows8, rows8],
        (seqs,),
        "conv_back",
        3,
    )

    def mended(value, tail, first, weights):
        later = shifted(first, "seq", -1)
        add = jnp.zeros_like(tail)
        for tap in range(CONV - 1):
            ahead = CONV - 1 - tap
            moved = jnp.pad(later[:, :ahead], ((0, 0), (EDGE - ahead, 0), (0, 0)))
            add = add + moved * weights[tap]
        return lax.dynamic_update_slice(value, (tail + add).astype(BF16), (0, slots - EDGE, 0))

    if not paired:
        grad_pre = mended(grad_pre, tail_x, first_x, conv_x)
    grad_pre = grad_pre.reshape(rows, inner)
    grad_pre_bc = mended(grad_pre_bc, tail_bc, first_bc, conv_bc).reshape(rows, 2 * state)
    grad_dtr = grad_dt.transpose(0, 3, 1, 2).reshape(rows, heads_dev).astype(BF16)

    if paired:
        a, b, z_pieces = first_transfers(parts_out, sum_z)
        a, b, z_pieces, grad_pre_bc, grad_dtr, grad_pre = tied(a, b, z_pieces, grad_pre_bc, grad_dtr, grad_pre)
        small = jnp.concatenate([halves(grad_pre_bc, 1, side), grad_dtr], axis=1)
        small = mm(small, normed, ((0,), (0,)))
    grad_zx = jnp.stack([grad_z, grad_pre], axis=1)
    portion = jnp.einsum("tjn,gjn->tg", grad_zx, gate_input_weight, preferred_element_type=F32)
    portion = portion + mm(grad_dtr, w_dt, ((1,), (1,)))
    if paired:
        small_rows = small.shape[0]
        out_sum, portion, mixed, sum_x = tied(second_transfers(a, b, small), portion, mixed, sum_x)
        out_pieces = sent_back(out_sum, "batch")
        x_pieces = sent_back(sum_x, "seq")
    mixed = head_sum(mixed)
    mixed_out = (mask * (hidden_f + mixed)).astype(BF16).reshape(seqs, slots, model)
    grad_normed = head_sum(portion) + mm(grad_pre_bc, w_bc, ((1,), (1,)))
    scaled_input = hidden_f * inv_rms
    grad_norm_gain = jnp.sum(grad_normed * scaled_input, axis=0)
    grad_scaled = grad_normed * norm_gain
    input_dot = jnp.mean(grad_scaled * scaled_input, axis=-1, keepdims=True)
    grad_hidden = grad_mix.astype(F32) + inv_rms * (grad_scaled - scaled_input * input_dot)
    grad_hidden = grad_hidden.reshape(seqs, slots, model)

    head_grad = params_grad.sum(axis=0).transpose(2, 0, 1).reshape(3, heads_dev)
    taps_sum = jnp.concatenate([taps_grad_x.sum(axis=0), taps_grad_bc.sum(axis=0)], axis=1)[: CONV + 1]
    pieces = [taps_sum, head_grad, gain_grad.sum(axis=0), grad_norm_gain]
    flat = jnp.concatenate([piece.reshape(-1) for piece in pieces])
    if paired:
        flat = added_over(flat, "seq")
        out_pieces, x_pieces, flat, grad_hidden, mixed_out = tied(out_pieces, x_pieces, flat, grad_hidden, mixed_out)
        flat = added_over(flat, "batch")
        grad_weight = finished(z_pieces, x_pieces)
        grad_w_out, done_small = out_weight(out_pieces, small_rows)
        bc_mine = done_small[:state]
        bc_other = swapped(bc_mine, "head", 1)
        grad_w_bc = jnp.concatenate(
            [jnp.where(side == 0, bc_mine, bc_other), jnp.where(side == 0, bc_other, bc_mine)], axis=0
        ).T
        grad_w_dt = done_small[state:].T
    else:
        scatter = functools.partial(lax.psum_scatter, axis_name=("batch", "seq"), tiled=True)
        over_slots = ((0,), (0,))
        grad_weight = scatter(
            jnp.stack([mm(normed, grad_z, over_slots), mm(normed, grad_pre, over_slots)], axis=1),
            scatter_dimension=0,
        )
        grad_w_bc = scatter(mm(normed, grad_pre_bc, over_slots), scatter_dimension=0)
        grad_w_dt = scatter(mm(normed, grad_dtr, over_slots), scatter_dimension=0)
        grad_w_out = scatter(mm(gated, grad_mix, over_slots), scatter_dimension=1)
        flat = lax.psum(flat, ("batch", "seq"))

    parted, start = [], 0
    for piece in pieces:
        parted.append(flat[start : start + piece.size].reshape(piece.shape))
        start += piece.size
    grad_conv, grad_head, grad_gate_gain, grad_norm_gain = parted
    return (
        mixed_out,
        grad_hidden,
        grad_norm_gain,
        grad_weight,
        grad_w_bc,
        grad_w_dt,
        grad_conv[:, :inner],
        grad_conv[:, inner:],
        grad_head,
        grad_gate_gain.reshape(inner),
        grad_w_out,
    )


def solution(mesh):
    placed = (
        P("batch", "seq", None),
        P(),
        P(None, None, "head"),
        P(),
        P(None, "head"),
        P(None, "head"),
        P(),
        P(None, "head"),
        P("head"),
        P("head", None),
        P("batch"),
        P("batch", "seq", None),
    )
    return jax.shard_map(
        per_device,
        mesh=mesh,
        in_specs=placed,
        out_specs=(
            P("batch", "seq", None),
            P("batch", "seq", None),
            P(),
            P(("batch", "seq"), None, "head"),
            P(("batch", "seq"), None),
            P(("batch", "seq"), "head"),
            P(None, "head"),
            P(),
            P(None, "head"),
            P("head"),
            P("head", ("batch", "seq")),
        ),
        check_vma=False,
    )
```
